32 devices in a mesh: row: 4 (over z), col: 8 (over y, x, core).
Axes of the slice: x: 2, y: 2, z: 4, core: 2. Of those that a mesh axis runs over, the one named last changes fastest.
Arguments:
- primitive: float32 [8, 32, 128, 512], P(None, None, 'col', 'row'), may hold values from -4 to 4, as said below
- current_sheet_bricks: int32 [4, 8, 8], P('row', 'col'), may hold values from 0 to 15, as said below
- brick_count: int32 [4, 8], P('row', 'col'), may hold values from 1 to 8, as said below
- w_in: bfloat16 [8, 128], replicated, may hold values from -2 to 2
- w_hid: bfloat16 [2, 128, 128], replicated, may hold values from -0.5 to 0.5
- w_out: bfloat16 [128], replicated, may hold values from -0.5 to 0.5
- b_hid: float32 [3, 128], replicated, may hold values from -3 to 3
Outputs:
- state_next: float32 [8, 32, 128, 512], P(None, None, 'col', 'row')
The draws below stay inside these ranges and needn't reach their ends.
Inputs may be any that keep to these rules, and one draw needn't show every extreme that they name: `primitive`: row 0 (density) lies in 0.5 to 2 and row 7 (pressure) in 0.2 to 2. `current_sheet_bricks`: each device's 8 entries are distinct numbers of its own bricks. `brick_count`: in every row of devices some device lists 8 bricks.
All inputs are finite; a program needn't handle non-finite values.
Results may differ from the reference program's by a relative error of at most 0.0013.
Values may be sent and summed in bfloat16 or wider, within the bound.
No kernel may reach another device: no remote copies, remote signals or barrier semaphores. Data moves between devices by JAX's collectives and lax.ppermute only.
A program may use at most 256 MiB of HBM per device.

```python
import jax
import jax.numpy as jnp
from jax import lax

NZ = 32
CX = 16
CY = 128
BRICK = 16
FEAT = 8
HID = 128
SUB = 4
NX = 128
NY = 512
BRICK_DEV = 16
LIST_MAX = 8
N_ROW = 4
N_COL = 8


def draw_primitive(key, part):
    subkeys = jax.random.split(key, 4)
    grid_shape = (NZ, NX, NY)
    density = 0.5 * 4.0 ** jax.random.uniform(subkeys[0], grid_shape, jnp.float32)
    pressure = 0.2 * 10.0 ** jax.random.uniform(subkeys[1], grid_shape, jnp.float32)
    velocity = jnp.clip(0.5 * jax.random.normal(subkeys[2], (3,) + grid_shape, jnp.float32), -1.5, 1.5)
    magnetic = jnp.clip(jax.random.normal(subkeys[3], (3,) + grid_shape, jnp.float32), -4.0, 4.0)
    return jnp.concatenate([density[None], velocity, magnetic, pressure[None]], axis=0).astype(jnp.float32)


def draw_current_sheet_bricks(key, part):
    rows_count = NY // CY
    cols_count = NX // CX
    subkeys = jax.random.split(key, rows_count * cols_count)

    def pick_bricks(single):
        return jax.random.permutation(single, BRICK_DEV)[:LIST_MAX].astype(jnp.int32)
    chosen = jax.vmap(pick_bricks)(subkeys)
    return chosen.reshape(rows_count, cols_count, LIST_MAX).astype(jnp.int32)


def draw_brick_count(key, part):
    rows_count = NY // CY
    cols_count = NX // CX
    centre = jax.random.randint(jax.random.fold_in(key, 5), (rows_count, 1), 0, cols_count).astype(jnp.int32)
    column = jnp.arange(cols_count, dtype=jnp.int32)[None, :]
    apart = jnp.abs(column - centre)
    apart = jnp.minimum(apart, cols_count - apart)
    base = LIST_MAX // (1 + apart // 2)
    jitter = jax.random.randint(jax.random.fold_in(key, 9), (rows_count, cols_count), 0, 3).astype(jnp.int32)
    counts = jnp.where(apart == 0, LIST_MAX, jnp.maximum(base - jitter, 1))
    return counts.astype(jnp.int32)


def noise(own_key, dims, deviation, most, kind=jnp.bfloat16):
    entries = jax.random.normal(own_key, dims, jnp.float32) * deviation
    return jnp.minimum(jnp.maximum(entries, -most), most).astype(kind)


def setup_inputs(seed: int = 0) -> dict:
    key_of = jax.random.split(jax.random.key(seed), 8)
    primitive = draw_primitive(jax.random.fold_in(key_of[7], 71), 0)
    current_sheet_bricks = draw_current_sheet_bricks(jax.random.fold_in(key_of[7], 71), 0)
    brick_count = draw_brick_count(jax.random.fold_in(key_of[7], 71), 0)
    w_in = noise(key_of[3], (FEAT, HID), FEAT ** -0.5, 2.0)
    w_hid = noise(key_of[4], (2, HID, HID), HID ** -0.5, 0.5)
    w_out = noise(key_of[5], (HID,), HID ** -0.5, 0.5)
    b_hid = noise(key_of[6], (3, HID), 0.5, 3.0, jnp.float32)
    return {"primitive": primitive, "current_sheet_bricks": current_sheet_bricks, "brick_count": brick_count, "w_in": w_in, "w_hid": w_hid, "w_out": w_out, "b_hid": b_hid}


ADIABATIC = 5.0 / 3.0
TIME_STEP = 0.02
RATE_LOW = 0.02
RATE_SPAN = 0.14

def cell_terms(primitive):
    density = primitive[0]
    velocity = primitive[1:4]
    magnetic = primitive[4:7]
    pressure = primitive[7]
    mag_square = lax.optimization_barrier(jnp.sum(magnetic * magnetic, axis=0))
    speed_square = lax.optimization_barrier(jnp.sum(velocity * velocity, axis=0))
    alignment = lax.optimization_barrier(jnp.sum(velocity * magnetic, axis=0))
    energy = pressure / (ADIABATIC - 1.0) + 0.5 * density * speed_square + 0.5 * mag_square
    pressure_total = pressure + 0.5 * mag_square
    conserved = jnp.concatenate([density[None], density[None] * velocity, magnetic, energy[None]], axis=0)
    fast_speed = jnp.sqrt((ADIABATIC * pressure + mag_square) / density)
    fluxes = []
    speeds = []
    for direction in range(3):
        vel_dir = velocity[direction]
        mag_dir = magnetic[direction]
        flux_rows = [density * vel_dir]
        for component in range(3):
            flux_term = density * velocity[component] * vel_dir - magnetic[component] * mag_dir
            if component == direction:
                flux_term = flux_term + pressure_total
            flux_rows.append(flux_term)
        for component in range(3):
            flux_rows.append(vel_dir * magnetic[component] - mag_dir * velocity[component])
        flux_rows.append((energy + pressure_total) * vel_dir - mag_dir * alignment)
        fluxes.append(jnp.stack(flux_rows))
        speeds.append(jnp.abs(vel_dir) + fast_speed)
    return (conserved, fluxes, speeds, mag_square, speed_square)

def rusanov(left_u, right_u, left_f, right_flux, left_s, right_s):
    return 0.5 * (left_f + right_flux) - 0.5 * jnp.maximum(left_s, right_s)[None] * (right_u - left_u)

def centred(values, array_axis):
    return 0.5 * (jnp.roll(values, -1, array_axis) - jnp.roll(values, 1, array_axis))

def closure(input_cells, first_weight, w_middle, w_last, bias_terms):
    hidden_units = jnp.einsum('nj,dno->djo', first_weight.astype(jnp.float32), input_cells.astype(jnp.float32)) + bias_terms[0][None, :, None]
    hidden_units = jax.nn.gelu(hidden_units).astype(jnp.bfloat16)
    for hidden_layer in range(2):
        hidden_units = jnp.einsum('ho,ghc->goc', w_middle[hidden_layer].astype(jnp.float32), hidden_units.astype(jnp.float32)) + bias_terms[hidden_layer + 1][None, :, None]
        hidden_units = jax.nn.gelu(hidden_units).astype(jnp.bfloat16)
    score = jnp.einsum('h,ghc->gc', w_last.astype(jnp.float32), hidden_units.astype(jnp.float32))
    return RATE_LOW + RATE_SPAN * jax.nn.sigmoid(score)

def reference(primitive, current_sheet_bricks, brick_count, w_in, w_hid, w_out, b_hid):
    conserved, fluxes, speeds, mag_square, speed_square = cell_terms(primitive)
    change = jnp.zeros_like(conserved)
    for direction, array_axis in ((0, 2), (1, 3), (2, 1)):
        face_flux = rusanov(conserved, jnp.roll(conserved, -1, array_axis), fluxes[direction], jnp.roll(fluxes[direction], -1, array_axis), speeds[direction], jnp.roll(speeds[direction], -1, array_axis - 1))
        change = change + face_flux - jnp.roll(face_flux, 1, array_axis)
    advanced = conserved - TIME_STEP * change
    density = primitive[0]
    velocity = primitive[1:4]
    magnetic = primitive[4:7]
    current_x = centred(magnetic[2], 2) - centred(magnetic[1], 0)
    current_y = centred(magnetic[0], 0) - centred(magnetic[2], 1)
    current_z = centred(magnetic[1], 1) - centred(magnetic[0], 2)
    divergence = centred(velocity[0], 1) + centred(velocity[1], 2) + centred(velocity[2], 0)
    features = jnp.stack([current_x, current_y, current_z, divergence, density, primitive[7], mag_square, speed_square]).astype(jnp.bfloat16)
    bricks_z, bricks_x, bricks_y = (NZ // BRICK, NX // BRICK, NY // BRICK)
    cell_count = BRICK ** 3
    blocks = features.reshape(8, bricks_z, BRICK, bricks_x, BRICK, bricks_y, BRICK).transpose(1, 3, 5, 0, 2, 4, 6).reshape(bricks_z * bricks_x * bricks_y, 8, cell_count)
    local_x, local_y = (CX // BRICK, CY // BRICK)
    row_index = lax.broadcasted_iota(jnp.int32, current_sheet_bricks.shape, 0)
    col_index = lax.broadcasted_iota(jnp.int32, current_sheet_bricks.shape, 1)
    slot_index = lax.broadcasted_iota(jnp.int32, current_sheet_bricks.shape, 2)
    brick_z = current_sheet_bricks // (local_x * local_y)
    brick_x = current_sheet_bricks // local_y % local_x
    brick_y = current_sheet_bricks % local_y
    global_ids = ((brick_z * bricks_x + col_index * local_x + brick_x) * bricks_y + row_index * local_y + brick_y).reshape(-1).astype(jnp.int32)
    live = (slot_index < brick_count[:, :, None]).reshape(-1)
    picked = blocks[global_ids].reshape(N_ROW * N_COL, LIST_MAX, 8, cell_count)

    def evaluate(input_cells):
        return closure(input_cells, w_in, w_hid, w_out, b_hid)
    rates = lax.map(evaluate, picked).reshape(-1, cell_count)
    rates = jnp.where(live[:, None], rates, jnp.float32(RATE_LOW))
    rate_bricks = jnp.full((bricks_z * bricks_x * bricks_y, cell_count), RATE_LOW, jnp.float32).at[global_ids].set(rates)
    rate_field = rate_bricks.reshape(bricks_z, bricks_x, bricks_y, BRICK, BRICK, BRICK).transpose(0, 3, 1, 4, 2, 5).reshape(NZ, NX, NY)
    field_b = advanced[4:7]
    for sub_step in range(SUB):
        laplace = jnp.roll(field_b, -1, 2) + jnp.roll(field_b, 1, 2) + jnp.roll(field_b, -1, 3) + jnp.roll(field_b, 1, 3) + jnp.roll(field_b, -1, 1) + jnp.roll(field_b, 1, 1) - 6.0 * field_b
        field_b = field_b + rate_field[None] * laplace
    return jnp.concatenate([advanced[:4], field_b, advanced[7:]], axis=0)
```

```python
import jax
import jax.numpy as jnp
from jax import lax
from jax.experimental import pallas as pl
from jax.experimental.pallas import tpu as pltpu
from jax.sharding import PartitionSpec as P

BRICK = 16
SUB = 4
ADIABATIC = 5.0 / 3.0
TIME_STEP = 0.02
RATE_LOW = 0.02
RATE_SPAN = 0.14
GELU_A = 0.7978845608
GELU_B = 0.7978845608 * 0.044715
F32 = jnp.float32
BF16 = jnp.bfloat16
LANES = 128
NZ = 32
CX = 16
HID = 128
PLANE = NZ * CX
KIN = 80
KHID = HID + 16
VMEM_LIMIT = 48 << 20


def iota(shape, dim):
    return lax.broadcasted_iota(jnp.int32, shape, dim)


def take(values, index):
    return jnp.take_along_axis(values, index, axis=1, mode="promise_in_bounds")


def next_row(v):
    return pltpu.roll(v, v.shape[0] - 1, 0)


def prev_row(v):
    return pltpu.roll(v, 1, 0)


def next_lane(v):
    return pltpu.roll(v, v.shape[1] - 1, 1)


def prev_lane(v):
    return pltpu.roll(v, 1, 1)


def derive(p):
    rho, pr = p[0], p[7]
    v, b = p[1:4], p[4:7]
    m = [rho * c for c in v]
    b2 = b[0] * b[0] + b[1] * b[1] + b[2] * b[2]
    v2 = v[0] * v[0] + v[1] * v[1] + v[2] * v[2]
    vb = v[0] * b[0] + v[1] * b[1] + v[2] * b[2]
    pt = pr + 0.5 * b2
    en = 1.5 * pr + 0.5 * (rho * v2 + b2)
    fast = jnp.sqrt((ADIABATIC * pr + b2) / rho)
    ep = en + pt
    tens = {(i, j): m[i] * v[j] - b[i] * b[j] for i in range(3) for j in range(i, 3)}
    elec = {(i, j): v[i] * b[j] - b[i] * v[j] for i in range(3) for j in range(i + 1, 3)}
    fluxes = []
    for d in range(3):
        rows = [m[d]]
        for c in range(3):
            t = tens[(min(c, d), max(c, d))]
            rows.append(t + pt if c == d else t)
        for c in range(3):
            rows.append(None if c == d else (elec[(d, c)] if d < c else -elec[(c, d)]))
        rows.append(ep * v[d] - b[d] * vb)
        fluxes.append(rows)
    speeds = [jnp.abs(c) + fast for c in v]
    return [rho] + m + list(b) + [en], fluxes, speeds


def face(u, un, f, fn, s, sn):
    a = 0.5 * jnp.maximum(s, sn)
    out = []
    for c in range(8):
        diss = a * (un[c] - u[c])
        out.append(-diss if f[c] is None else 0.5 * (f[c] + fn[c]) - diss)
    return out


def gelu_twice(u):
    u = u.astype(BF16)
    t = jnp.tanh(u * (jnp.asarray(GELU_A, BF16) + jnp.asarray(GELU_B, BF16) * (u * u)))
    return u + u * t


def closure_rates(first, w1, w2, wo):
    us = first
    for w in (w1, w2):
        hs = [jnp.concatenate([gelu_twice(u), bias_rows(u.shape[1]).astype(BF16)], axis=0) for u in us]
        us = [jnp.dot(w, h, preferred_element_type=F32) for h in hs]
    hs = [gelu_twice(u) for u in us]
    scores = [jnp.dot(wo, h, preferred_element_type=F32) for h in hs]
    return [(RATE_LOW + 0.5 * RATE_SPAN) + (0.5 * RATE_SPAN) * jnp.tanh(0.5 * s) for s in scores]


def features(load, z, patch_x=None, patch_y=None):
    zn, zp = lax.rem(z + 1, NZ), lax.rem(z + NZ - 1, NZ)
    row, lane = iota((CX, LANES), 0), iota((CX, LANES), 1)

    def dx(f, v):
        up, dn = next_row(v), prev_row(v)
        if patch_x is not None:
            lo, hi = patch_x(f, z)
            up = jnp.where(row == CX - 1, hi, up)
            dn = jnp.where(row == 0, lo, dn)
        return 0.5 * (up - dn)

    def dy(f, v):
        up, dn = next_lane(v), prev_lane(v)
        if patch_y is not None:
            edge = patch_y(f, z)
            up = jnp.where(lane == LANES - 1, edge, up)
            dn = jnp.where(lane == 0, edge, dn)
        return 0.5 * (up - dn)

    def dz(f):
        return 0.5 * (load(f, zn) - load(f, zp))

    rho, vx, vy, vz, bx, by, bz, pr = [load(f, z) for f in range(8)]
    jx = dy(6, bz) - dz(5)
    jy = dz(4) - dx(6, bz)
    jz = dx(5, by) - dy(4, bx)
    div = dx(1, vx) + dy(2, vy) + dz(3)
    return [jx, jy, jz, div, rho, pr, bx * bx + by * by + bz * bz, vx * vx + vy * vy + vz * vz]


def bias_rows(n):
    return jnp.where(iota((16, n), 0) < 3, 1.0, 0.0)


def plane_loader(prim_ref):
    def load(f, z):
        return prim_ref[pl.ds(pl.multiple_of((f * NZ + z) * CX, CX), CX), :]

    return load


def edge_lane_index():
    return jnp.where(iota((8, LANES), 1) % 2 == 0, 0, LANES - 1)


def pack_kernel(prim_ref, lo_ref, hi_ref, py_ref):
    lane = iota((8, LANES), 1)
    index = edge_lane_index()
    for f in range(8):
        lo_ref[pl.ds(f * NZ, NZ), :] = prim_ref[pl.ds(f * PLANE, NZ, stride=CX), :]
        hi_ref[pl.ds(f * NZ, NZ), :] = prim_ref[pl.ds(f * PLANE + CX - 1, NZ, stride=CX), :]
        acc = jnp.zeros((8, LANES), F32)
        for z in range(NZ):
            for o in range(2):
                v = prim_ref[pl.ds((f * NZ + z) * CX + o * 8, 8), :]
                acc = jnp.where(lane // 2 == o * NZ + z, take(v, index), acc)
        py_ref[pl.ds(f * 8, 8), :] = acc


def brick_rows(bricks_ref, count_ref):
    lane = iota((8, LANES), 1)
    slot, inner = lane // BRICK, lane % BRICK
    source = jnp.zeros((8, LANES), jnp.int32)
    half = jnp.zeros((8, LANES), jnp.int32)
    back = [jnp.full((8, LANES), -1, jnp.int32) for _ in range(2)]
    per_half = LANES // BRICK
    for j in range(8):
        b = bricks_ref[0, j]
        bz, by = b // per_half, b % per_half
        source = jnp.where(slot == j, by * BRICK + inner, source)
        half = jnp.where(slot == j, bz, half)
        for h in range(2):
            use = jnp.logical_and(bz == h, j < count_ref[0, 0])
            want = jnp.where(use, by, -1)
            back[h] = jnp.where(slot == want, j * BRICK + inner, back[h])
    return source, half, back


def main_kernel(bricks_ref, count_ref, prim_ref, win_ref, whid_ref, wout_ref, bias_ref,
                adv_ref, kap_ref, wb_ref, w1_ref, w2_ref, wo_ref,
                x_ref, u_ref, fz_ref, sz_ref, ch_ref):
    load = plane_loader(prim_ref)
    def split(b):
        hi = b.astype(BF16)
        r = b - hi.astype(F32)
        mid = r.astype(BF16)
        return [hi.astype(F32), mid.astype(F32), r - mid.astype(F32)]

    cols = (((0,), (0,)), ((), ()))
    rows = iota((16, KIN), 0)
    col = iota((16, KIN), 1)
    first = jnp.concatenate(
        [win_ref[...].astype(F32)] + split(bias_ref[0:1, :]) + [jnp.zeros((5, HID), F32)], axis=0
    ).astype(BF16)
    for s in range(8):
        place = jnp.where(rows < 8, rows * 8 + s, jnp.where(rows < 11, 64 + rows - 8, -1))
        pick = jnp.where(col == place, 1.0, 0.0).astype(BF16)
        wb_ref[pl.ds(s * HID, HID), :] = lax.dot_general(
            first, pick, cols, preferred_element_type=F32).astype(BF16)
    eye = jnp.where(iota((HID, HID), 0) == iota((HID, HID), 1), 0.5, 0.0).astype(BF16)
    eye16 = jnp.where(iota((16, 16), 0) == iota((16, 16), 1), 1.0, 0.0).astype(BF16)
    for layer, ref in ((0, w1_ref), (1, w2_ref)):
        turned = lax.dot_general(whid_ref[pl.ds(layer * HID, HID), :], eye, cols,
                                 preferred_element_type=F32)
        brow = jnp.concatenate(
            split(bias_ref[layer + 1 : layer + 2, :]) + [jnp.zeros((13, HID), F32)], axis=0
        ).astype(BF16)
        bcol = lax.dot_general(brow, eye16, cols, preferred_element_type=F32)
        ref[...] = jnp.concatenate([turned, bcol], axis=1).astype(BF16)
    wo_ref[...] = jnp.broadcast_to(0.5 * wout_ref[...].astype(F32), (16, HID)).astype(BF16)

    source, half, _ = brick_rows(bricks_ref, count_ref)
    tail = bias_rows(LANES)

    @pl.loop(0, NZ // 2)
    def _(z):
        low = features(load, z)
        high = features(load, z + NZ // 2)
        at = pl.ds(pl.multiple_of(z * LANES, LANES), LANES)
        for o in range(2):
            parts = []
            for a, b in zip(low, high):
                a, b = a[o * 8 : o * 8 + 8], b[o * 8 : o * 8 + 8]
                parts.append(jnp.where(half == 1, take(b, source), take(a, source)))
            x_ref[pl.ds(o * KIN, KIN), at] = jnp.concatenate(parts + [tail], axis=0).astype(BF16)

    w1, w2, wo = w1_ref[...], w2_ref[...], wo_ref[...]
    chunk = 8 * LANES

    @pl.loop(0, 4)
    def _(i):
        o, part = i // 2, i % 2
        x = x_ref[pl.ds(pl.multiple_of(o * KIN, 16), KIN),
                  pl.ds(pl.multiple_of(part * chunk, LANES), chunk)]
        us = [jnp.dot(wb_ref[pl.ds(s * HID, HID), :], x, preferred_element_type=F32)
              for s in range(8)]
        rates = closure_rates(us, w1, w2, wo)
        sub = iota((8, chunk), 0)
        out = rates[0][:8]
        for s in range(1, 8):
            out = jnp.where(sub == s, rates[s][:8], out)
        for j in range(8):
            kap_ref[pl.ds(pl.multiple_of((part * 8 + j) * CX + o * 8, 8), 8), :] = (
                out[:, j * LANES : (j + 1) * LANES])

    row, lane = iota((CX, LANES), 0), iota((CX, LANES), 1)

    @pl.loop(0, NZ)
    def _(z):
        u, f, s = derive([load(k, z) for k in range(8)])

        def along(d, nxt, prv, last):
            sn = nxt(s[d])
            fc = face(u, [nxt(c) for c in u], f[d],
                      [None if c is None else nxt(c) for c in f[d]], s[d], sn)
            fc = [jnp.where(last, 0.0, c) for c in fc]
            return [c - prv(c) for c in fc]

        cx = along(0, next_row, prev_row, row == CX - 1)
        cy = along(1, next_lane, prev_lane, lane == LANES - 1)
        at = [pl.ds(pl.multiple_of((k * NZ + z) * CX, CX), CX) for k in range(8)]
        for k in range(8):
            ch_ref[at[k], :] = cx[k] + cy[k]
            u_ref[at[k], :] = u[k]
            if f[2][k] is not None:
                fz_ref[at[k], :] = f[2][k]
        sz_ref[at[0], :] = s[2]

    def zface(z):
        zn = lax.rem(z + 1, NZ)

        def get(ref, k, zz):
            return ref[pl.ds(pl.multiple_of((k * NZ + zz) * CX, CX), CX), :]

        ks = range(8)
        f = [None if k == 6 else get(fz_ref, k, z) for k in ks]
        fn = [None if k == 6 else get(fz_ref, k, zn) for k in ks]
        return face([get(u_ref, k, z) for k in ks], [get(u_ref, k, zn) for k in ks], f, fn,
                    get(sz_ref, 0, z), get(sz_ref, 0, zn))

    def finish(z, before):
        here = zface(z)
        for k in range(8):
            at = pl.ds(pl.multiple_of((k * NZ + z) * CX, CX), CX)
            adv_ref[at, :] = u_ref[at, :] - TIME_STEP * (ch_ref[at, :] + (here[k] - before[k]))
        return tuple(here)

    lax.fori_loop(0, NZ, finish, tuple(zface(NZ - 1)))


def edge_kernel(bricks_ref, count_ref, prim_ref, advin_ref, kapin_ref, py_ref,
                xlo_ref, xhi_ref, yfl_ref, yfr_ref, wb_ref, w1_ref, w2_ref, wo_ref,
                adv_ref, kap_ref, ylo_ref, yhi_ref, sxlo_ref, sxhi_ref,
                x_ref, yh_ref, d_ref):
    load = plane_loader(prim_ref)
    lane8 = iota((8, LANES), 1)
    side0 = lane8 % 2 == 0
    last_lane = jnp.where(lane8 == LANES - 1, 1, 0)
    on_edge = jnp.logical_or(lane8 == 0, lane8 == LANES - 1)

    halo, own = [], []
    for f in range(8):
        at = pl.ds(f * 8, 8)
        h = jnp.where(side0, next_lane(yfl_ref[at, :]), prev_lane(yfr_ref[at, :]))
        yh_ref[at, :] = h
        halo.append(h)
        own.append(py_ref[at, :])
    uh, fh, sh = derive(halo)
    uo, fo, so = derive(own)

    def pair(a, b):
        return [None if p is None else jnp.where(side0, p, q) for p, q in zip(a, b)]

    fc = face(pair(uh, uo), pair(uo, uh), pair(fh[1], fo[1]), pair(fo[1], fh[1]),
              jnp.where(side0, sh[1], so[1]), jnp.where(side0, so[1], sh[1]))
    for c in range(8):
        d_ref[pl.ds(c * 8, 8), :] = jnp.where(side0, TIME_STEP, -TIME_STEP) * fc[c]

    @pl.loop(0, NZ)
    def _(z):
        for c in range(8):
            delta = d_ref[pl.ds(c * 8, 8), :]
            for o in range(2):
                at = pl.ds(pl.multiple_of((c * NZ + z) * CX + o * 8, 8), 8)
                g = take(delta, (o * NZ + z) * 2 + last_lane)
                adv_ref[at, :] = advin_ref[at, :] + jnp.where(on_edge, g, 0.0)

    for k in range(NZ // 8):
        zs = k * 8
        for lo in (True, False):
            start = 0 if lo else CX - 1
            ref = xlo_ref if lo else xhi_ref
            rows = [pl.ds(f * PLANE + zs * CX + start, 8, stride=CX) for f in range(8)]
            uo, fo, so = derive([prim_ref[r, :] for r in rows])
            uh, fh, sh = derive([ref[pl.ds(f * NZ + zs, 8), :].astype(F32) for f in range(8)])
            if lo:
                fc = face(uh, uo, fh[0], fo[0], sh[0], so[0])
            else:
                fc = face(uo, uh, fo[0], fh[0], so[0], sh[0])
            for c in range(8):
                step = TIME_STEP * fc[c]
                adv_ref[rows[c], :] = adv_ref[rows[c], :] + (step if lo else -step)

    source, half, back = brick_rows(bricks_ref, count_ref)
    tail = bias_rows(LANES)
    index = edge_lane_index()
    sub = iota((8, LANES), 0)

    def patch_x(f, z):
        return (xlo_ref[pl.ds(f * NZ + z, 1), :].astype(F32), xhi_ref[pl.ds(f * NZ + z, 1), :].astype(F32))

    def patch_y(f, z):
        h = yh_ref[pl.ds(f * 8, 8), :]
        return jnp.concatenate([take(h, (o * NZ + z) * 2 + last_lane) for o in range(2)], axis=0)

    def gather_edges(z, acc):
        sets = []
        for zz in (z, z + NZ // 2):
            fs = features(load, zz, patch_x, patch_y)
            for o in range(2):
                acc = tuple(
                    jnp.where(lane8 // 2 == o * NZ + zz, take(v[o * 8 : o * 8 + 8], index), a)
                    for v, a in zip(fs, acc))
            sets.append([jnp.where(sub == 7, v[8:16], v[0:8]) for v in fs])
        parts = [jnp.where(half == 1, take(b, source), take(a, source)) for a, b in zip(*sets)]
        at = pl.ds(pl.multiple_of(z * LANES, LANES), LANES)
        x_ref[:, at] = jnp.concatenate(parts + [tail], axis=0).astype(BF16)
        return acc

    zero = jnp.zeros((8, LANES), F32)
    acc = lax.fori_loop(0, NZ // 2, gather_edges, (zero,) * 8)
    w1, w2, wo = w1_ref[...], w2_ref[...], wo_ref[...]
    ycells = jnp.concatenate(list(acc) + [tail], axis=0).astype(BF16)
    xcells = x_ref[...]
    us = [jnp.dot(wb_ref[pl.ds(s * HID, HID), :], xcells, preferred_element_type=F32)
          for s in (0, 7)]
    uy = jnp.dot(wb_ref[...], ycells, preferred_element_type=F32)
    us.append(jnp.concatenate([uy[s * HID : (s + 1) * HID] for s in range(8)], axis=1))
    r0, r7, ry = closure_rates(us, w1, w2, wo)
    kapy = ry[:8, 0:LANES]
    for s in range(1, 8):
        kapy = jnp.where(sub == s, ry[:8, s * LANES : (s + 1) * LANES], kapy)
    for z in range(NZ // 2):
        at = slice(z * LANES, (z + 1) * LANES)
        for o in range(2):
            k = kapin_ref[pl.ds(z * CX + o * 8, 8), :]
            k = jnp.where(sub == 0, r0[:8, at], k) if o == 0 else jnp.where(sub == 7, r7[:8, at], k)
            for h in range(2):
                zz = z + h * (NZ // 2)
                listed = back[h] >= 0
                full = take(k, jnp.where(listed, back[h], 0))
                edge = take(kapy, (o * NZ + zz) * 2 + last_lane)
                full = jnp.where(on_edge, edge, full)
                kap_ref[pl.ds(zz * CX + o * 8, 8), :] = jnp.where(listed, full, RATE_LOW)

    low4 = lane8 % 4
    high4 = LANES - 4 + low4
    for f in range(4):
        src, base = (adv_ref, (4 + f) * PLANE) if f < 3 else (kap_ref, 0)
        lows, highs = [], []
        for o in range(2):
            lo = jnp.zeros((8, LANES), F32)
            hi = jnp.zeros((8, LANES), F32)
            for z in range(NZ):
                v = src[pl.ds(base + z * CX + o * 8, 8), :]
                mine = lane8 // 4 == z
                lo = jnp.where(mine, take(v, low4), lo)
                hi = jnp.where(mine, take(v, high4), hi)
            lows.append(lo)
            highs.append(hi)
        ylo_ref[pl.ds(f * CX, CX), :] = jnp.concatenate(lows, axis=0).astype(BF16)
        yhi_ref[pl.ds(f * CX, CX), :] = jnp.concatenate(highs, axis=0).astype(BF16)
        for r in range(4):
            at = pl.ds((f * 4 + r) * NZ, NZ)
            sxlo_ref[at, :] = src[pl.ds(base + r, NZ, stride=CX), :].astype(BF16)
            sxhi_ref[at, :] = src[pl.ds(base + CX - 4 + r, NZ, stride=CX), :].astype(BF16)


DEEP = CX + 8
YG = NZ // 4


def diffuse_kernel(adv_ref, kap_ref, xlo_ref, xhi_ref, ylo_ref, yhi_ref, out_ref,
                   m0, m1, km, y0, y1, ky, xl, xh, yl, yh):
    comp = pl.program_id(0)
    lane = iota((8, LANES), 1)
    sub = iota((8, LANES), 0)
    window = lane % 32
    block = lane // 32
    own_index = jnp.maximum(jnp.where(window < 16, window - 4, window + 100), 0)
    own_index = jnp.minimum(own_index, LANES - 1)

    def build(field, own_ref, main, edge):
        base = field * (4 * NZ)
        for z in range(NZ):
            main[pl.ds(z * DEEP, CX), :] = own_ref[pl.ds(z * CX, CX), :]
        for r in range(4):
            at = pl.ds(pl.multiple_of(base + r * NZ, 8), NZ)
            main[pl.ds(CX + r, NZ, stride=DEEP), :] = xh[at, :]
            main[pl.ds(CX + 4 + r, NZ, stride=DEEP), :] = xl[at, :]
        for o in range(3):
            if o < 2:
                at = pl.ds(pl.multiple_of(field * CX + o * 8, 8), 8)
                left, right = yl[at, :], yh[at, :]
            else:
                at = pl.ds(pl.multiple_of(16 * NZ + field * 8, 8), 8)
                left = jnp.where(sub < 4, xh[at, :], xl[at, :])
                at = pl.ds(pl.multiple_of(16 * NZ + 32 + field * 8, 8), 8)
                right = jnp.where(sub < 4, xh[at, :], xl[at, :])
            for g in range(YG):
                v = jnp.zeros((8, LANES), F32)
                for b in range(4):
                    piece = main[pl.ds((b * YG + g) * DEEP + o * 8, 8), :]
                    v = jnp.where(block == b, take(piece, own_index), v)
                v = jnp.where(window < 4, pltpu.roll(left, (LANES - 4 * g) % LANES, 1), v)
                v = jnp.where(window >= 28, pltpu.roll(right, (28 + LANES - 4 * g) % LANES, 1), v)
                edge[pl.ds(g * DEEP + o * 8, 8), :] = v

    @pl.when(comp == 0)
    def _():
        xl[...] = xlo_ref[...].astype(F32)
        xh[...] = xhi_ref[...].astype(F32)
        yl[...] = ylo_ref[...].astype(F32)
        yh[...] = yhi_ref[...].astype(F32)
        build(3, kap_ref, km, ky)

    build(comp, adv_ref, m0, y0)

    def relax(c, up, dn, k):
        total = next_row(c) + prev_row(c) + next_lane(c) + prev_lane(c) + (up + dn)
        return c + k * (total - 6.0 * c)

    mains, edges = (m0, m1), (y0, y1)
    for step in range(SUB):
        a, b = mains[step % 2], mains[1 - step % 2]
        ea, eb = edges[step % 2], edges[1 - step % 2]

        def at(z):
            return pl.ds(pl.multiple_of(z * DEEP, 8), DEEP)

        @pl.loop(0, NZ)
        def _(z):
            zn, zp = lax.rem(z + 1, NZ), lax.rem(z + NZ - 1, NZ)
            b[at(z), :] = relax(a[at(z), :], a[at(zn), :], a[at(zp), :], km[at(z), :])

        for g in range(YG):
            up = ea[at(g + 1), :] if g + 1 < YG else pltpu.roll(ea[at(0), :], LANES - 32, 1)
            dn = ea[at(g - 1), :] if g > 0 else pltpu.roll(ea[at(YG - 1), :], 32, 1)
            eb[at(g), :] = relax(ea[at(g), :], up, dn, ky[at(g), :])

    main, edge = mains[SUB % 2], edges[SUB % 2]
    on_edge = jnp.logical_or(lane < 4, lane >= LANES - 4)
    for z in range(NZ):
        b, g = z // YG, z % YG
        index = jnp.where(lane < 4, b * 32 + 4 + lane, b * 32 + 24 + lane - (LANES - 4))
        index = jnp.minimum(jnp.maximum(index, 0), LANES - 1)
        for o in range(2):
            e = take(edge[pl.ds(g * DEEP + o * 8, 8), :], index)
            out_ref[pl.ds(z * CX + o * 8, 8), :] = jnp.where(
                on_edge, e, main[pl.ds(z * DEEP + o * 8, 8), :])


def struct(shape, dtype=F32):
    return jax.ShapeDtypeStruct(shape, dtype)


def params():
    return pltpu.CompilerParams(vmem_limit_bytes=VMEM_LIMIT)


VSPEC = pl.BlockSpec(memory_space=pltpu.VMEM)
SSPEC = pl.BlockSpec(memory_space=pltpu.SMEM)


def step_up(axis):
    n = lax.axis_size(axis)
    return [(i, (i + 1) % n) for i in range(n)]


def step_down(axis):
    n = lax.axis_size(axis)
    return [((i + 1) % n, i) for i in range(n)]


def shards(primitive, current_sheet_bricks, brick_count, w_in, w_hid, w_out, b_hid):
    shape = primitive.shape
    prim = primitive.reshape(8 * PLANE, LANES)
    bricks = current_sheet_bricks.reshape(1, -1)
    count = brick_count.reshape(1, 1)

    lo, hi, py = pl.pallas_call(
        pack_kernel,
        out_shape=[struct((8 * NZ, LANES)), struct((8 * NZ, LANES)), struct((64, LANES))],
        compiler_params=params(),
        name="pack",
    )(prim)
    yfl = lax.ppermute(py, "row", step_up("row"))
    yfr = lax.ppermute(py, "row", step_down("row"))
    xlo = lax.ppermute(hi, "col", step_up("col"))
    xhi = lax.ppermute(lo, "col", step_down("col"))

    weights = [struct((8 * HID, KIN), BF16), struct((HID, KHID), BF16), struct((HID, KHID), BF16),
               struct((16, HID), BF16)]
    adv, kap, wb, w1, w2, wo = pl.pallas_call(
        main_kernel,
        in_specs=[SSPEC, SSPEC] + [VSPEC] * 5,
        out_shape=[struct((8 * PLANE, LANES)), struct((NZ // 2 * CX, LANES))] + weights,
        scratch_shapes=[pltpu.VMEM((2 * KIN, NZ // 2 * LANES), BF16),
                        pltpu.VMEM((8 * PLANE, LANES), F32), pltpu.VMEM((8 * PLANE, LANES), F32),
                        pltpu.VMEM((PLANE, LANES), F32), pltpu.VMEM((8 * PLANE, LANES), F32)],
        compiler_params=params(),
        cost_estimate=pl.CostEstimate(flops=6_000_000_000, bytes_accessed=4 << 20, transcendentals=0),
        name="bulk",
    )(bricks, count, prim, w_in, w_hid.reshape(2 * HID, HID), w_out.reshape(1, HID), b_hid)

    adv, kap, ylo, yhi, sxlo, sxhi = pl.pallas_call(
        edge_kernel,
        in_specs=[SSPEC, SSPEC] + [VSPEC] * 12,
        out_shape=[struct((8 * PLANE, LANES)), struct((PLANE, LANES)),
                   struct((4 * CX, LANES), BF16), struct((4 * CX, LANES), BF16),
                   struct((16 * NZ, LANES), BF16), struct((16 * NZ, LANES), BF16)],
        scratch_shapes=[pltpu.VMEM((KIN, NZ // 2 * LANES), BF16), pltpu.VMEM((64, LANES), F32),
                        pltpu.VMEM((64, LANES), F32)],
        compiler_params=params(),
        name="edges",
    )(bricks, count, prim, adv, kap, py, xlo, xhi, yfl, yfr, wb, w1, w2, wo)

    hlo = lax.ppermute(yhi, "row", step_up("row"))
    hhi = lax.ppermute(ylo, "row", step_down("row"))

    def with_corners(rows, start):
        parts = [h.reshape(4, CX, LANES)[:, start : start + 8].reshape(32, LANES) for h in (hlo, hhi)]
        return jnp.concatenate([rows] + parts, axis=0)

    dhi = lax.ppermute(with_corners(sxlo, 0), "col", step_down("col"))
    dlo = lax.ppermute(with_corners(sxhi, 8), "col", step_up("col"))

    full = lambda rows: pl.BlockSpec((rows, LANES), lambda c: (0, 0))
    part = pl.BlockSpec((PLANE, LANES), lambda c: (4 + c, 0))
    xrows = 16 * NZ + 64
    out = pl.pallas_call(
        diffuse_kernel,
        grid=(3,),
        in_specs=[part, full(PLANE), full(xrows), full(xrows), full(4 * CX), full(4 * CX)],
        out_specs=part,
        out_shape=struct((8 * PLANE, LANES)),
        input_output_aliases={0: 0},
        scratch_shapes=[pltpu.VMEM((NZ * DEEP, LANES), F32)] * 3
        + [pltpu.VMEM((YG * DEEP, LANES), F32)] * 3
        + [pltpu.VMEM((xrows, LANES), F32)] * 2
        + [pltpu.VMEM((4 * CX, LANES), F32)] * 2,
        compiler_params=params(),
        name="diffuse",
    )(adv, kap, dlo, dhi, hlo, hhi)
    return out.reshape(shape)


def solution(mesh):
    return jax.shard_map(
        shards,
        mesh=mesh,
        in_specs=(
            P(None, None, "col", "row"),
            P("row", "col", None),
            P("row", "col"),
            P(),
            P(),
            P(),
            P(),
        ),
        out_specs=P(None, None, "col", "row"),
        check_vma=False,
    )
```

```python
import jax
import jax.numpy as jnp
from jax import lax
from jax.experimental import pallas as pl
from jax.experimental.pallas import tpu as pltpu
from jax.sharding import PartitionSpec as P

BRICK = 16
SUB = 4
ADIABATIC = 5.0 / 3.0
TIME_STEP = 0.02
RATE_LOW = 0.02
RATE_SPAN = 0.14
GELU_A = 0.7978845608
GELU_B = 0.7978845608 * 0.044715
F32 = jnp.float32
BF16 = jnp.bfloat16
LANES = 128
NZ = 32
CX = 16
HID = 128
PLANE = NZ * CX
KIN = 80
KHID = HID + 16
VMEM_LIMIT = 48 << 20


def iota(shape, dim):
    return lax.broadcasted_iota(jnp.int32, shape, dim)


def take(values, index):
    return jnp.take_along_axis(values, index, axis=1, mode="promise_in_bounds")


def next_row(v):
    return pltpu.roll(v, v.shape[0] - 1, 0)


def prev_row(v):
    return pltpu.roll(v, 1, 0)


def next_lane(v):
    return pltpu.roll(v, v.shape[1] - 1, 1)


def prev_lane(v):
    return pltpu.roll(v, 1, 1)


def derive(p):
    rho, pr = p[0], p[7]
    v, b = p[1:4], p[4:7]
    m = [rho * c for c in v]
    b2 = b[0] * b[0] + b[1] * b[1] + b[2] * b[2]
    v2 = v[0] * v[0] + v[1] * v[1] + v[2] * v[2]
    vb = v[0] * b[0] + v[1] * b[1] + v[2] * b[2]
    pt = pr + 0.5 * b2
    en = 1.5 * pr + 0.5 * (rho * v2 + b2)
    fast = jnp.sqrt((ADIABATIC * pr + b2) / rho)
    ep = en + pt
    tens = {(i, j): m[i] * v[j] - b[i] * b[j] for i in range(3) for j in range(i, 3)}
    elec = {(i, j): v[i] * b[j] - b[i] * v[j] for i in range(3) for j in range(i + 1, 3)}
    fluxes = []
    for d in range(3):
        rows = [m[d]]
        for c in range(3):
            t = tens[(min(c, d), max(c, d))]
            rows.append(t + pt if c == d else t)
        for c in range(3):
            rows.append(None if c == d else (elec[(d, c)] if d < c else -elec[(c, d)]))
        rows.append(ep * v[d] - b[d] * vb)
        fluxes.append(rows)
    speeds = [jnp.abs(c) + fast for c in v]
    return [rho] + m + list(b) + [en], fluxes, speeds


def face(rows, u, un, f, fn, s, sn):
    a = 0.5 * jnp.maximum(s, sn)
    out = {}
    for c in rows:
        diss = a * (un[c] - u[c])
        out[c] = -diss if f[c] is None else 0.5 * (f[c] + fn[c]) - diss
    return out


def gelu_twice(u):
    u = u.astype(BF16)
    t = jnp.tanh(u * (jnp.asarray(GELU_A, BF16) + jnp.asarray(GELU_B, BF16) * (u * u)))
    return u + u * t


def closure_rates(first, w1, w2, wo):
    us = first
    for w in (w1, w2):
        hs = [jnp.concatenate([gelu_twice(u), bias_rows(u.shape[1]).astype(BF16)], axis=0) for u in us]
        us = [jnp.dot(w, h, preferred_element_type=F32) for h in hs]
    hs = [gelu_twice(u) for u in us]
    scores = [jnp.dot(wo, h, preferred_element_type=F32) for h in hs]
    return [(RATE_LOW + 0.5 * RATE_SPAN) + (0.5 * RATE_SPAN) * jnp.tanh(0.5 * s) for s in scores]


def features(load, z, patch_x=None, patch_y=None):
    zn, zp = lax.rem(z + 1, NZ), lax.rem(z + NZ - 1, NZ)
    row, lane = iota((CX, LANES), 0), iota((CX, LANES), 1)

    def dx(f, v):
        up, dn = next_row(v), prev_row(v)
        if patch_x is not None:
            lo, hi = patch_x(f, z)
            up = jnp.where(row == CX - 1, hi, up)
            dn = jnp.where(row == 0, lo, dn)
        return 0.5 * (up - dn)

    def dy(f, v):
        up, dn = next_lane(v), prev_lane(v)
        if patch_y is not None:
            edge = patch_y(f, z)
            up = jnp.where(lane == LANES - 1, edge, up)
            dn = jnp.where(lane == 0, edge, dn)
        return 0.5 * (up - dn)

    def dz(f):
        return 0.5 * (load(f, zn) - load(f, zp))

    rho, vx, vy, vz, bx, by, bz, pr = [load(f, z) for f in range(8)]
    jx = dy(6, bz) - dz(5)
    jy = dz(4) - dx(6, bz)
    jz = dx(5, by) - dy(4, bx)
    div = dx(1, vx) + dy(2, vy) + dz(3)
    return [jx, jy, jz, div, rho, pr, bx * bx + by * by + bz * bz, vx * vx + vy * vy + vz * vz]


def bias_rows(n):
    return jnp.where(iota((16, n), 0) < 3, 1.0, 0.0)


def plane_at(f, z):
    return pl.ds(pl.multiple_of((f * NZ + z) * CX, CX), CX)


def plane_loader(prim_ref):
    def load(f, z):
        return prim_ref[plane_at(f, z), :]

    return load


def pack_kernel(prim_ref, lo_ref, hi_ref, py_ref):
    lane = iota((8, LANES), 1)
    index = jnp.where(lane % 2 == 0, 0, LANES - 1)
    for f in range(8):
        lo_ref[pl.ds(f * NZ, NZ), :] = prim_ref[pl.ds(f * PLANE, NZ, stride=CX), :]
        hi_ref[pl.ds(f * NZ, NZ), :] = prim_ref[pl.ds(f * PLANE + CX - 1, NZ, stride=CX), :]
        acc = jnp.zeros((8, LANES), F32)
        for z in range(NZ):
            for o in range(2):
                v = prim_ref[pl.ds((f * NZ + z) * CX + o * 8, 8), :]
                acc = jnp.where(lane // 2 == o * NZ + z, take(v, index), acc)
        py_ref[pl.ds(f * 8, 8), :] = acc


def brick_rows(bricks_ref, count_ref):
    lane = iota((8, LANES), 1)
    slot, inner = lane // BRICK, lane % BRICK
    source = jnp.zeros((8, LANES), jnp.int32)
    half = jnp.zeros((8, LANES), jnp.int32)
    back = [jnp.full((8, LANES), -1, jnp.int32) for _ in range(2)]
    per_half = LANES // BRICK
    ends = [[0, 0], [0, 0]]
    for j in range(8):
        b = bricks_ref[0, j]
        bz, by = b // per_half, b % per_half
        source = jnp.where(slot == j, by * BRICK + inner, source)
        half = jnp.where(slot == j, bz, half)
        for h in range(2):
            use = jnp.logical_and(bz == h, j < count_ref[0, 0])
            want = jnp.where(use, by, -1)
            back[h] = jnp.where(slot == want, j * BRICK + inner, back[h])
            for side, end in enumerate((0, per_half - 1)):
                ends[h][side] = jnp.where(want == end, 1, ends[h][side])
    return source, half, back, ends


def mhd_bulk(rows, prim_ref, u_ref, fz_ref, sz_ref, ch_ref, out_ref, unroll):
    load = plane_loader(prim_ref)
    row, lane = iota((CX, LANES), 0), iota((CX, LANES), 1)
    slots = {c: k for k, c in enumerate(rows)}

    @pl.loop(0, NZ, unroll=unroll)
    def _(z):
        u, f, s = derive([load(k, z) for k in range(8)])

        def along(d, nxt, prv, last):
            un = {c: nxt(u[c]) for c in rows}
            fn = {c: None if f[d][c] is None else nxt(f[d][c]) for c in rows}
            fc = face(rows, u, un, f[d], fn, s[d], nxt(s[d]))
            out = {}
            for c in rows:
                inside = jnp.where(last, 0.0, fc[c])
                out[c] = inside - prv(inside)
            return out

        cx = along(0, next_row, prev_row, row == CX - 1)
        cy = along(1, next_lane, prev_lane, lane == LANES - 1)
        for c, k in slots.items():
            ch_ref[plane_at(k, z), :] = u[c] - TIME_STEP * (cx[c] + cy[c])
            u_ref[plane_at(k, z), :] = u[c]
            if f[2][c] is not None:
                fz_ref[plane_at(k, z), :] = f[2][c]
        sz_ref[plane_at(0, z), :] = s[2]

    def zface(z):
        zn = lax.rem(z + 1, NZ)
        u = {c: u_ref[plane_at(k, z), :] for c, k in slots.items()}
        un = {c: u_ref[plane_at(k, zn), :] for c, k in slots.items()}
        f = {c: None if c == 6 else fz_ref[plane_at(k, z), :] for c, k in slots.items()}
        fn = {c: None if c == 6 else fz_ref[plane_at(k, zn), :] for c, k in slots.items()}
        return face(rows, u, un, f, fn, sz_ref[plane_at(0, z), :], sz_ref[plane_at(0, zn), :])

    def finish(z, before):
        here = zface(z)
        for i, (c, k) in enumerate(slots.items()):
            out_ref[plane_at(place(rows, c), z), :] = (
                ch_ref[plane_at(k, z), :] - TIME_STEP * (here[c] - before[i]))
        return tuple(here[c] for c in rows)

    last = zface(NZ - 1)
    lax.fori_loop(0, NZ, finish, tuple(last[c] for c in rows), unroll=unroll)


FIELD_ROWS = (4, 5, 6)
OTHER_ROWS = (0, 1, 2, 3, 7)


def place(rows, c):
    return c - 4 if rows == FIELD_ROWS else c


def y_halo(f, yfl_ref, yfr_ref):
    at = pl.ds(f * 8, 8)
    side0 = iota((8, LANES), 1) % 2 == 0
    return jnp.where(side0, next_lane(yfl_ref[at, :]), prev_lane(yfr_ref[at, :]))


def mhd_ends(rows, prim_ref, py_ref, xlo_ref, xhi_ref, yfl_ref, yfr_ref, out_ref):
    lane8 = iota((8, LANES), 1)
    side0 = lane8 % 2 == 0
    last_lane = jnp.where(lane8 == LANES - 1, 1, 0)
    on_edge = jnp.logical_or(lane8 == 0, lane8 == LANES - 1)
    uh, fh, sh = derive([y_halo(f, yfl_ref, yfr_ref) for f in range(8)])
    uo, fo, so = derive([py_ref[pl.ds(f * 8, 8), :] for f in range(8)])

    def pair(a, b):
        return [None if p is None else jnp.where(side0, p, q) for p, q in zip(a, b)]

    fc = face(rows, pair(uh, uo), pair(uo, uh), pair(fh[1], fo[1]), pair(fo[1], fh[1]),
              jnp.where(side0, sh[1], so[1]), jnp.where(side0, so[1], sh[1]))
    for c in rows:
        delta = jnp.where(side0, TIME_STEP, -TIME_STEP) * fc[c]
        base = place(rows, c) * PLANE
        for z in range(NZ):
            for o in range(2):
                at = pl.ds(base + z * CX + o * 8, 8)
                g = take(delta, (o * NZ + z) * 2 + last_lane)
                out_ref[at, :] = out_ref[at, :] + jnp.where(on_edge, g, 0.0)

    for zs in range(0, NZ, 8):
        for lo in (True, False):
            start = zs * CX + (0 if lo else CX - 1)
            ref = xlo_ref if lo else xhi_ref
            uo, fo, so = derive([prim_ref[pl.ds(f * PLANE + start, 8, stride=CX), :] for f in range(8)])
            uh, fh, sh = derive([ref[pl.ds(f * NZ + zs, 8), :] for f in range(8)])
            if lo:
                fc = face(rows, uh, uo, fh[0], fo[0], sh[0], so[0])
            else:
                fc = face(rows, uo, uh, fo[0], fh[0], so[0], sh[0])
            for c in rows:
                at = pl.ds(place(rows, c) * PLANE + start, 8, stride=CX)
                step = TIME_STEP * fc[c]
                out_ref[at, :] = out_ref[at, :] + (step if lo else -step)


def field_kernel(prim_ref, win_ref, whid_ref, wout_ref, bias_ref,
                 adv_ref, wb_ref, w1_ref, w2_ref, wo_ref,
                 u_ref, fz_ref, sz_ref, ch_ref):
    def split(b):
        hi = b.astype(BF16)
        r = b - hi.astype(F32)
        mid = r.astype(BF16)
        return [hi.astype(F32), mid.astype(F32), r - mid.astype(F32)]

    cols = (((0,), (0,)), ((), ()))
    rows = iota((16, KIN), 0)
    col = iota((16, KIN), 1)
    first = jnp.concatenate(
        [win_ref[...].astype(F32)] + split(bias_ref[0:1, :]) + [jnp.zeros((5, HID), F32)], axis=0
    ).astype(BF16)
    for s in range(8):
        spot = jnp.where(rows < 8, rows * 8 + s, jnp.where(rows < 11, 64 + rows - 8, -1))
        pick = jnp.where(col == spot, 1.0, 0.0).astype(BF16)
        wb_ref[pl.ds(s * HID, HID), :] = lax.dot_general(
            first, pick, cols, preferred_element_type=F32).astype(BF16)
    eye = jnp.where(iota((HID, HID), 0) == iota((HID, HID), 1), 0.5, 0.0).astype(BF16)
    eye16 = jnp.where(iota((16, 16), 0) == iota((16, 16), 1), 1.0, 0.0).astype(BF16)
    for layer, ref in ((0, w1_ref), (1, w2_ref)):
        turned = lax.dot_general(whid_ref[pl.ds(layer * HID, HID), :], eye, cols,
                                 preferred_element_type=F32)
        brow = jnp.concatenate(
            split(bias_ref[layer + 1 : layer + 2, :]) + [jnp.zeros((13, HID), F32)], axis=0
        ).astype(BF16)
        bcol = lax.dot_general(brow, eye16, cols, preferred_element_type=F32)
        ref[...] = jnp.concatenate([turned, bcol], axis=1).astype(BF16)
    wo_ref[...] = jnp.broadcast_to(0.5 * wout_ref[...].astype(F32), (16, HID)).astype(BF16)

    mhd_bulk(FIELD_ROWS, prim_ref, u_ref, fz_ref, sz_ref, ch_ref, adv_ref, 2)


HALF = NZ // 2
WIDE = HALF * LANES


def edge_kernel(bricks_ref, count_ref, prim_ref, advin_ref, py_ref,
                xlo_ref, xhi_ref, yfl_ref, yfr_ref, wb_ref, w1_ref, w2_ref, wo_ref,
                adv_ref, x_ref, kape_ref, sy_ref, sxlo_ref, sxhi_ref,
                feat_ref, yh_ref):
    load = plane_loader(prim_ref)
    lane8 = iota((8, LANES), 1)
    last_lane = jnp.where(lane8 == LANES - 1, 1, 0)
    sub = iota((8, LANES), 0)
    adv_ref[...] = advin_ref[...]
    mhd_ends(FIELD_ROWS, prim_ref, py_ref, xlo_ref, xhi_ref, yfl_ref, yfr_ref, adv_ref)

    source, half, back, ends = brick_rows(bricks_ref, count_ref)
    tail = bias_rows(LANES)
    for f in range(8):
        yh_ref[pl.ds(f * 8, 8), :] = y_halo(f, yfl_ref, yfr_ref)

    def patch_x(f, z):
        return xlo_ref[pl.ds(f * NZ + z, 1), :], xhi_ref[pl.ds(f * NZ + z, 1), :]

    def patch_y(f, z):
        h = yh_ref[pl.ds(f * 8, 8), :]
        return jnp.concatenate([take(h, (o * NZ + z) * 2 + last_lane) for o in range(2)], axis=0)

    @pl.loop(0, HALF)
    def _(z):
        both = []
        for zz in (z, z + HALF):
            fs = features(load, zz, patch_x, patch_y)
            both.append(fs)
            for k in range(8):
                feat_ref[plane_at(k, zz), :] = fs[k]
        at = pl.ds(pl.multiple_of(z * LANES, LANES), LANES)
        for o in range(2):
            parts = []
            for a, b in zip(*both):
                a, b = a[o * 8 : o * 8 + 8], b[o * 8 : o * 8 + 8]
                parts.append(jnp.where(half == 1, take(b, source), take(a, source)))
            x_ref[pl.ds(o * KIN, KIN), at] = jnp.concatenate(parts + [tail], axis=0).astype(BF16)

    inner = lane8 % 8
    index = jnp.where(inner < 4, inner, LANES - 8 + inner)

    def y_pack(ref, base):
        out = {}
        for o in range(2):
            for h in range(2):
                acc = jnp.zeros((8, LANES), F32)
                for z in range(HALF):
                    v = ref[pl.ds(base + (h * HALF + z) * CX + o * 8, 8), :]
                    acc = jnp.where(lane8 // 8 == z, take(v, index), acc)
                out[o, h] = acc
        return out

    packs = [y_pack(feat_ref, k * PLANE) for k in range(8)]
    ycells = jnp.concatenate(
        [jnp.concatenate([p[o, h] for p in packs] + [tail], axis=0) for o in range(2) for h in range(2)],
        axis=1).astype(BF16)
    w1, w2, wo = w1_ref[...], w2_ref[...], wo_ref[...]
    us = []
    for o, s in ((0, 0), (0, 1), (0, 2), (1, 5), (1, 6), (1, 7)):
        us.append(jnp.dot(wb_ref[pl.ds(s * HID, HID), :], x_ref[pl.ds(o * KIN, KIN), :],
                          preferred_element_type=F32))
    uy = [jnp.dot(wb_ref[pl.ds(s * HID, HID), :], ycells, preferred_element_type=F32) for s in range(8)]
    for part in range(2):
        us.append(jnp.concatenate(uy[part * 4 : part * 4 + 4], axis=1))
    rates = closure_rates(us, w1, w2, wo)

    low = jnp.full((NZ, LANES), RATE_LOW, BF16)
    for e in range(6):
        packed = []
        for q in range(2):
            acc = jnp.zeros((8, LANES), F32)
            for k in range(8):
                z = q * 8 + k
                acc = jnp.where(sub == k, rates[e][:8, z * LANES : (z + 1) * LANES], acc)
            packed.append(acc)
            kape_ref[pl.ds(e * HALF + q * 8, 8), :] = acc
        full = []
        for h in range(2):
            listed = back[h] >= 0
            for q in range(2):
                full.append(jnp.where(listed, take(packed[q], jnp.maximum(back[h], 0)), RATE_LOW))
        full = jnp.concatenate(full, axis=0).astype(BF16)
        if e < 3:
            sxlo_ref[pl.ds((12 + e) * NZ, NZ), :] = full
        else:
            sxhi_ref[pl.ds((12 + e - 2) * NZ, NZ), :] = full
    sxlo_ref[pl.ds(15 * NZ, NZ), :] = low
    sxhi_ref[pl.ds(12 * NZ, NZ), :] = low
    for o in range(2):
        for h in range(2):
            acc = jnp.zeros((8, LANES), F32)
            for s in range(8):
                at = (s % 4) * 512 + (o * 2 + h) * LANES
                acc = jnp.where(sub == s, rates[6 + s // 4][:8, at : at + LANES], acc)
            use = jnp.where(inner < 4, ends[h][0], ends[h][1])
            packs[0][o, h] = jnp.where(use == 1, acc, RATE_LOW)
    rate_pack = packs[0]

    for f in range(4):
        got = rate_pack if f == 3 else y_pack(adv_ref, f * PLANE)
        for h in range(2):
            sy_ref[pl.ds((f * 2 + h) * CX, CX), :] = jnp.concatenate(
                [got[0, h], got[1, h]], axis=0).astype(BF16)
        if f < 3:
            for r in range(4):
                at = pl.ds((f * 4 + r) * NZ, NZ)
                sxlo_ref[at, :] = adv_ref[pl.ds(f * PLANE + r, NZ, stride=CX), :].astype(BF16)
                sxhi_ref[at, :] = adv_ref[pl.ds(f * PLANE + CX - 4 + r, NZ, stride=CX), :].astype(BF16)


def inner_kernel(bricks_ref, count_ref, x_ref, kape_ref, wb_ref, w1_ref, w2_ref, wo_ref,
                 kap_ref, kp_ref):
    w1, w2, wo = w1_ref[...], w2_ref[...], wo_ref[...]
    sub = iota((8, LANES), 0)
    _, _, back, _ = brick_rows(bricks_ref, count_ref)
    for o in range(2):
        which = range(3, 8) if o == 0 else range(5)
        us = [jnp.dot(wb_ref[pl.ds(s * HID, HID), :], x_ref[pl.ds(o * KIN, KIN), :],
                      preferred_element_type=F32) for s in which]
        rates = closure_rates(us, w1, w2, wo)
        for z in range(HALF):
            acc = jnp.zeros((8, LANES), F32)
            for s, r in zip(which, rates):
                acc = jnp.where(sub == s, r[:8, z * LANES : (z + 1) * LANES], acc)
            kp_ref[pl.ds(z * CX + o * 8, 8), :] = acc
    for e in range(6):
        x = e if e < 3 else CX - 6 + e
        kp_ref[pl.ds(x, HALF, stride=CX), :] = kape_ref[pl.ds(e * HALF, HALF), :]
    for h in range(2):
        listed = back[h] >= 0
        index = jnp.maximum(back[h], 0)
        for z in range(HALF):
            for o in range(2):
                k = kp_ref[pl.ds(z * CX + o * 8, 8), :]
                kap_ref[pl.ds((h * HALF + z) * CX + o * 8, 8), :] = jnp.where(
                    listed, take(k, index), RATE_LOW)


def corner_kernel(yfl_ref, yfr_ref, sxlo_ref, sxhi_ref, yh_ref, dlo_ref, dhi_ref):
    upper = iota((4 * 2 * CX, LANES), 1) % 8 < 4
    merged = jnp.where(upper, yfr_ref[...].astype(F32), yfl_ref[...].astype(F32))
    yh_ref[...] = merged
    rows = 16 * NZ
    dlo_ref[pl.ds(0, rows), :] = sxlo_ref[...]
    dhi_ref[pl.ds(0, rows), :] = sxhi_ref[...]
    firsts = [merged[k * CX : k * CX + 8] for k in range(8)]
    lasts = [merged[k * CX + 8 : k * CX + 16] for k in range(8)]
    dlo_ref[pl.ds(rows, 64), :] = jnp.concatenate(firsts, axis=0).astype(BF16)
    dhi_ref[pl.ds(rows, 64), :] = jnp.concatenate(lasts, axis=0).astype(BF16)


def others_kernel(prim_ref, py_ref, xlo_ref, xhi_ref, yfl_ref, yfr_ref, out_ref,
                  u_ref, fz_ref, sz_ref, ch_ref):
    mhd_bulk(OTHER_ROWS, prim_ref, u_ref, fz_ref, sz_ref, ch_ref, out_ref, 2)
    mhd_ends(OTHER_ROWS, prim_ref, py_ref, xlo_ref, xhi_ref, yfl_ref, yfr_ref, out_ref)


DEEP = CX + 8
YG = NZ // 4


def diffuse_kernel(out_in_ref, adv_ref, kap_ref, xlo_ref, xhi_ref, yh_ref, out_ref,
                   m0, m1, km, y0, y1, ky, xl, xh):
    comp = pl.program_id(0)
    lane = iota((8, LANES), 1)
    sub = iota((8, LANES), 0)
    window = lane % 32
    block = lane // 32
    own_index = jnp.maximum(jnp.where(window < 16, window - 4, window + 100), 0)
    own_index = jnp.minimum(own_index, LANES - 1)
    on_halo = jnp.logical_or(window < 4, window >= 28)
    halo_index = (block % 2) * 64 + jnp.where(window < 4, 4 + window, window - 28)
    halo_index = jnp.where(on_halo, halo_index, 0)

    def build(field, own_ref, main, edge):
        base = field * (4 * NZ)
        for z in range(NZ):
            main[pl.ds(z * DEEP, CX), :] = own_ref[pl.ds(z * CX, CX), :]
        for r in range(4):
            at = pl.ds(pl.multiple_of(base + r * NZ, 8), NZ)
            main[pl.ds(CX + r, NZ, stride=DEEP), :] = xh[at, :]
            main[pl.ds(CX + 4 + r, NZ, stride=DEEP), :] = xl[at, :]
        for o in range(3):
            halves = []
            for h in range(2):
                if o < 2:
                    at = pl.ds(pl.multiple_of((field * 2 + h) * CX + o * 8, 8), 8)
                    halves.append(yh_ref[at, :])
                else:
                    at = pl.ds(pl.multiple_of(16 * NZ + (field * 2 + h) * 8, 8), 8)
                    halves.append(jnp.where(sub < 4, xh[at, :], xl[at, :]))
            for g in range(YG):
                v = jnp.zeros((8, LANES), F32)
                for b in range(4):
                    piece = main[pl.ds((b * YG + g) * DEEP + o * 8, 8), :]
                    v = jnp.where(block == b, take(piece, own_index), v)
                index = jnp.where(on_halo, halo_index + g * 8, 0)
                got = jnp.where(block < 2, take(halves[0], index), take(halves[1], index))
                edge[pl.ds(g * DEEP + o * 8, 8), :] = jnp.where(on_halo, got, v)

    @pl.when(comp == 0)
    def _():
        xl[...] = xlo_ref[...].astype(F32)
        xh[...] = xhi_ref[...].astype(F32)
        build(3, kap_ref, km, ky)

    build(comp, adv_ref, m0, y0)

    def relax(c, up, dn, k):
        total = next_row(c) + prev_row(c) + next_lane(c) + prev_lane(c) + (up + dn)
        return c + k * (total - 6.0 * c)

    mains, edges = (m0, m1), (y0, y1)
    for step in range(SUB):
        a, b = mains[step % 2], mains[1 - step % 2]
        ea, eb = edges[step % 2], edges[1 - step % 2]

        def at(z):
            return pl.ds(z * DEEP, DEEP)

        dn, c = a[at(NZ - 1), :], a[at(0), :]
        for z in range(NZ):
            up = a[at((z + 1) % NZ), :]
            b[at(z), :] = relax(c, up, dn, km[at(z), :])
            dn, c = c, up

        for g in range(YG):
            up = ea[at(g + 1), :] if g + 1 < YG else pltpu.roll(ea[at(0), :], LANES - 32, 1)
            dn = ea[at(g - 1), :] if g > 0 else pltpu.roll(ea[at(YG - 1), :], 32, 1)
            eb[at(g), :] = relax(ea[at(g), :], up, dn, ky[at(g), :])

    main, edge = mains[SUB % 2], edges[SUB % 2]
    on_edge = jnp.logical_or(lane < 4, lane >= LANES - 4)
    for z in range(NZ):
        b, g = z // YG, z % YG
        index = jnp.where(lane < 4, b * 32 + 4 + lane, b * 32 + 24 + lane - (LANES - 4))
        index = jnp.minimum(jnp.maximum(index, 0), LANES - 1)
        for o in range(2):
            e = take(edge[pl.ds(g * DEEP + o * 8, 8), :], index)
            out_ref[pl.ds(z * CX + o * 8, 8), :] = jnp.where(
                on_edge, e, main[pl.ds(z * DEEP + o * 8, 8), :])


def struct(shape, dtype=F32):
    return jax.ShapeDtypeStruct(shape, dtype)


def params():
    return pltpu.CompilerParams(vmem_limit_bytes=VMEM_LIMIT)


def cost(us):
    return pl.CostEstimate(flops=us * 500_000_000, bytes_accessed=us << 20, transcendentals=0)


VSPEC = pl.BlockSpec(memory_space=pltpu.VMEM)
SSPEC = pl.BlockSpec(memory_space=pltpu.SMEM)


def step_up(axis):
    n = lax.axis_size(axis)
    return [(i, (i + 1) % n) for i in range(n)]


def step_down(axis):
    n = lax.axis_size(axis)
    return [((i + 1) % n, i) for i in range(n)]


def shards(primitive, current_sheet_bricks, brick_count, w_in, w_hid, w_out, b_hid):
    shape = primitive.shape
    prim = primitive.reshape(8 * PLANE, LANES)
    bricks = current_sheet_bricks.reshape(1, -1)
    count = brick_count.reshape(1, 1)

    lo, hi, py = pl.pallas_call(
        pack_kernel,
        out_shape=[struct((8 * NZ, LANES)), struct((8 * NZ, LANES)), struct((64, LANES))],
        compiler_params=params(),
        name="pack",
    )(prim)
    yfl = lax.ppermute(py, "row", step_up("row"))
    yfr = lax.ppermute(py, "row", step_down("row"))
    xlo = lax.ppermute(hi, "col", step_up("col"))
    xhi = lax.ppermute(lo, "col", step_down("col"))

    weights = [struct((8 * HID, KIN), BF16), struct((HID, KHID), BF16), struct((HID, KHID), BF16),
               struct((16, HID), BF16)]

    def mhd_scratch(rows):
        many = pltpu.VMEM((len(rows) * PLANE, LANES), F32)
        return [many, many, pltpu.VMEM((PLANE, LANES), F32), many]

    badv, wb, w1, w2, wo = pl.pallas_call(
        field_kernel,
        out_shape=[struct((3 * PLANE, LANES))] + weights,
        scratch_shapes=mhd_scratch(FIELD_ROWS),
        compiler_params=params(),
        cost_estimate=cost(4),
        name="field",
    )(prim, w_in, w_hid.reshape(2 * HID, HID), w_out.reshape(1, HID), b_hid)

    halos = (py, xlo, xhi, yfl, yfr)
    badv, xcells, kape, sy, sxlo, sxhi = pl.pallas_call(
        edge_kernel,
        in_specs=[SSPEC, SSPEC] + [VSPEC] * 11,
        out_shape=[struct((3 * PLANE, LANES)), struct((2 * KIN, WIDE), BF16), struct((6 * HALF, LANES)),
                   struct((8 * CX, LANES), BF16),
                   struct((16 * NZ, LANES), BF16), struct((16 * NZ, LANES), BF16)],
        scratch_shapes=[pltpu.VMEM((8 * PLANE, LANES), F32), pltpu.VMEM((64, LANES), F32)],
        compiler_params=params(),
        cost_estimate=cost(8),
        name="edges",
    )(bricks, count, prim, badv, *halos, wb, w1, w2, wo)

    hlo = lax.ppermute(sy, "row", step_up("row"))
    hhi = lax.ppermute(sy, "row", step_down("row"))

    kap = pl.pallas_call(
        inner_kernel,
        in_specs=[SSPEC, SSPEC] + [VSPEC] * 6,
        out_shape=struct((PLANE, LANES)),
        scratch_shapes=[pltpu.VMEM((HALF * CX, LANES), F32)],
        compiler_params=params(),
        cost_estimate=cost(6),
        name="inner",
    )(bricks, count, xcells, kape, wb, w1, w2, wo)

    xrows = 16 * NZ + 64
    yh, dlo, dhi = pl.pallas_call(
        corner_kernel,
        out_shape=[struct((8 * CX, LANES)), struct((xrows, LANES), BF16), struct((xrows, LANES), BF16)],
        compiler_params=params(),
        name="corners",
    )(hlo, hhi, sxlo, sxhi)
    gothi = lax.ppermute(dlo, "col", step_down("col"))
    gotlo = lax.ppermute(dhi, "col", step_up("col"))

    rest = pl.pallas_call(
        others_kernel,
        out_shape=struct((8 * PLANE, LANES)),
        scratch_shapes=mhd_scratch(OTHER_ROWS),
        compiler_params=params(),
        cost_estimate=cost(6),
        name="others",
    )(prim, *halos)

    full = lambda rows: pl.BlockSpec((rows, LANES), lambda c: (0, 0))
    out = pl.pallas_call(
        diffuse_kernel,
        grid=(3,),
        in_specs=[pl.BlockSpec(memory_space=pl.ANY), pl.BlockSpec((PLANE, LANES), lambda c: (c, 0)),
                  full(PLANE), full(xrows), full(xrows), full(8 * CX)],
        out_specs=pl.BlockSpec((PLANE, LANES), lambda c: (4 + c, 0)),
        out_shape=struct((8 * PLANE, LANES)),
        input_output_aliases={0: 0},
        scratch_shapes=[pltpu.VMEM((NZ * DEEP, LANES), F32)] * 3
        + [pltpu.VMEM((YG * DEEP, LANES), F32)] * 3
        + [pltpu.VMEM((xrows, LANES), F32)] * 2,
        compiler_params=params(),
        name="diffuse",
    )(rest, badv, kap, gotlo, gothi, yh)
    return out.reshape(shape)


def solution(mesh):
    return jax.shard_map(
        shards,
        mesh=mesh,
        in_specs=(
            P(None, None, "col", "row"),
            P("row", "col", None),
            P("row", "col"),
            P(),
            P(),
            P(),
            P(),
        ),
        out_specs=P(None, None, "col", "row"),
        check_vma=False,
    )
```

```python
import jax
import jax.numpy as jnp
from jax import lax
from jax.experimental import pallas as pl
from jax.experimental.pallas import tpu as pltpu
from jax.sharding import PartitionSpec as P

BRICK = 16
SUB = 4
ADIABATIC = 5.0 / 3.0
TIME_STEP = 0.02
RATE_LOW = 0.02
RATE_SPAN = 0.14
GELU_A = 0.7978845608
GELU_B = 0.7978845608 * 0.044715
F32 = jnp.float32
BF16 = jnp.bfloat16
LANES = 128
NZ = 32
CX = 16
HID = 128
PLANE = NZ * CX
KIN = 80
KHID = HID + 16
VMEM_LIMIT = 48 << 20


def iota(shape, dim):
    return lax.broadcasted_iota(jnp.int32, shape, dim)


def take(values, index):
    return jnp.take_along_axis(values, index, axis=1, mode="promise_in_bounds")


def next_row(v):
    return pltpu.roll(v, v.shape[0] - 1, 0)


def prev_row(v):
    return pltpu.roll(v, 1, 0)


def next_lane(v):
    return pltpu.roll(v, v.shape[1] - 1, 1)


def prev_lane(v):
    return pltpu.roll(v, 1, 1)


def derive(p):
    rho, pr = p[0], p[7]
    v, b = p[1:4], p[4:7]
    m = [rho * c for c in v]
    b2 = b[0] * b[0] + b[1] * b[1] + b[2] * b[2]
    v2 = v[0] * v[0] + v[1] * v[1] + v[2] * v[2]
    vb = v[0] * b[0] + v[1] * b[1] + v[2] * b[2]
    pt = pr + 0.5 * b2
    en = 1.5 * pr + 0.5 * (rho * v2 + b2)
    wave = ADIABATIC * pr + b2
    fast = wave * lax.rsqrt(wave * rho)
    ep = en + pt
    tens = {(i, j): m[i] * v[j] - b[i] * b[j] for i in range(3) for j in range(i, 3)}
    elec = {(i, j): v[i] * b[j] - b[i] * v[j] for i in range(3) for j in range(i + 1, 3)}
    fluxes = []
    for d in range(3):
        rows = [m[d]]
        for c in range(3):
            t = tens[(min(c, d), max(c, d))]
            rows.append(t + pt if c == d else t)
        for c in range(3):
            rows.append(None if c == d else (elec[(d, c)] if d < c else -elec[(c, d)]))
        rows.append(ep * v[d] - b[d] * vb)
        fluxes.append(rows)
    speeds = [jnp.abs(c) + fast for c in v]
    return [rho] + m + list(b) + [en], fluxes, speeds


def face(rows, u, un, f, fn, s, sn):
    a = 0.5 * jnp.maximum(s, sn)
    out = {}
    for c in rows:
        diss = a * (un[c] - u[c])
        out[c] = -diss if f[c] is None else 0.5 * (f[c] + fn[c]) - diss
    return out


def gelu_twice(u):
    u = u.astype(BF16)
    t = jnp.tanh(u * (jnp.asarray(GELU_A, BF16) + jnp.asarray(GELU_B, BF16) * (u * u)))
    return u + u * t


def closure_rates(first, w1, w2, wo):
    us = first
    for w in (w1, w2):
        hs = [jnp.concatenate([gelu_twice(u), bias_rows(u.shape[1]).astype(BF16)], axis=0) for u in us]
        us = [jnp.dot(w, h, preferred_element_type=F32) for h in hs]
    hs = [gelu_twice(u) for u in us]
    scores = [jnp.dot(wo, h, preferred_element_type=F32) for h in hs]
    return [(RATE_LOW + 0.5 * RATE_SPAN) + (0.5 * RATE_SPAN) * jnp.tanh(0.5 * s) for s in scores]


def features(load, z, up_of, dn_of, patch_x=None):
    row = iota((CX, LANES), 0)

    def dx(f, v):
        up, dn = next_row(v), prev_row(v)
        if patch_x is not None:
            lo, hi = patch_x(f, z)
            up = jnp.where(row == CX - 1, hi, up)
            dn = jnp.where(row == 0, lo, dn)
        return 0.5 * (up - dn)

    def dy(v):
        return 0.5 * (next_lane(v) - prev_lane(v))

    def dz(f):
        return 0.5 * (up_of(f, z) - dn_of(f, z))

    rho, vx, vy, vz, bx, by, bz, pr = [load(f, z) for f in range(8)]
    return feature_list(rho, (vx, vy, vz), (bx, by, bz), pr, lambda f, v: dx(f, v), dy, dz)


def feature_list(rho, v, b, pr, dx, dy, dz):
    jx = dy(b[2]) - dz(5)
    jy = dz(4) - dx(6, b[2])
    jz = dx(5, b[1]) - dy(b[0])
    div = dx(1, v[0]) + dy(v[1]) + dz(3)
    return [jx, jy, jz, div, rho, pr, b[0] * b[0] + b[1] * b[1] + b[2] * b[2],
            v[0] * v[0] + v[1] * v[1] + v[2] * v[2]]


def bias_rows(n):
    return jnp.where(iota((16, n), 0) < 3, 1.0, 0.0)


def plane_at(f, z):
    return pl.ds(pl.multiple_of((f * NZ + z) * CX, CX), CX)


def plane_loader(prim_ref):
    def load(f, z):
        return prim_ref[plane_at(f, z), :]

    return load


HALF = NZ // 2
WIDE = HALF * LANES
YG = NZ // 4
YPLANE = YG * CX
ENDS = 8
YROWS = 8 * 2 * CX


def pack_kernel(bricks_ref, count_ref, prim_ref, lo_ref, hi_ref):
    lane = iota((8, LANES), 1)
    spot = lane % ENDS
    for f in range(8):
        for h in range(2):
            los, his = [], []
            for o in range(2):
                lo = jnp.zeros((8, LANES), F32)
                hi = jnp.zeros((8, LANES), F32)
                for z in range(HALF):
                    v = prim_ref[pl.ds((f * NZ + h * HALF + z) * CX + o * 8, 8), :]
                    mine = lane // ENDS == z
                    lo = jnp.where(mine, take(v, spot), lo)
                    hi = jnp.where(mine, take(v, spot + (LANES - ENDS)), hi)
                los.append(lo)
                his.append(hi)
            at = pl.ds((f * 2 + h) * CX, CX)
            lo_ref[at, :] = jnp.concatenate(los, axis=0).astype(BF16)
            hi_ref[at, :] = jnp.concatenate(his, axis=0).astype(BF16)
    _, _, _, ends = brick_rows(bricks_ref, count_ref)
    second = iota((16, LANES), 1) >= LANES // 2
    for ref, side in ((lo_ref, 0), (hi_ref, 1)):
        flag = jnp.where(second, ends[1][side], ends[0][side])
        ref[pl.ds(YROWS, 16), :] = flag.astype(F32).astype(BF16)


def brick_rows(bricks_ref, count_ref):
    lane = iota((8, LANES), 1)
    slot, inner = lane // BRICK, lane % BRICK
    source = jnp.zeros((8, LANES), jnp.int32)
    half = jnp.zeros((8, LANES), jnp.int32)
    back = [jnp.full((8, LANES), -1, jnp.int32) for _ in range(2)]
    per_half = LANES // BRICK
    ends = [[0, 0], [0, 0]]
    for j in range(8):
        b = bricks_ref[0, j]
        bz, by = b // per_half, b % per_half
        source = jnp.where(slot == j, by * BRICK + inner, source)
        half = jnp.where(slot == j, bz, half)
        for h in range(2):
            use = jnp.logical_and(bz == h, j < count_ref[0, 0])
            want = jnp.where(use, by, -1)
            back[h] = jnp.where(slot == want, j * BRICK + inner, back[h])
            for side, end in enumerate((0, per_half - 1)):
                ends[h][side] = jnp.where(want == end, 1, ends[h][side])
    return source, half, back, ends


def mhd_bulk(count, prim_ref, u_ref, fz_ref, sz_ref, ch_ref, out_ref, unroll, windows):
    rows = range(8)
    row, lane = iota((CX, LANES), 0), iota((CX, LANES), 1)

    def at(f, z):
        return pl.ds(pl.multiple_of((f * count + z) * CX, CX), CX)

    @pl.loop(0, count, unroll=unroll)
    def _(z):
        u, f, s = derive([prim_ref[at(k, z), :] for k in rows])

        def along(d, nxt, prv, last):
            un = {c: nxt(u[c]) for c in rows}
            fn = {c: None if f[d][c] is None else nxt(f[d][c]) for c in rows}
            fc = face(rows, u, un, f[d], fn, s[d], nxt(s[d]))
            out = {}
            for c in rows:
                inside = fc[c] if last is None else jnp.where(last, 0.0, fc[c])
                out[c] = inside - prv(inside)
            return out

        cx = along(0, next_row, prev_row, row == CX - 1)
        cy = along(1, next_lane, prev_lane, None if windows else lane == LANES - 1)
        for c in rows:
            ch_ref[at(c, z), :] = u[c] - TIME_STEP * (cx[c] + cy[c])
            u_ref[at(c, z), :] = u[c]
            if f[2][c] is not None:
                fz_ref[at(c, z), :] = f[2][c]
        sz_ref[at(0, z), :] = s[2]

    def zface(z, zn, turn):
        u = {c: u_ref[at(c, z), :] for c in rows}
        un = {c: turn(u_ref[at(c, zn), :]) for c in rows}
        f = {c: None if c == 6 else fz_ref[at(c, z), :] for c in rows}
        fn = {c: None if c == 6 else turn(fz_ref[at(c, zn), :]) for c in rows}
        return face(rows, u, un, f, fn, sz_ref[at(0, z), :], turn(sz_ref[at(0, zn), :]))

    def finish(z, before, here):
        for c in rows:
            out_ref[at(c, z), :] = ch_ref[at(c, z), :] - TIME_STEP * (here[c] - before[c])
        return tuple(here[c] for c in rows)

    if windows:
        last = zface(count - 1, 0, lambda v: pltpu.roll(v, LANES - 32, 1))
        before = tuple(pltpu.roll(last[c], 32, 1) for c in rows)
        for z in range(count):
            here = last if z == count - 1 else zface(z, z + 1, lambda v: v)
            before = finish(z, before, here)
    else:
        def step(z, before):
            return finish(z, before, zface(z, lax.rem(z + 1, count), lambda v: v))

        last = zface(count - 1, 0, lambda v: v)
        lax.fori_loop(0, count, step, tuple(last[c] for c in rows), unroll=unroll)


def x_ends(own_of, halo_of, lo, add):
    rows = range(8)
    uo, fo, so = derive([own_of(f) for f in rows])
    uh, fh, sh = derive([halo_of(f) for f in rows])
    if lo:
        fc = face(rows, uh, uo, fh[0], fo[0], sh[0], so[0])
    else:
        fc = face(rows, uo, uh, fo[0], fh[0], so[0], sh[0])
    for c in rows:
        step = TIME_STEP * fc[c]
        add(c, step if lo else -step)


def bulk_kernel(prim_ref, adv_ref, xlo_ref, xhi_ref, u_ref, fz_ref, sz_ref, ch_ref):
    mhd_bulk(NZ, prim_ref, u_ref, fz_ref, sz_ref, ch_ref, adv_ref, 4, False)
    for f in range(8):
        at = pl.ds(f * NZ, NZ)
        xlo_ref[at, :] = prim_ref[pl.ds(f * PLANE, NZ, stride=CX), :].astype(BF16)
        xhi_ref[at, :] = prim_ref[pl.ds(f * PLANE + CX - 1, NZ, stride=CX), :].astype(BF16)


def window_kernel(prim_ref, yfl_ref, yfr_ref, xlo_ref, xhi_ref, yp_ref, sxlo_ref, sxhi_ref,
                  left_ref, right_ref):
    lane = iota((8, LANES), 1)
    window, block = lane % 32, lane // 32
    own = jnp.where(window < 16, window - 6, LANES - 26 + window)
    own = jnp.minimum(jnp.maximum(own, 0), LANES - 1)
    spot = (block % 2) * 64 + jnp.where(window < 16, jnp.minimum(window + 2, 7), jnp.maximum(window - 26, 0))
    left_ref[...] = yfl_ref[pl.ds(0, YROWS), :].astype(F32)
    right_ref[...] = yfr_ref[pl.ds(0, YROWS), :].astype(F32)
    low, high, first = window < 6, window >= 26, block < 2
    for f in range(8):
        for o in range(2):
            here = [[ref[pl.ds((f * 2 + h) * CX + o * 8, 8), :] for h in range(2)]
                    for ref in (left_ref, right_ref)]
            for g in range(YG):
                v = None
                for b in range(4):
                    piece = take(prim_ref[pl.ds((f * NZ + b * YG + g) * CX + o * 8, 8), :], own)
                    v = piece if v is None else jnp.where(block == b, piece, v)
                index = spot + g * ENDS
                for side, where in ((0, low), (1, high)):
                    got = jnp.where(first, take(here[side][0], index), take(here[side][1], index))
                    v = jnp.where(where, got, v)
                yp_ref[pl.ds((f * YG + g) * CX + o * 8, 8), :] = v
    rows = 8 * NZ
    sxlo_ref[pl.ds(0, rows), :] = xlo_ref[...]
    sxhi_ref[pl.ds(0, rows), :] = xhi_ref[...]
    for f in range(0, 8, 2):
        for ref, start in ((sxlo_ref, 0), (sxhi_ref, CX - 1)):
            ref[pl.ds(rows + f * YG, 2 * YG), :] = yp_ref[
                pl.ds(f * YPLANE + start, 2 * YG, stride=CX), :].astype(BF16)


def ready_kernel(bricks_ref, count_ref, prim_ref, yp_ref, win_ref, whid_ref, wout_ref, bias_ref,
                 yadv_ref, x_ref, wb_ref, w1_ref, w2_ref, wo_ref,
                 u_ref, fz_ref, sz_ref, ch_ref):
    def split(b):
        hi = b.astype(BF16)
        r = b - hi.astype(F32)
        mid = r.astype(BF16)
        return [hi.astype(F32), mid.astype(F32), r - mid.astype(F32)]

    cols = (((0,), (0,)), ((), ()))
    rows = iota((16, KIN), 0)
    col = iota((16, KIN), 1)
    first = jnp.concatenate(
        [win_ref[...].astype(F32)] + split(bias_ref[0:1, :]) + [jnp.zeros((5, HID), F32)], axis=0
    ).astype(BF16)
    for s in range(8):
        spot = jnp.where(rows < 8, rows * 8 + s, jnp.where(rows < 11, 64 + rows - 8, -1))
        pick = jnp.where(col == spot, 1.0, 0.0).astype(BF16)
        wb_ref[pl.ds(s * HID, HID), :] = lax.dot_general(
            first, pick, cols, preferred_element_type=F32).astype(BF16)
    eye = jnp.where(iota((HID, HID), 0) == iota((HID, HID), 1), 0.5, 0.0).astype(BF16)
    eye16 = jnp.where(iota((16, 16), 0) == iota((16, 16), 1), 1.0, 0.0).astype(BF16)
    for layer, ref in ((0, w1_ref), (1, w2_ref)):
        turned = lax.dot_general(whid_ref[pl.ds(layer * HID, HID), :], eye, cols,
                                 preferred_element_type=F32)
        brow = jnp.concatenate(
            split(bias_ref[layer + 1 : layer + 2, :]) + [jnp.zeros((13, HID), F32)], axis=0
        ).astype(BF16)
        bcol = lax.dot_general(brow, eye16, cols, preferred_element_type=F32)
        ref[...] = jnp.concatenate([turned, bcol], axis=1).astype(BF16)
    wo_ref[...] = jnp.broadcast_to(0.5 * wout_ref[...].astype(F32), (16, HID)).astype(BF16)

    mhd_bulk(YG, yp_ref, u_ref, fz_ref, sz_ref, ch_ref, yadv_ref, 4, True)

    source, half, _, _ = brick_rows(bricks_ref, count_ref)
    tail = bias_rows(LANES)
    load = plane_loader(prim_ref)

    def up_of(f, z):
        return load(f, lax.rem(z + 1, NZ))

    def dn_of(f, z):
        return load(f, lax.rem(z + NZ - 1, NZ))

    @pl.loop(0, HALF, unroll=4)
    def _(z):
        both = [features(load, zz, up_of, dn_of) for zz in (z, z + HALF)]
        at = pl.ds(pl.multiple_of(z * LANES, LANES), LANES)
        for o in range(2):
            parts = []
            for a, b in zip(*both):
                a, b = a[o * 8 : o * 8 + 8], b[o * 8 : o * 8 + 8]
                parts.append(jnp.where(half == 1, take(b, source), take(a, source)))
            x_ref[pl.ds(o * KIN, KIN), at] = jnp.concatenate(parts + [tail], axis=0).astype(BF16)


def edge_kernel(bricks_ref, count_ref, prim_ref, bulk_ref, yp_ref, ybulk_ref, x_ref,
                xlo_ref, xhi_ref, yfl_ref, yfr_ref, wb_ref, w1_ref, w2_ref, wo_ref,
                rest_ref, badv_ref, yb_ref, ky_ref, kape_ref, sxlo_ref, sxhi_ref,
                lo_ref, hi_ref, yadv_ref):
    lane8 = iota((8, LANES), 1)
    sub = iota((8, LANES), 0)
    lo_ref[...] = xlo_ref[...].astype(F32)
    hi_ref[...] = xhi_ref[...].astype(F32)
    yrows = 8 * NZ

    yadv_ref[...] = ybulk_ref[...]
    badv_ref[...] = bulk_ref[pl.ds(4 * PLANE, 3 * PLANE), :]
    for lo in (True, False):
        start = 0 if lo else CX - 1
        ref = lo_ref if lo else hi_ref

        def add_window(c, step):
            at = pl.ds(c * YPLANE + start, YG, stride=CX)
            yadv_ref[at, :] = yadv_ref[at, :] + step

        x_ends(lambda f: yp_ref[pl.ds(f * YPLANE + start, YG, stride=CX), :],
               lambda f: ref[pl.ds(yrows + f * YG, YG), :], lo, add_window)
    yb_ref[...] = yadv_ref[pl.ds(4 * YPLANE, 3 * YPLANE), :]
    on_edge = jnp.logical_or(lane8 == 0, lane8 == LANES - 1)
    for c in (0, 1, 2, 3, 7):
        for z in range(NZ):
            b, g = z // YG, z % YG
            index = b * 32 + jnp.where(lane8 == LANES - 1, 25, 6)
            for o in range(2):
                at = pl.ds(c * PLANE + z * CX + o * 8, 8)
                edge = take(yadv_ref[pl.ds(c * YPLANE + g * CX + o * 8, 8), :], index)
                rest_ref[at, :] = jnp.where(on_edge, edge, bulk_ref[at, :])
    at_end = jnp.logical_or(lane8 == 0, lane8 == LANES - 1)
    for zs in range(0, NZ, 8):
        for lo in (True, False):
            start = zs * CX + (0 if lo else CX - 1)
            ref = lo_ref if lo else hi_ref

            def add_block(c, step):
                if 4 <= c < 7:
                    at = pl.ds((c - 4) * PLANE + start, 8, stride=CX)
                    badv_ref[at, :] = badv_ref[at, :] + step
                else:
                    at = pl.ds(c * PLANE + start, 8, stride=CX)
                    rest_ref[at, :] = rest_ref[at, :] + jnp.where(at_end, 0.0, step)

            x_ends(lambda f: prim_ref[pl.ds(f * PLANE + start, 8, stride=CX), :],
                   lambda f: ref[pl.ds(f * NZ + zs, 8), :], lo, add_block)

    source, half, back, ends = brick_rows(bricks_ref, count_ref)
    tail = bias_rows(LANES)
    parts = []
    for lo in (True, False):
        start = 0 if lo else CX - 1
        ref = lo_ref if lo else hi_ref

        def row_of(f, x=start):
            return prim_ref[pl.ds(f * PLANE + x, NZ, stride=CX), :]

        def dx(f, v):
            beyond = ref[pl.ds(f * NZ, NZ), :]
            within = row_of(f, start + (1 if lo else -1))
            return 0.5 * (within - beyond) if lo else 0.5 * (beyond - within)

        def dy(v):
            return 0.5 * (next_lane(v) - prev_lane(v))

        p = [row_of(f) for f in range(8)]

        def dz(f):
            return 0.5 * (next_row(p[f]) - prev_row(p[f]))

        fs = feature_list(p[0], p[1:4], p[4:7], p[7], dx, dy, dz)
        for q in range(2):
            packed = [jnp.where(half == 1, take(v[HALF + q * 8 : HALF + q * 8 + 8], source),
                                take(v[q * 8 : q * 8 + 8], source)) for v in fs]
            parts.append(jnp.concatenate(packed + [tail], axis=0))
    xend = jnp.concatenate(parts, axis=1).astype(BF16)

    def yload(f, z):
        return yp_ref[pl.ds((f * YG + z) * CX, CX), :]

    def yup(f, z):
        return yload(f, z + 1) if z + 1 < YG else pltpu.roll(yload(f, 0), LANES - 32, 1)

    def ydn(f, z):
        return yload(f, z - 1) if z > 0 else pltpu.roll(yload(f, YG - 1), 32, 1)

    def patch_x(f, z):
        at = pl.ds(yrows + f * YG + z, 1)
        return lo_ref[at, :], hi_ref[at, :]

    window, block = lane8 % 32, lane8 // 32
    inner = window % 8
    from_window = block * 32 + jnp.where(inner < 4, inner + 3, inner + 21)
    ycells = {(o, q): [jnp.zeros((8, LANES), F32)] * 8 for o in range(2) for q in range(2)}
    for g in range(YG):
        fs = features(yload, g, yup, ydn, patch_x)
        mine = window // 8 == g % 4
        for o in range(2):
            ycells[o, g // 4] = [jnp.where(mine, take(v[o * 8 : o * 8 + 8], from_window), a)
                                 for v, a in zip(fs, ycells[o, g // 4])]
    yend = jnp.concatenate([jnp.concatenate(ycells[o, q] + [tail], axis=0)
                            for o in range(2) for q in range(2)], axis=1).astype(BF16)

    us = []
    for o, s in ((0, 1), (0, 2), (1, 5), (1, 6)):
        us.append(jnp.dot(wb_ref[pl.ds(s * HID, HID), :], x_ref[pl.ds(o * KIN, KIN), :],
                          preferred_element_type=F32))
    for cells in (xend, yend):
        ue = [jnp.dot(wb_ref[pl.ds(s * HID, HID), :], cells, preferred_element_type=F32) for s in range(8)]
        for part in range(2):
            us.append(jnp.concatenate(ue[part * 4 : part * 4 + 4], axis=1))
    rates = closure_rates(us, w1_ref[...], w2_ref[...], wo_ref[...])

    def by_row(first, k):
        acc = jnp.zeros((8, LANES), F32)
        for s in range(8):
            at = (s % 4) * 512 + k * LANES
            acc = jnp.where(sub == s, rates[first + s // 4][:8, at : at + LANES], acc)
        return acc

    low = jnp.full((NZ, LANES), RATE_LOW, BF16)
    for e in range(6):
        packed = []
        for q in range(2):
            if e in (0, 5):
                acc = by_row(4, (0 if e == 0 else 2) + q)
            else:
                acc = jnp.zeros((8, LANES), F32)
                for k in range(8):
                    z = q * 8 + k
                    acc = jnp.where(sub == k, rates[e - 1][:8, z * LANES : (z + 1) * LANES], acc)
            packed.append(acc)
            kape_ref[pl.ds(e * HALF + q * 8, 8), :] = acc
        full = []
        for h in range(2):
            listed = back[h] >= 0
            for q in range(2):
                full.append(jnp.where(listed, take(packed[q], jnp.maximum(back[h], 0)), RATE_LOW))
        full = jnp.concatenate(full, axis=0).astype(BF16)
        if e < 3:
            sxlo_ref[pl.ds((12 + e) * NZ, NZ), :] = full
        else:
            sxhi_ref[pl.ds((12 + e - 2) * NZ, NZ), :] = full
    sxlo_ref[pl.ds(15 * NZ, NZ), :] = low
    sxhi_ref[pl.ds(12 * NZ, NZ), :] = low

    second = lane8 >= LANES // 2
    mine = jnp.where(window < 16, jnp.where(second, ends[1][0], ends[0][0]),
                     jnp.where(second, ends[1][1], ends[0][1]))
    left = yfl_ref[pl.ds(YROWS, 16), :].astype(F32)[:8]
    right = yfr_ref[pl.ds(YROWS, 16), :].astype(F32)[:8]
    listed = jnp.where(window < 6, left, jnp.where(window >= 26, right, mine.astype(F32))) > 0.5
    known = jnp.where(window < 16, window - 3, window - 21)
    known = jnp.minimum(jnp.maximum(known, 0), 7)
    for o in range(2):
        for q in range(2):
            got = by_row(6, o * 2 + q)
            for g in range(4):
                k = take(got, block * 32 + g * 8 + known)
                ky_ref[pl.ds((q * 4 + g) * CX + o * 8, 8), :] = jnp.where(listed, k, RATE_LOW)

    for f in range(3):
        for r in range(4):
            at = pl.ds((f * 4 + r) * NZ, NZ)
            sxlo_ref[at, :] = badv_ref[pl.ds(f * PLANE + r, NZ, stride=CX), :].astype(BF16)
            sxhi_ref[at, :] = badv_ref[pl.ds(f * PLANE + CX - 4 + r, NZ, stride=CX), :].astype(BF16)
    for f in range(4):
        ref, base = (yb_ref, f * YPLANE) if f < 3 else (ky_ref, 0)
        for dst, start in ((sxlo_ref, 0), (sxhi_ref, CX - 4)):
            for r in range(0, 4, 2):
                pair = [ref[pl.ds(base + start + r + k, YG, stride=CX), :] for k in range(2)]
                dst[pl.ds(16 * NZ + (f * 4 + r) * YG, 2 * YG), :] = jnp.concatenate(pair, axis=0).astype(BF16)


def inner_rates(o, x_ref, wb_ref, w1_ref, w2_ref, wo_ref, kp_ref):
    sub = iota((8, LANES), 0)
    which = range(3, 8) if o == 0 else range(5)
    us = [jnp.dot(wb_ref[pl.ds(s * HID, HID), :], x_ref[pl.ds(o * KIN, KIN), :],
                  preferred_element_type=F32) for s in which]
    rates = closure_rates(us, w1_ref[...], w2_ref[...], wo_ref[...])
    for z in range(HALF):
        acc = jnp.zeros((8, LANES), F32)
        for s, r in zip(which, rates):
            acc = jnp.where(sub == s, r[:8, z * LANES : (z + 1) * LANES], acc)
        kp_ref[pl.ds(z * 8, 8), :] = acc


def inner_kernel(bricks_ref, count_ref, x_ref, kape_ref, wb_ref, w1_ref, w2_ref, wo_ref,
                 kap_ref, kp_ref):
    rows = HALF * 8
    for o in range(2):
        inner_rates(o, x_ref, wb_ref, w1_ref, w2_ref, wo_ref, kp_ref.at[pl.ds(o * rows, rows), :])
    _, _, back, _ = brick_rows(bricks_ref, count_ref)
    for e in range(6):
        x = e if e < 3 else rows + 2 + e
        kp_ref[pl.ds(x, HALF, stride=8), :] = kape_ref[pl.ds(e * HALF, HALF), :]
    for h in range(2):
        listed = back[h] >= 0
        index = jnp.maximum(back[h], 0)
        for z in range(HALF):
            for o in range(2):
                k = kp_ref[pl.ds(o * rows + z * 8, 8), :]
                kap_ref[pl.ds((h * HALF + z) * CX + o * 8, 8), :] = jnp.where(
                    listed, take(k, index), RATE_LOW)


DEEP = CX + 8


def diffuse_kernel(rest_ref, b_ref, kap_ref, yb_ref, kapy_ref, xlo_ref, xhi_ref, out_ref,
                   m0, m1, km, y0, y1, ky, xl, xh):
    comp = pl.program_id(0)
    lane = iota((8, LANES), 1)
    window, block = lane % 32, lane // 32

    def build(field, own_ref, yown_ref, main, edge):
        for z in range(NZ):
            main[pl.ds(z * DEEP, CX), :] = own_ref[pl.ds(z * CX, CX), :]
        for g in range(YG):
            edge[pl.ds(g * DEEP, CX), :] = yown_ref[pl.ds(g * CX, CX), :]
        for r in range(4):
            for src, row in ((xh, CX + r), (xl, CX + 4 + r)):
                at = pl.ds(pl.multiple_of((field * 4 + r) * NZ, 8), NZ)
                main[pl.ds(row, NZ, stride=DEEP), :] = src[at, :]
                at = pl.ds(pl.multiple_of(16 * NZ + (field * 4 + r) * YG, 8), YG)
                edge[pl.ds(row, YG, stride=DEEP), :] = src[at, :]

    @pl.when(comp == 0)
    def _():
        xl[...] = xlo_ref[...].astype(F32)
        xh[...] = xhi_ref[...].astype(F32)
        build(3, kap_ref, kapy_ref, km, ky)
        own = jnp.where(window < 16, window - 6, LANES - 26 + window)
        own = jnp.minimum(jnp.maximum(own, 0), LANES - 1)
        made = jnp.logical_or(window < 7, window >= 25)
        for g in range(YG):
            for o in range(3):
                v = None
                for b in range(4):
                    piece = take(km[pl.ds((b * YG + g) * DEEP + o * 8, 8), :], own)
                    v = piece if v is None else jnp.where(block == b, piece, v)
                at = pl.ds(g * DEEP + o * 8, 8)
                ky[at, :] = jnp.where(made, ky[at, :], v)

    build(comp, b_ref, yb_ref, m0, y0)

    def relax(c, up, dn, k):
        total = next_row(c) + prev_row(c) + next_lane(c) + prev_lane(c) + (up + dn)
        return c + k * (total - 6.0 * c)

    def at(z):
        return pl.ds(z * DEEP, DEEP)

    on_edge = jnp.logical_or(lane < 5, lane >= LANES - 5)
    mains, edges = (m0, m1), (y0, y1)
    for step in range(SUB):
        a, b = mains[step % 2], mains[1 - step % 2]
        ea, eb = edges[step % 2], edges[1 - step % 2]
        for g in range(YG):
            up = ea[at(g + 1), :] if g + 1 < YG else pltpu.roll(ea[at(0), :], LANES - 32, 1)
            dn = ea[at(g - 1), :] if g > 0 else pltpu.roll(ea[at(YG - 1), :], 32, 1)
            eb[at(g), :] = relax(ea[at(g), :], up, dn, ky[at(g), :])
        dn, c = a[at(NZ - 1), :], a[at(0), :]
        for z in range(NZ):
            up = a[at((z + 1) % NZ), :]
            new = relax(c, up, dn, km[at(z), :])
            dn, c = c, up
            if step < SUB - 1:
                b[at(z), :] = new
                continue
            k, g = z // YG, z % YG
            index = k * 32 + jnp.where(lane < 5, 6 + lane, lane - (LANES - 26))
            index = jnp.minimum(jnp.maximum(index, 0), LANES - 1)
            for o in range(2):
                e = take(eb[pl.ds(g * DEEP + o * 8, 8), :], index)
                out_ref[pl.ds(z * CX + o * 8, 8), :] = jnp.where(on_edge, e, new[o * 8 : o * 8 + 8])


def struct(shape, dtype=F32):
    return jax.ShapeDtypeStruct(shape, dtype)


def params():
    return pltpu.CompilerParams(vmem_limit_bytes=VMEM_LIMIT)


def cost(us):
    return pl.CostEstimate(flops=us * 500_000_000, bytes_accessed=us << 20, transcendentals=0)


VSPEC = pl.BlockSpec(memory_space=pltpu.VMEM)
SSPEC = pl.BlockSpec(memory_space=pltpu.SMEM)


def step_up(axis):
    n = lax.axis_size(axis)
    return [(i, (i + 1) % n) for i in range(n)]


def step_down(axis):
    n = lax.axis_size(axis)
    return [((i + 1) % n, i) for i in range(n)]


def shards(primitive, current_sheet_bricks, brick_count, w_in, w_hid, w_out, b_hid):
    shape = primitive.shape
    prim = primitive.reshape(8 * PLANE, LANES)
    bricks = current_sheet_bricks.reshape(1, -1)
    count = brick_count.reshape(1, 1)

    blo, bhi = pl.pallas_call(
        pack_kernel,
        in_specs=[SSPEC, SSPEC, VSPEC],
        out_shape=[struct((YROWS + 16, LANES), BF16)] * 2,
        compiler_params=params(),
        name="pack",
    )(bricks, count, prim)
    yfl = lax.ppermute(bhi, "row", step_up("row"))
    yfr = lax.ppermute(blo, "row", step_down("row"))

    def mhd_scratch(planes):
        many = pltpu.VMEM((8 * planes * CX, LANES), F32)
        return [many, many, pltpu.VMEM((planes * CX, LANES), F32), many]

    adv, xmlo, xmhi = pl.pallas_call(
        bulk_kernel,
        out_shape=[struct((8 * PLANE, LANES))] + [struct((8 * NZ, LANES), BF16)] * 2,
        scratch_shapes=mhd_scratch(NZ),
        compiler_params=params(),
        cost_estimate=cost(4),
        name="bulk",
    )(prim)

    sxrows = 8 * NZ + 8 * YG
    yp, slo, shi = pl.pallas_call(
        window_kernel,
        out_shape=[struct((8 * YPLANE, LANES))] + [struct((sxrows, LANES), BF16)] * 2,
        scratch_shapes=[pltpu.VMEM((YROWS, LANES), F32)] * 2,
        compiler_params=params(),
        cost_estimate=cost(1),
        name="windows",
    )(prim, yfl, yfr, xmlo, xmhi)
    xlo = lax.ppermute(shi, "col", step_up("col"))
    xhi = lax.ppermute(slo, "col", step_down("col"))

    weights = [struct((8 * HID, KIN), BF16), struct((HID, KHID), BF16), struct((HID, KHID), BF16),
               struct((16, HID), BF16)]
    yadv, xcells, *closure = pl.pallas_call(
        ready_kernel,
        in_specs=[SSPEC, SSPEC] + [VSPEC] * 6,
        out_shape=[struct((8 * YPLANE, LANES)), struct((2 * KIN, WIDE), BF16)] + weights,
        scratch_shapes=mhd_scratch(YG),
        compiler_params=params(),
        cost_estimate=cost(4),
        name="ready",
    )(bricks, count, prim, yp, w_in, w_hid.reshape(2 * HID, HID), w_out.reshape(1, HID), b_hid)

    xrows = 16 * NZ + 16 * YG
    rest, badv, yb, ky, kape, sxlo, sxhi = pl.pallas_call(
        edge_kernel,
        in_specs=[SSPEC, SSPEC] + [VSPEC] * 13,
        out_shape=[struct((8 * PLANE, LANES)), struct((3 * PLANE, LANES)), struct((3 * YPLANE, LANES)),
                   struct((YPLANE, LANES)), struct((6 * HALF, LANES)),
                   struct((xrows, LANES), BF16), struct((xrows, LANES), BF16)],
        scratch_shapes=[pltpu.VMEM((sxrows, LANES), F32)] * 2 + [pltpu.VMEM((8 * YPLANE, LANES), F32)],
        compiler_params=params(),
        cost_estimate=cost(8),
        name="edges",
    )(bricks, count, prim, adv, yp, yadv, xcells, xlo, xhi, yfl, yfr, *closure)

    gothi = lax.ppermute(sxlo, "col", step_down("col"))
    gotlo = lax.ppermute(sxhi, "col", step_up("col"))

    kap = pl.pallas_call(
        inner_kernel,
        in_specs=[SSPEC, SSPEC] + [VSPEC] * 6,
        out_shape=struct((PLANE, LANES)),
        scratch_shapes=[pltpu.VMEM((HALF * CX, LANES), F32)],
        compiler_params=params(),
        cost_estimate=cost(6),
        name="inner",
    )(bricks, count, xcells, kape, *closure)

    full = lambda rows: pl.BlockSpec((rows, LANES), lambda c: (0, 0))
    part = lambda rows: pl.BlockSpec((rows, LANES), lambda c: (c, 0))
    out = pl.pallas_call(
        diffuse_kernel,
        grid=(3,),
        in_specs=[pl.BlockSpec(memory_space=pl.ANY), part(PLANE), full(PLANE), part(YPLANE), full(YPLANE),
                  full(xrows), full(xrows)],
        out_specs=pl.BlockSpec((PLANE, LANES), lambda c: (4 + c, 0)),
        out_shape=struct((8 * PLANE, LANES)),
        input_output_aliases={0: 0},
        scratch_shapes=[pltpu.VMEM((NZ * DEEP, LANES), F32)] * 3
        + [pltpu.VMEM((YG * DEEP, LANES), F32)] * 3
        + [pltpu.VMEM((xrows, LANES), F32)] * 2,
        compiler_params=params(),
        name="diffuse",
    )(rest, badv, kap, yb, ky, gotlo, gothi)
    return out.reshape(shape)


def solution(mesh):
    return jax.shard_map(
        shards,
        mesh=mesh,
        in_specs=(
            P(None, None, "col", "row"),
            P("row", "col", None),
            P("row", "col"),
            P(),
            P(),
            P(),
            P(),
        ),
        out_specs=P(None, None, "col", "row"),
        check_vma=False,
    )
```

```python
import jax
import jax.numpy as jnp
from jax import lax
from jax.experimental import pallas as pl
from jax.experimental.pallas import tpu as pltpu
from jax.sharding import PartitionSpec as P

BRICK = 16
SUB = 4
ADIABATIC = 5.0 / 3.0
TIME_STEP = 0.02
RATE_LOW = 0.02
RATE_SPAN = 0.14
GELU_A = 0.7978845608
GELU_B = 0.7978845608 * 0.044715
F32 = jnp.float32
BF16 = jnp.bfloat16
LANES = 128
NZ = 32
CX = 16
HID = 128
PLANE = NZ * CX
KIN = 80
KHID = HID + 16


def iota(shape, dim):
    return lax.broadcasted_iota(jnp.int32, shape, dim)


def take(values, index):
    return jnp.take_along_axis(values, index, axis=1, mode="promise_in_bounds")


def next_row(v):
    return pltpu.roll(v, v.shape[0] - 1, 0)


def prev_row(v):
    return pltpu.roll(v, 1, 0)


def next_lane(v):
    return pltpu.roll(v, v.shape[1] - 1, 1)


def prev_lane(v):
    return pltpu.roll(v, 1, 1)


def derive(p):
    rho, pr = p[0], p[7]
    v, b = p[1:4], p[4:7]
    m = [rho * c for c in v]
    b2 = b[0] * b[0] + b[1] * b[1] + b[2] * b[2]
    v2 = v[0] * v[0] + v[1] * v[1] + v[2] * v[2]
    vb = v[0] * b[0] + v[1] * b[1] + v[2] * b[2]
    pt = pr + 0.5 * b2
    en = 1.5 * pr + 0.5 * (rho * v2 + b2)
    wave = ADIABATIC * pr + b2
    fast = wave * lax.rsqrt(wave * rho)
    ep = en + pt
    tens = {(i, j): m[i] * v[j] - b[i] * b[j] for i in range(3) for j in range(i, 3)}
    elec = {(i, j): v[i] * b[j] - b[i] * v[j] for i in range(3) for j in range(i + 1, 3)}
    fluxes = []
    for d in range(3):
        rows = [m[d]]
        for c in range(3):
            t = tens[(min(c, d), max(c, d))]
            rows.append(t + pt if c == d else t)
        for c in range(3):
            rows.append(None if c == d else (elec[(d, c)] if d < c else -elec[(c, d)]))
        rows.append(ep * v[d] - b[d] * vb)
        fluxes.append(rows)
    speeds = [jnp.abs(c) + fast for c in v]
    return [rho] + m + list(b) + [en], fluxes, speeds


def face(rows, u, un, f, fn, s, sn):
    a = 0.5 * jnp.maximum(s, sn)
    out = {}
    for c in rows:
        diss = a * (un[c] - u[c])
        out[c] = -diss if f[c] is None else 0.5 * (f[c] + fn[c]) - diss
    return out


def gelu_twice(u):
    u = u.astype(BF16)
    t = jnp.tanh(u * (jnp.asarray(GELU_A, BF16) + jnp.asarray(GELU_B, BF16) * (u * u)))
    return u + u * t


def closure_rates(first, w1, w2, wo):
    us = first
    for w in (w1, w2):
        hs = [jnp.concatenate([gelu_twice(u), bias_rows(u.shape[1]).astype(BF16)], axis=0) for u in us]
        us = [jnp.dot(w, h, preferred_element_type=F32) for h in hs]
    hs = [gelu_twice(u) for u in us]
    scores = [jnp.dot(wo, h, preferred_element_type=F32) for h in hs]
    return [(RATE_LOW + 0.5 * RATE_SPAN) + (0.5 * RATE_SPAN) * jnp.tanh(0.5 * s) for s in scores]


def features(load, z, up_of, dn_of, patch_x=None):
    row = iota((CX, LANES), 0)

    def dx(f, v):
        up, dn = next_row(v), prev_row(v)
        if patch_x is not None:
            lo, hi = patch_x(f, z)
            up = jnp.where(row == CX - 1, hi, up)
            dn = jnp.where(row == 0, lo, dn)
        return 0.5 * (up - dn)

    def dy(v):
        return 0.5 * (next_lane(v) - prev_lane(v))

    def dz(f):
        return 0.5 * (up_of(f, z) - dn_of(f, z))

    rho, vx, vy, vz, bx, by, bz, pr = [load(f, z) for f in range(8)]
    return feature_list(rho, (vx, vy, vz), (bx, by, bz), pr, lambda f, v: dx(f, v), dy, dz)


def feature_list(rho, v, b, pr, dx, dy, dz):
    jx = dy(b[2]) - dz(5)
    jy = dz(4) - dx(6, b[2])
    jz = dx(5, b[1]) - dy(b[0])
    div = dx(1, v[0]) + dy(v[1]) + dz(3)
    return [jx, jy, jz, div, rho, pr, b[0] * b[0] + b[1] * b[1] + b[2] * b[2],
            v[0] * v[0] + v[1] * v[1] + v[2] * v[2]]


def bias_rows(n):
    return jnp.where(iota((16, n), 0) < 3, 1.0, 0.0)


def plane_at(f, z):
    return pl.ds(pl.multiple_of((f * NZ + z) * CX, CX), CX)


def plane_loader(prim_ref):
    def load(f, z):
        return prim_ref[plane_at(f, z), :]

    return load


HALF = NZ // 2
WIDE = HALF * LANES
YG = NZ // 4
YPLANE = YG * CX
ENDS = 8
YROWS = 8 * 2 * CX


def pack_kernel(bricks_hbm, count_hbm, hbm_ref, lo_ref, hi_ref, maps_ref, prim_ref, bricks_ref, count_ref, sems):
    lane = iota((8, LANES), 1)
    spot = lane % ENDS

    def fetch(f):
        at = pl.ds(f * PLANE, PLANE)
        return pltpu.make_async_copy(hbm_ref.at[at, :], prim_ref.at[at, :], sems.at[f])

    for f in range(8):
        fetch(f).start()
    lists = [pltpu.make_async_copy(bricks_hbm, bricks_ref, sems.at[8]),
             pltpu.make_async_copy(count_hbm, count_ref, sems.at[9])]
    for copy in lists:
        copy.start()
    for f in range(8):
        fetch(f).wait()
        for h in range(2):
            los, his = [], []
            for o in range(2):
                lo = jnp.zeros((8, LANES), F32)
                hi = jnp.zeros((8, LANES), F32)
                for z in range(HALF):
                    v = prim_ref[pl.ds((f * NZ + h * HALF + z) * CX + o * 8, 8), :]
                    mine = lane // ENDS == z
                    lo = jnp.where(mine, take(v, spot), lo)
                    hi = jnp.where(mine, take(v, spot + (LANES - ENDS)), hi)
                los.append(lo)
                his.append(hi)
            at = pl.ds((f * 2 + h) * CX, CX)
            lo_ref[at, :] = jnp.concatenate(los, axis=0).astype(BF16)
            hi_ref[at, :] = jnp.concatenate(his, axis=0).astype(BF16)
    for copy in lists:
        copy.wait()
    source, half, back, ends = brick_rows(bricks_ref, count_ref)
    second = lane >= LANES // 2
    listed = [jnp.where(second, ends[1][side], ends[0][side]) for side in range(2)]
    for k, v in enumerate([source, half] + back + listed):
        maps_ref[pl.ds(k * 8, 8), :] = v
    for ref, flag in ((lo_ref, listed[0]), (hi_ref, listed[1])):
        ref[pl.ds(YROWS, 16), :] = jnp.concatenate([flag, flag], axis=0).astype(F32).astype(BF16)


def brick_rows(bricks_ref, count_ref):
    lane = iota((8, LANES), 1)
    slot, inner = lane // BRICK, lane % BRICK
    source = jnp.zeros((8, LANES), jnp.int32)
    half = jnp.zeros((8, LANES), jnp.int32)
    back = [jnp.full((8, LANES), -1, jnp.int32) for _ in range(2)]
    per_half = LANES // BRICK
    ends = [[0, 0], [0, 0]]
    for j in range(8):
        b = bricks_ref[0, j]
        bz, by = b // per_half, b % per_half
        source = jnp.where(slot == j, by * BRICK + inner, source)
        half = jnp.where(slot == j, bz, half)
        for h in range(2):
            use = jnp.logical_and(bz == h, j < count_ref[0, 0])
            want = jnp.where(use, by, -1)
            back[h] = jnp.where(slot == want, j * BRICK + inner, back[h])
            for side, end in enumerate((0, per_half - 1)):
                ends[h][side] = jnp.where(want == end, 1, ends[h][side])
    return source, half, back, ends


def read_maps(maps_ref):
    source, half, back0, back1, low, high = [maps_ref[pl.ds(k * 8, 8), :] for k in range(6)]
    return source, half, [back0, back1], [low, high]


def mhd_bulk(count, prim_ref, u_ref, fz_ref, sz_ref, ch_ref, out_ref, unroll, windows):
    rows = range(8)
    row, lane = iota((CX, LANES), 0), iota((CX, LANES), 1)

    def at(f, z):
        return pl.ds(pl.multiple_of((f * count + z) * CX, CX), CX)

    @pl.loop(0, count, unroll=unroll)
    def _(z):
        u, f, s = derive([prim_ref[at(k, z), :] for k in rows])

        def along(d, nxt, prv, last):
            un = {c: nxt(u[c]) for c in rows}
            fn = {c: None if f[d][c] is None else nxt(f[d][c]) for c in rows}
            fc = face(rows, u, un, f[d], fn, s[d], nxt(s[d]))
            out = {}
            for c in rows:
                inside = fc[c] if last is None else jnp.where(last, 0.0, fc[c])
                out[c] = inside - prv(inside)
            return out

        cx = along(0, next_row, prev_row, row == CX - 1)
        cy = along(1, next_lane, prev_lane, None if windows else lane == LANES - 1)
        for c in rows:
            ch_ref[at(c, z), :] = u[c] - TIME_STEP * (cx[c] + cy[c])
            u_ref[at(c, z), :] = u[c]
            if f[2][c] is not None:
                fz_ref[at(c, z), :] = f[2][c]
        sz_ref[at(0, z), :] = s[2]

    def zface(z, zn, turn):
        u = {c: u_ref[at(c, z), :] for c in rows}
        un = {c: turn(u_ref[at(c, zn), :]) for c in rows}
        f = {c: None if c == 6 else fz_ref[at(c, z), :] for c in rows}
        fn = {c: None if c == 6 else turn(fz_ref[at(c, zn), :]) for c in rows}
        return face(rows, u, un, f, fn, sz_ref[at(0, z), :], turn(sz_ref[at(0, zn), :]))

    def finish(z, before, here):
        for c in rows:
            out_ref[at(c, z), :] = ch_ref[at(c, z), :] - TIME_STEP * (here[c] - before[c])
        return tuple(here[c] for c in rows)

    if windows:
        last = zface(count - 1, 0, lambda v: pltpu.roll(v, LANES - 32, 1))
        before = tuple(pltpu.roll(last[c], 32, 1) for c in rows)
        for z in range(count):
            here = last if z == count - 1 else zface(z, z + 1, lambda v: v)
            before = finish(z, before, here)
    else:
        def step(z, before):
            return finish(z, before, zface(z, lax.rem(z + 1, count), lambda v: v))

        last = zface(count - 1, 0, lambda v: v)
        lax.fori_loop(0, count, step, tuple(last[c] for c in rows), unroll=unroll)


def x_ends(own_of, halo_of, lo, add):
    rows = range(8)
    uo, fo, so = derive([own_of(f) for f in rows])
    uh, fh, sh = derive([halo_of(f) for f in rows])
    if lo:
        fc = face(rows, uh, uo, fh[0], fo[0], sh[0], so[0])
    else:
        fc = face(rows, uo, uh, fo[0], fh[0], so[0], sh[0])
    for c in rows:
        step = TIME_STEP * fc[c]
        add(c, step if lo else -step)


def bulk_kernel(prim_ref, adv_ref, xlo_ref, xhi_ref, u_ref, fz_ref, sz_ref, ch_ref):
    mhd_bulk(NZ, prim_ref, u_ref, fz_ref, sz_ref, ch_ref, adv_ref, 4, False)
    for f in range(8):
        at = pl.ds(f * NZ, NZ)
        xlo_ref[at, :] = prim_ref[pl.ds(f * PLANE, NZ, stride=CX), :].astype(BF16)
        xhi_ref[at, :] = prim_ref[pl.ds(f * PLANE + CX - 1, NZ, stride=CX), :].astype(BF16)


def window_kernel(prim_ref, yfl_ref, yfr_ref, xlo_ref, xhi_ref, yp_ref, sxlo_ref, sxhi_ref,
                  left_ref, right_ref):
    lane = iota((8, LANES), 1)
    window, block = lane % 32, lane // 32
    own = jnp.where(window < 16, window - 6, LANES - 26 + window)
    own = jnp.minimum(jnp.maximum(own, 0), LANES - 1)
    spot = (block % 2) * 64 + jnp.where(window < 16, jnp.minimum(window + 2, 7), jnp.maximum(window - 26, 0))
    left_ref[...] = yfl_ref[pl.ds(0, YROWS), :].astype(F32)
    right_ref[...] = yfr_ref[pl.ds(0, YROWS), :].astype(F32)
    low, high, first = window < 6, window >= 26, block < 2
    for f in range(8):
        for o in range(2):
            here = [[ref[pl.ds((f * 2 + h) * CX + o * 8, 8), :] for h in range(2)]
                    for ref in (left_ref, right_ref)]
            for g in range(YG):
                v = None
                for b in range(4):
                    piece = take(prim_ref[pl.ds((f * NZ + b * YG + g) * CX + o * 8, 8), :], own)
                    v = piece if v is None else jnp.where(block == b, piece, v)
                index = spot + g * ENDS
                for side, where in ((0, low), (1, high)):
                    got = jnp.where(first, take(here[side][0], index), take(here[side][1], index))
                    v = jnp.where(where, got, v)
                yp_ref[pl.ds((f * YG + g) * CX + o * 8, 8), :] = v
    rows = 8 * NZ
    sxlo_ref[pl.ds(0, rows), :] = xlo_ref[...]
    sxhi_ref[pl.ds(0, rows), :] = xhi_ref[...]
    for f in range(0, 8, 2):
        for ref, start in ((sxlo_ref, 0), (sxhi_ref, CX - 1)):
            ref[pl.ds(rows + f * YG, 2 * YG), :] = yp_ref[
                pl.ds(f * YPLANE + start, 2 * YG, stride=CX), :].astype(BF16)


def ready_kernel(maps_ref, prim_ref, yp_ref, win_ref, whid_ref, wout_ref, bias_ref,
                 yadv_ref, x_ref, wb_ref, w1_ref, w2_ref, wo_ref,
                 u_ref, fz_ref, sz_ref, ch_ref):
    def split(b):
        hi = b.astype(BF16)
        r = b - hi.astype(F32)
        mid = r.astype(BF16)
        return [hi.astype(F32), mid.astype(F32), r - mid.astype(F32)]

    cols = (((0,), (0,)), ((), ()))
    rows = iota((16, KIN), 0)
    col = iota((16, KIN), 1)
    first = jnp.concatenate(
        [win_ref[...].astype(F32)] + split(bias_ref[0:1, :]) + [jnp.zeros((5, HID), F32)], axis=0
    ).astype(BF16)
    for s in range(8):
        spot = jnp.where(rows < 8, rows * 8 + s, jnp.where(rows < 11, 64 + rows - 8, -1))
        pick = jnp.where(col == spot, 1.0, 0.0).astype(BF16)
        wb_ref[pl.ds(s * HID, HID), :] = lax.dot_general(
            first, pick, cols, preferred_element_type=F32).astype(BF16)
    eye = jnp.where(iota((HID, HID), 0) == iota((HID, HID), 1), 0.5, 0.0).astype(BF16)
    eye16 = jnp.where(iota((16, 16), 0) == iota((16, 16), 1), 1.0, 0.0).astype(BF16)
    for layer, ref in ((0, w1_ref), (1, w2_ref)):
        turned = lax.dot_general(whid_ref[pl.ds(layer * HID, HID), :], eye, cols,
                                 preferred_element_type=F32)
        brow = jnp.concatenate(
            split(bias_ref[layer + 1 : layer + 2, :]) + [jnp.zeros((13, HID), F32)], axis=0
        ).astype(BF16)
        bcol = lax.dot_general(brow, eye16, cols, preferred_element_type=F32)
        ref[...] = jnp.concatenate([turned, bcol], axis=1).astype(BF16)
    wo_ref[...] = jnp.broadcast_to(0.5 * wout_ref[...].astype(F32), (16, HID)).astype(BF16)

    mhd_bulk(YG, yp_ref, u_ref, fz_ref, sz_ref, ch_ref, yadv_ref, 4, True)

    source, half, _, _ = read_maps(maps_ref)
    tail = bias_rows(LANES)
    load = plane_loader(prim_ref)

    def up_of(f, z):
        return load(f, lax.rem(z + 1, NZ))

    def dn_of(f, z):
        return load(f, lax.rem(z + NZ - 1, NZ))

    @pl.loop(0, HALF, unroll=4)
    def _(z):
        both = [features(load, zz, up_of, dn_of) for zz in (z, z + HALF)]
        at = pl.ds(pl.multiple_of(z * LANES, LANES), LANES)
        for o in range(2):
            parts = []
            for a, b in zip(*both):
                a, b = a[o * 8 : o * 8 + 8], b[o * 8 : o * 8 + 8]
                parts.append(jnp.where(half == 1, take(b, source), take(a, source)))
            x_ref[pl.ds(o * KIN, KIN), at] = jnp.concatenate(parts + [tail], axis=0).astype(BF16)


def edge_kernel(maps_ref, prim_ref, bulk_ref, yp_ref, ybulk_ref, x_ref,
                xlo_ref, xhi_ref, yfl_ref, yfr_ref, wb_ref, w1_ref, w2_ref, wo_ref,
                rest_ref, badv_ref, yb_ref, ky_ref, kape_ref, sxlo_ref, sxhi_ref,
                lo_ref, hi_ref, yadv_ref):
    lane8 = iota((8, LANES), 1)
    sub = iota((8, LANES), 0)
    lo_ref[...] = xlo_ref[...].astype(F32)
    hi_ref[...] = xhi_ref[...].astype(F32)
    yrows = 8 * NZ

    yadv_ref[...] = ybulk_ref[...]
    badv_ref[...] = bulk_ref[pl.ds(4 * PLANE, 3 * PLANE), :]
    for lo in (True, False):
        start = 0 if lo else CX - 1
        ref = lo_ref if lo else hi_ref

        def add_window(c, step):
            at = pl.ds(c * YPLANE + start, YG, stride=CX)
            yadv_ref[at, :] = yadv_ref[at, :] + step

        x_ends(lambda f: yp_ref[pl.ds(f * YPLANE + start, YG, stride=CX), :],
               lambda f: ref[pl.ds(yrows + f * YG, YG), :], lo, add_window)
    yb_ref[...] = yadv_ref[pl.ds(4 * YPLANE, 3 * YPLANE), :]
    on_edge = jnp.logical_or(lane8 == 0, lane8 == LANES - 1)
    for c in (0, 1, 2, 3, 7):
        k = c if c < 4 else 4
        for z in range(NZ):
            b, g = z // YG, z % YG
            index = b * 32 + jnp.where(lane8 == LANES - 1, 25, 6)
            for o in range(2):
                at = pl.ds(c * PLANE + z * CX + o * 8, 8)
                edge = take(yadv_ref[pl.ds(c * YPLANE + g * CX + o * 8, 8), :], index)
                to = pl.ds(k * PLANE + z * CX + o * 8, 8)
                rest_ref[to, :] = jnp.where(on_edge, edge, bulk_ref[at, :])
    at_end = jnp.logical_or(lane8 == 0, lane8 == LANES - 1)
    for zs in range(0, NZ, 8):
        for lo in (True, False):
            start = zs * CX + (0 if lo else CX - 1)
            ref = lo_ref if lo else hi_ref

            def add_block(c, step):
                if 4 <= c < 7:
                    at = pl.ds((c - 4) * PLANE + start, 8, stride=CX)
                    badv_ref[at, :] = badv_ref[at, :] + step
                else:
                    at = pl.ds(min(c, 4) * PLANE + start, 8, stride=CX)
                    rest_ref[at, :] = rest_ref[at, :] + jnp.where(at_end, 0.0, step)

            x_ends(lambda f: prim_ref[pl.ds(f * PLANE + start, 8, stride=CX), :],
                   lambda f: ref[pl.ds(f * NZ + zs, 8), :], lo, add_block)

    source, half, back, ends = read_maps(maps_ref)
    tail = bias_rows(LANES)
    parts = []
    for lo in (True, False):
        start = 0 if lo else CX - 1
        ref = lo_ref if lo else hi_ref

        def row_of(f, x=start):
            return prim_ref[pl.ds(f * PLANE + x, NZ, stride=CX), :]

        def dx(f, v):
            beyond = ref[pl.ds(f * NZ, NZ), :]
            within = row_of(f, start + (1 if lo else -1))
            return 0.5 * (within - beyond) if lo else 0.5 * (beyond - within)

        def dy(v):
            return 0.5 * (next_lane(v) - prev_lane(v))

        p = [row_of(f) for f in range(8)]

        def dz(f):
            return 0.5 * (next_row(p[f]) - prev_row(p[f]))

        fs = feature_list(p[0], p[1:4], p[4:7], p[7], dx, dy, dz)
        for q in range(2):
            packed = [jnp.where(half == 1, take(v[HALF + q * 8 : HALF + q * 8 + 8], source),
                                take(v[q * 8 : q * 8 + 8], source)) for v in fs]
            parts.append(jnp.concatenate(packed + [tail], axis=0))
    xend = jnp.concatenate(parts, axis=1).astype(BF16)

    def yload(f, z):
        return yp_ref[pl.ds((f * YG + z) * CX, CX), :]

    def yup(f, z):
        return yload(f, z + 1) if z + 1 < YG else pltpu.roll(yload(f, 0), LANES - 32, 1)

    def ydn(f, z):
        return yload(f, z - 1) if z > 0 else pltpu.roll(yload(f, YG - 1), 32, 1)

    def patch_x(f, z):
        at = pl.ds(yrows + f * YG + z, 1)
        return lo_ref[at, :], hi_ref[at, :]

    window, block = lane8 % 32, lane8 // 32
    inner = window % 8
    from_window = block * 32 + jnp.where(inner < 4, inner + 3, inner + 21)
    ycells = {(o, q): [jnp.zeros((8, LANES), F32)] * 8 for o in range(2) for q in range(2)}
    for g in range(YG):
        fs = features(yload, g, yup, ydn, patch_x)
        mine = window // 8 == g % 4
        for o in range(2):
            ycells[o, g // 4] = [jnp.where(mine, take(v[o * 8 : o * 8 + 8], from_window), a)
                                 for v, a in zip(fs, ycells[o, g // 4])]
    yend = jnp.concatenate([jnp.concatenate(ycells[o, q] + [tail], axis=0)
                            for o in range(2) for q in range(2)], axis=1).astype(BF16)

    us = []
    for o, s in ((0, 1), (0, 2), (1, 5), (1, 6)):
        us.append(jnp.dot(wb_ref[pl.ds(s * HID, HID), :], x_ref[pl.ds(o * KIN, KIN), :],
                          preferred_element_type=F32))
    for cells in (xend, yend):
        ue = [jnp.dot(wb_ref[pl.ds(s * HID, HID), :], cells, preferred_element_type=F32) for s in range(8)]
        for part in range(2):
            us.append(jnp.concatenate(ue[part * 4 : part * 4 + 4], axis=1))
    rates = closure_rates(us, w1_ref[...], w2_ref[...], wo_ref[...])

    def by_row(first, k):
        acc = jnp.zeros((8, LANES), F32)
        for s in range(8):
            at = (s % 4) * 512 + k * LANES
            acc = jnp.where(sub == s, rates[first + s // 4][:8, at : at + LANES], acc)
        return acc

    low = jnp.full((NZ, LANES), RATE_LOW, BF16)
    for e in range(6):
        packed = []
        for q in range(2):
            if e in (0, 5):
                acc = by_row(4, (0 if e == 0 else 2) + q)
            else:
                acc = jnp.zeros((8, LANES), F32)
                for k in range(8):
                    z = q * 8 + k
                    acc = jnp.where(sub == k, rates[e - 1][:8, z * LANES : (z + 1) * LANES], acc)
            packed.append(acc)
            kape_ref[pl.ds(e * HALF + q * 8, 8), :] = acc
        full = []
        for h in range(2):
            listed = back[h] >= 0
            for q in range(2):
                full.append(jnp.where(listed, take(packed[q], jnp.maximum(back[h], 0)), RATE_LOW))
        full = jnp.concatenate(full, axis=0).astype(BF16)
        if e < 3:
            sxlo_ref[pl.ds((12 + e) * NZ, NZ), :] = full
        else:
            sxhi_ref[pl.ds((12 + e - 2) * NZ, NZ), :] = full
    sxlo_ref[pl.ds(15 * NZ, NZ), :] = low
    sxhi_ref[pl.ds(12 * NZ, NZ), :] = low

    mine = jnp.where(window < 16, ends[0], ends[1])
    left = yfl_ref[pl.ds(YROWS, 16), :].astype(F32)[:8]
    right = yfr_ref[pl.ds(YROWS, 16), :].astype(F32)[:8]
    listed = jnp.where(window < 6, left, jnp.where(window >= 26, right, mine.astype(F32))) > 0.5
    known = jnp.where(window < 16, window - 3, window - 21)
    known = jnp.minimum(jnp.maximum(known, 0), 7)
    for o in range(2):
        for q in range(2):
            got = by_row(6, o * 2 + q)
            for g in range(4):
                k = take(got, block * 32 + g * 8 + known)
                ky_ref[pl.ds((q * 4 + g) * CX + o * 8, 8), :] = jnp.where(listed, k, RATE_LOW)

    for f in range(3):
        for r in range(4):
            at = pl.ds((f * 4 + r) * NZ, NZ)
            sxlo_ref[at, :] = badv_ref[pl.ds(f * PLANE + r, NZ, stride=CX), :].astype(BF16)
            sxhi_ref[at, :] = badv_ref[pl.ds(f * PLANE + CX - 4 + r, NZ, stride=CX), :].astype(BF16)
    for f in range(4):
        ref, base = (yb_ref, f * YPLANE) if f < 3 else (ky_ref, 0)
        for dst, start in ((sxlo_ref, 0), (sxhi_ref, CX - 4)):
            for r in range(0, 4, 2):
                pair = [ref[pl.ds(base + start + r + k, YG, stride=CX), :] for k in range(2)]
                dst[pl.ds(16 * NZ + (f * 4 + r) * YG, 2 * YG), :] = jnp.concatenate(pair, axis=0).astype(BF16)


def inner_rates(o, x_ref, wb_ref, w1_ref, w2_ref, wo_ref, kp_ref):
    sub = iota((8, LANES), 0)
    which = range(3, 8) if o == 0 else range(5)
    us = [jnp.dot(wb_ref[pl.ds(s * HID, HID), :], x_ref[pl.ds(o * KIN, KIN), :],
                  preferred_element_type=F32) for s in which]
    rates = closure_rates(us, w1_ref[...], w2_ref[...], wo_ref[...])
    for z in range(HALF):
        acc = jnp.zeros((8, LANES), F32)
        for s, r in zip(which, rates):
            acc = jnp.where(sub == s, r[:8, z * LANES : (z + 1) * LANES], acc)
        kp_ref[pl.ds(z * 8, 8), :] = acc


def inner_kernel(maps_ref, x_ref, kape_ref, wb_ref, w1_ref, w2_ref, wo_ref,
                 kap_ref, kp_ref):
    rows = HALF * 8
    for o in range(2):
        inner_rates(o, x_ref, wb_ref, w1_ref, w2_ref, wo_ref, kp_ref.at[pl.ds(o * rows, rows), :])
    _, _, back, _ = read_maps(maps_ref)
    for e in range(6):
        x = e if e < 3 else rows + 2 + e
        kp_ref[pl.ds(x, HALF, stride=8), :] = kape_ref[pl.ds(e * HALF, HALF), :]
    for h in range(2):
        listed = back[h] >= 0
        index = jnp.maximum(back[h], 0)
        for z in range(HALF):
            for o in range(2):
                k = kp_ref[pl.ds(o * rows + z * 8, 8), :]
                kap_ref[pl.ds((h * HALF + z) * CX + o * 8, 8), :] = jnp.where(
                    listed, take(k, index), RATE_LOW)


DEEP = CX + 8


def diffuse_kernel(rest_ref, b_ref, kap_ref, yb_ref, kapy_ref, xlo_ref, xhi_ref, out_ref,
                   m0, m1, km, y0, y1, ky, xl, xh, done, sems):
    copies = [pltpu.make_async_copy(rest_ref.at[pl.ds(0, 4 * PLANE), :],
                                    out_ref.at[pl.ds(0, 4 * PLANE), :], sems.at[0]),
              pltpu.make_async_copy(rest_ref.at[pl.ds(4 * PLANE, PLANE), :],
                                    out_ref.at[pl.ds(7 * PLANE, PLANE), :], sems.at[1])]
    for copy in copies:
        copy.start()
    lane = iota((8, LANES), 1)
    window, block = lane % 32, lane // 32

    def build(field, own_ref, own_at, yown_ref, yown_at, main, edge):
        for z in range(NZ):
            main[pl.ds(z * DEEP, CX), :] = own_ref[pl.ds(own_at + z * CX, CX), :]
        for g in range(YG):
            edge[pl.ds(g * DEEP, CX), :] = yown_ref[pl.ds(yown_at + g * CX, CX), :]
        for r in range(4):
            for src, row in ((xh, CX + r), (xl, CX + 4 + r)):
                at = pl.ds((field * 4 + r) * NZ, NZ)
                main[pl.ds(row, NZ, stride=DEEP), :] = src[at, :]
                at = pl.ds(16 * NZ + (field * 4 + r) * YG, YG)
                edge[pl.ds(row, YG, stride=DEEP), :] = src[at, :]

    xl[...] = xlo_ref[...].astype(F32)
    xh[...] = xhi_ref[...].astype(F32)
    build(3, kap_ref, 0, kapy_ref, 0, km, ky)
    own = jnp.where(window < 16, window - 6, LANES - 26 + window)
    own = jnp.minimum(jnp.maximum(own, 0), LANES - 1)
    made = jnp.logical_or(window < 7, window >= 25)
    for g in range(YG):
        for o in range(3):
            v = None
            for b in range(4):
                piece = take(km[pl.ds((b * YG + g) * DEEP + o * 8, 8), :], own)
                v = piece if v is None else jnp.where(block == b, piece, v)
            at = pl.ds(g * DEEP + o * 8, 8)
            ky[at, :] = jnp.where(made, ky[at, :], v)

    def relax(c, up, dn, k):
        total = next_row(c) + prev_row(c) + next_lane(c) + prev_lane(c) + (up + dn)
        return c + k * (total - 6.0 * c)

    def at(z):
        return pl.ds(z * DEEP, DEEP)

    on_edge = jnp.logical_or(lane < 5, lane >= LANES - 5)
    for comp in range(3):
        build(comp, b_ref, comp * PLANE, yb_ref, comp * YPLANE, m0, y0)
        mains, edges = (m0, m1), (y0, y1)
        for step in range(SUB):
            a, b = mains[step % 2], mains[1 - step % 2]
            ea, eb = edges[step % 2], edges[1 - step % 2]
            for g in range(YG):
                up = ea[at(g + 1), :] if g + 1 < YG else pltpu.roll(ea[at(0), :], LANES - 32, 1)
                dn = ea[at(g - 1), :] if g > 0 else pltpu.roll(ea[at(YG - 1), :], 32, 1)
                eb[at(g), :] = relax(ea[at(g), :], up, dn, ky[at(g), :])
            dn, c = a[at(NZ - 1), :], a[at(0), :]
            for z in range(NZ):
                up = a[at((z + 1) % NZ), :]
                new = relax(c, up, dn, km[at(z), :])
                dn, c = c, up
                if step < SUB - 1:
                    b[at(z), :] = new
                    continue
                k, g = z // YG, z % YG
                index = k * 32 + jnp.where(lane < 5, 6 + lane, lane - (LANES - 26))
                index = jnp.minimum(jnp.maximum(index, 0), LANES - 1)
                for o in range(2):
                    e = take(eb[pl.ds(g * DEEP + o * 8, 8), :], index)
                    done[pl.ds(comp * PLANE + z * CX + o * 8, 8), :] = jnp.where(on_edge, e, new[o * 8 : o * 8 + 8])
        copy = pltpu.make_async_copy(done.at[pl.ds(comp * PLANE, PLANE), :],
                                     out_ref.at[pl.ds((4 + comp) * PLANE, PLANE), :], sems.at[2 + comp])
        copy.start()
        copies.append(copy)
    for copy in copies:
        copy.wait()


def struct(shape, dtype=F32):
    return jax.ShapeDtypeStruct(shape, dtype)


def params(mib):
    return pltpu.CompilerParams(vmem_limit_bytes=mib << 20)


def cost(us):
    return pl.CostEstimate(flops=us * 500_000_000, bytes_accessed=us << 20, transcendentals=0)


VSPEC = pl.BlockSpec(memory_space=pltpu.VMEM)


def step_up(axis):
    n = lax.axis_size(axis)
    return [(i, (i + 1) % n) for i in range(n)]


def step_down(axis):
    n = lax.axis_size(axis)
    return [((i + 1) % n, i) for i in range(n)]


def shards(primitive, current_sheet_bricks, brick_count, w_in, w_hid, w_out, b_hid):
    shape = primitive.shape
    prim = primitive.reshape(8 * PLANE, LANES)
    bricks = current_sheet_bricks.reshape(1, -1)
    count = brick_count.reshape(1, 1)

    blo, bhi, maps = pl.pallas_call(
        pack_kernel,
        in_specs=[pl.BlockSpec(memory_space=pltpu.HBM)] * 3,
        out_shape=[struct((YROWS + 16, LANES), BF16)] * 2 + [struct((48, LANES), jnp.int32)],
        scratch_shapes=[pltpu.VMEM((8 * PLANE, LANES), F32), pltpu.SMEM((1, 8), jnp.int32),
                        pltpu.SMEM((1, 1), jnp.int32), pltpu.SemaphoreType.DMA((10,))],
        compiler_params=params(60),
        name="pack",
    )(bricks, count, prim)
    yfl = lax.ppermute(bhi, "row", step_up("row"))
    yfr = lax.ppermute(blo, "row", step_down("row"))

    def mhd_scratch(planes):
        many = pltpu.VMEM((8 * planes * CX, LANES), F32)
        return [many, many, pltpu.VMEM((planes * CX, LANES), F32), many]

    adv, xmlo, xmhi = pl.pallas_call(
        bulk_kernel,
        out_shape=[struct((8 * PLANE, LANES))] + [struct((8 * NZ, LANES), BF16)] * 2,
        scratch_shapes=mhd_scratch(NZ),
        compiler_params=params(20),
        cost_estimate=cost(4),
        name="bulk",
    )(prim)

    sxrows = 8 * NZ + 8 * YG
    yp, slo, shi = pl.pallas_call(
        window_kernel,
        out_shape=[struct((8 * YPLANE, LANES))] + [struct((sxrows, LANES), BF16)] * 2,
        scratch_shapes=[pltpu.VMEM((YROWS, LANES), F32)] * 2,
        compiler_params=params(12),
        cost_estimate=cost(1),
        name="windows",
    )(prim, yfl, yfr, xmlo, xmhi)
    xlo = lax.ppermute(shi, "col", step_up("col"))
    xhi = lax.ppermute(slo, "col", step_down("col"))

    weights = [struct((8 * HID, KIN), BF16), struct((HID, KHID), BF16), struct((HID, KHID), BF16),
               struct((16, HID), BF16)]
    yadv, xcells, *closure = pl.pallas_call(
        ready_kernel,
        in_specs=[VSPEC] * 7,
        out_shape=[struct((8 * YPLANE, LANES)), struct((2 * KIN, WIDE), BF16)] + weights,
        scratch_shapes=mhd_scratch(YG),
        compiler_params=params(16),
        cost_estimate=cost(4),
        name="ready",
    )(maps, prim, yp, w_in, w_hid.reshape(2 * HID, HID), w_out.reshape(1, HID), b_hid)

    xrows = 16 * NZ + 16 * YG
    rest, badv, yb, ky, kape, sxlo, sxhi = pl.pallas_call(
        edge_kernel,
        in_specs=[VSPEC] * 14,
        out_shape=[struct((5 * PLANE, LANES)), struct((3 * PLANE, LANES)), struct((3 * YPLANE, LANES)),
                   struct((YPLANE, LANES)), struct((6 * HALF, LANES)),
                   struct((xrows, LANES), BF16), struct((xrows, LANES), BF16)],
        scratch_shapes=[pltpu.VMEM((sxrows, LANES), F32)] * 2 + [pltpu.VMEM((8 * YPLANE, LANES), F32)],
        compiler_params=params(32),
        cost_estimate=cost(8),
        name="edges",
    )(maps, prim, adv, yp, yadv, xcells, xlo, xhi, yfl, yfr, *closure)

    gothi = lax.ppermute(sxlo, "col", step_down("col"))
    gotlo = lax.ppermute(sxhi, "col", step_up("col"))

    kap = pl.pallas_call(
        inner_kernel,
        in_specs=[VSPEC] * 7,
        out_shape=struct((PLANE, LANES)),
        scratch_shapes=[pltpu.VMEM((HALF * CX, LANES), F32)],
        compiler_params=params(24),
        cost_estimate=cost(6),
        name="inner",
    )(maps, xcells, kape, *closure)

    out = pl.pallas_call(
        diffuse_kernel,
        out_specs=pl.BlockSpec(memory_space=pltpu.HBM),
        out_shape=struct((8 * PLANE, LANES)),
        scratch_shapes=[pltpu.VMEM((NZ * DEEP, LANES), F32)] * 3
        + [pltpu.VMEM((YG * DEEP, LANES), F32)] * 3
        + [pltpu.VMEM((xrows, LANES), F32)] * 2
        + [pltpu.VMEM((3 * PLANE, LANES), F32), pltpu.SemaphoreType.DMA((5,))],
        compiler_params=params(16),
        name="diffuse",
    )(rest, badv, kap, yb, ky, gotlo, gothi)
    return out.reshape(shape)


def solution(mesh):
    return jax.shard_map(
        shards,
        mesh=mesh,
        in_specs=(
            P(None, None, "col", "row"),
            P("row", "col", None),
            P("row", "col"),
            P(),
            P(),
            P(),
            P(),
        ),
        out_specs=P(None, None, "col", "row"),
        check_vma=False,
    )
```

```python
import jax
import jax.numpy as jnp
from jax import lax
from jax.experimental import pallas as pl
from jax.experimental.pallas import tpu as pltpu
from jax.sharding import PartitionSpec as P

BRICK = 16
SUB = 4
ADIABATIC = 5.0 / 3.0
TIME_STEP = 0.02
RATE_LOW = 0.02
RATE_SPAN = 0.14
GELU_A = 0.7978845608
GELU_B = 0.7978845608 * 0.044715
F32 = jnp.float32
BF16 = jnp.bfloat16
LANES = 128
NZ = 32
CX = 16
HID = 128
PLANE = NZ * CX
KIN = 80
KHID = HID + 16


def iota(shape, dim):
    return lax.broadcasted_iota(jnp.int32, shape, dim)


def take(values, index):
    return jnp.take_along_axis(values, index, axis=1, mode="promise_in_bounds")


def next_row(v):
    return pltpu.roll(v, v.shape[0] - 1, 0)


def prev_row(v):
    return pltpu.roll(v, 1, 0)


def next_lane(v):
    return pltpu.roll(v, v.shape[1] - 1, 1)


def prev_lane(v):
    return pltpu.roll(v, 1, 1)


def derive(p):
    rho, pr = p[0], p[7]
    v, b = p[1:4], p[4:7]
    m = [rho * c for c in v]
    b2 = b[0] * b[0] + b[1] * b[1] + b[2] * b[2]
    v2 = v[0] * v[0] + v[1] * v[1] + v[2] * v[2]
    vb = v[0] * b[0] + v[1] * b[1] + v[2] * b[2]
    pt = pr + 0.5 * b2
    en = 1.5 * pr + 0.5 * (rho * v2 + b2)
    wave = ADIABATIC * pr + b2
    fast = wave * lax.rsqrt(wave * rho)
    ep = en + pt
    tens = {(i, j): m[i] * v[j] - b[i] * b[j] for i in range(3) for j in range(i, 3)}
    elec = {(i, j): v[i] * b[j] - b[i] * v[j] for i in range(3) for j in range(i + 1, 3)}
    fluxes = []
    for d in range(3):
        rows = [m[d]]
        for c in range(3):
            t = tens[(min(c, d), max(c, d))]
            rows.append(t + pt if c == d else t)
        for c in range(3):
            rows.append(None if c == d else (elec[(d, c)] if d < c else -elec[(c, d)]))
        rows.append(ep * v[d] - b[d] * vb)
        fluxes.append(rows)
    speeds = [jnp.abs(c) + fast for c in v]
    return [rho] + m + list(b) + [en], fluxes, speeds


def face(rows, u, un, f, fn, s, sn):
    a = 0.5 * jnp.maximum(s, sn)
    out = {}
    for c in rows:
        diss = a * (un[c] - u[c])
        out[c] = -diss if f[c] is None else 0.5 * (f[c] + fn[c]) - diss
    return out


def gelu_twice(u):
    u = u.astype(BF16)
    t = jnp.tanh(u * (jnp.asarray(GELU_A, BF16) + jnp.asarray(GELU_B, BF16) * (u * u)))
    return u + u * t


def closure_rates(first, w1, w2, wo):
    us = first
    for w in (w1, w2):
        hs = [jnp.concatenate([gelu_twice(u), bias_rows(u.shape[1]).astype(BF16)], axis=0) for u in us]
        us = [jnp.dot(w, h, preferred_element_type=F32) for h in hs]
    hs = [gelu_twice(u) for u in us]
    scores = [jnp.dot(wo, h, preferred_element_type=F32) for h in hs]
    return [(RATE_LOW + 0.5 * RATE_SPAN) + (0.5 * RATE_SPAN) * jnp.tanh(0.5 * s) for s in scores]


def features(load, z, up_of, dn_of, patch_x=None):
    row = iota((CX, LANES), 0)

    def dx(f, v):
        up, dn = next_row(v), prev_row(v)
        if patch_x is not None:
            lo, hi = patch_x(f, z)
            up = jnp.where(row == CX - 1, hi, up)
            dn = jnp.where(row == 0, lo, dn)
        return 0.5 * (up - dn)

    def dy(v):
        return 0.5 * (next_lane(v) - prev_lane(v))

    def dz(f):
        return 0.5 * (up_of(f, z) - dn_of(f, z))

    rho, vx, vy, vz, bx, by, bz, pr = [load(f, z) for f in range(8)]
    return feature_list(rho, (vx, vy, vz), (bx, by, bz), pr, lambda f, v: dx(f, v), dy, dz)


def feature_list(rho, v, b, pr, dx, dy, dz):
    jx = dy(b[2]) - dz(5)
    jy = dz(4) - dx(6, b[2])
    jz = dx(5, b[1]) - dy(b[0])
    div = dx(1, v[0]) + dy(v[1]) + dz(3)
    return [jx, jy, jz, div, rho, pr, b[0] * b[0] + b[1] * b[1] + b[2] * b[2],
            v[0] * v[0] + v[1] * v[1] + v[2] * v[2]]


def bias_rows(n):
    return jnp.where(iota((16, n), 0) < 3, 1.0, 0.0)


def plane_at(f, z):
    return pl.ds(pl.multiple_of((f * NZ + z) * CX, CX), CX)


def plane_loader(prim_ref):
    def load(f, z):
        return prim_ref[plane_at(f, z), :]

    return load


HALF = NZ // 2
WIDE = HALF * LANES
YG = NZ // 4
YPLANE = YG * CX
ENDS = 8
YROWS = 8 * 2 * CX


def pack_kernel(bricks_hbm, count_hbm, hbm_ref, lo_ref, hi_ref, maps_ref, prim_ref, bricks_ref, count_ref, sems):
    lane = iota((8, LANES), 1)
    spot = lane % ENDS

    def fetch(f):
        at = pl.ds(f * PLANE, PLANE)
        return pltpu.make_async_copy(hbm_ref.at[at, :], prim_ref.at[at, :], sems.at[f])

    for f in range(8):
        fetch(f).start()
    lists = [pltpu.make_async_copy(bricks_hbm, bricks_ref, sems.at[8]),
             pltpu.make_async_copy(count_hbm, count_ref, sems.at[9])]
    for copy in lists:
        copy.start()
    for f in range(8):
        fetch(f).wait()
        for h in range(2):
            los, his = [], []
            for o in range(2):
                lo = jnp.zeros((8, LANES), F32)
                hi = jnp.zeros((8, LANES), F32)
                for spot_z in range(HALF):
                    z = spot_z // 4 * YG + h * 4 + spot_z % 4
                    v = prim_ref[pl.ds((f * NZ + z) * CX + o * 8, 8), :]
                    mine = lane // ENDS == spot_z
                    lo = jnp.where(mine, take(v, spot), lo)
                    hi = jnp.where(mine, take(v, spot + (LANES - ENDS)), hi)
                los.append(lo)
                his.append(hi)
            at = pl.ds((f * 2 + h) * CX, CX)
            lo_ref[at, :] = jnp.concatenate(los, axis=0).astype(BF16)
            hi_ref[at, :] = jnp.concatenate(his, axis=0).astype(BF16)
    for copy in lists:
        copy.wait()
    source, half, back, ends = brick_rows(bricks_ref, count_ref)
    second = lane >= LANES // 2
    listed = [jnp.where(second, ends[1][side], ends[0][side]) for side in range(2)]
    for k, v in enumerate([source, half] + back + listed):
        maps_ref[pl.ds(k * 8, 8), :] = v
    for ref, flag in ((lo_ref, listed[0]), (hi_ref, listed[1])):
        ref[pl.ds(YROWS, 16), :] = jnp.concatenate([flag, flag], axis=0).astype(F32).astype(BF16)


def brick_rows(bricks_ref, count_ref):
    lane = iota((8, LANES), 1)
    slot, inner = lane // BRICK, lane % BRICK
    source = jnp.zeros((8, LANES), jnp.int32)
    half = jnp.zeros((8, LANES), jnp.int32)
    back = [jnp.full((8, LANES), -1, jnp.int32) for _ in range(2)]
    per_half = LANES // BRICK
    ends = [[0, 0], [0, 0]]
    for j in range(8):
        b = bricks_ref[0, j]
        bz, by = b // per_half, b % per_half
        source = jnp.where(slot == j, by * BRICK + inner, source)
        half = jnp.where(slot == j, bz, half)
        for h in range(2):
            use = jnp.logical_and(bz == h, j < count_ref[0, 0])
            want = jnp.where(use, by, -1)
            back[h] = jnp.where(slot == want, j * BRICK + inner, back[h])
            for side, end in enumerate((0, per_half - 1)):
                ends[h][side] = jnp.where(want == end, 1, ends[h][side])
    return source, half, back, ends


def read_maps(maps_ref):
    source, half, back0, back1, low, high = [maps_ref[pl.ds(k * 8, 8), :] for k in range(6)]
    return source, half, [back0, back1], [low, high]


def mhd_bulk(count, prim_ref, u_ref, fz_ref, sz_ref, ch_ref, out_ref, unroll, windows):
    rows = range(8)
    row, lane = iota((CX, LANES), 0), iota((CX, LANES), 1)

    def at(f, z):
        return pl.ds(pl.multiple_of((f * count + z) * CX, CX), CX)

    @pl.loop(0, count, unroll=unroll)
    def _(z):
        u, f, s = derive([prim_ref[at(k, z), :] for k in rows])

        def along(d, nxt, prv, last):
            un = {c: nxt(u[c]) for c in rows}
            fn = {c: None if f[d][c] is None else nxt(f[d][c]) for c in rows}
            fc = face(rows, u, un, f[d], fn, s[d], nxt(s[d]))
            out = {}
            for c in rows:
                inside = fc[c] if last is None else jnp.where(last, 0.0, fc[c])
                out[c] = inside - prv(inside)
            return out

        cx = along(0, next_row, prev_row, row == CX - 1)
        cy = along(1, next_lane, prev_lane, None if windows else lane == LANES - 1)
        for c in rows:
            ch_ref[at(c, z), :] = u[c] - TIME_STEP * (cx[c] + cy[c])
            u_ref[at(c, z), :] = u[c]
            if f[2][c] is not None:
                fz_ref[at(c, z), :] = f[2][c]
        sz_ref[at(0, z), :] = s[2]

    def zface(z, zn, turn):
        u = {c: u_ref[at(c, z), :] for c in rows}
        un = {c: turn(u_ref[at(c, zn), :]) for c in rows}
        f = {c: None if c == 6 else fz_ref[at(c, z), :] for c in rows}
        fn = {c: None if c == 6 else turn(fz_ref[at(c, zn), :]) for c in rows}
        return face(rows, u, un, f, fn, sz_ref[at(0, z), :], turn(sz_ref[at(0, zn), :]))

    def finish(z, before, here):
        for c in rows:
            out_ref[at(c, z), :] = ch_ref[at(c, z), :] - TIME_STEP * (here[c] - before[c])
        return tuple(here[c] for c in rows)

    if windows:
        last = zface(count - 1, 0, lambda v: pltpu.roll(v, LANES - 32, 1))
        before = tuple(pltpu.roll(last[c], 32, 1) for c in rows)
        for z in range(count):
            here = last if z == count - 1 else zface(z, z + 1, lambda v: v)
            before = finish(z, before, here)
    else:
        def step(z, before):
            return finish(z, before, zface(z, lax.rem(z + 1, count), lambda v: v))

        last = zface(count - 1, 0, lambda v: v)
        lax.fori_loop(0, count, step, tuple(last[c] for c in rows), unroll=unroll)


def x_ends(own_of, halo_of, lo, add):
    rows = range(8)
    uo, fo, so = derive([own_of(f) for f in rows])
    uh, fh, sh = derive([halo_of(f) for f in rows])
    if lo:
        fc = face(rows, uh, uo, fh[0], fo[0], sh[0], so[0])
    else:
        fc = face(rows, uo, uh, fo[0], fh[0], so[0], sh[0])
    for c in rows:
        step = TIME_STEP * fc[c]
        add(c, step if lo else -step)


def bulk_kernel(prim_ref, adv_ref, xlo_ref, xhi_ref, u_ref, fz_ref, sz_ref, ch_ref):
    mhd_bulk(NZ, prim_ref, u_ref, fz_ref, sz_ref, ch_ref, adv_ref, 4, False)
    for f in range(8):
        at = pl.ds(f * NZ, NZ)
        xlo_ref[at, :] = prim_ref[pl.ds(f * PLANE, NZ, stride=CX), :].astype(BF16)
        xhi_ref[at, :] = prim_ref[pl.ds(f * PLANE + CX - 1, NZ, stride=CX), :].astype(BF16)


def prepare_weights(win_ref, whid_ref, wout_ref, bias_ref, wb_ref, w1_ref, w2_ref, wo_ref):
    def split(b):
        hi = b.astype(BF16)
        r = b - hi.astype(F32)
        mid = r.astype(BF16)
        return [hi.astype(F32), mid.astype(F32), r - mid.astype(F32)]

    cols = (((0,), (0,)), ((), ()))
    rows = iota((16, KIN), 0)
    col = iota((16, KIN), 1)
    first = jnp.concatenate(
        [win_ref[...].astype(F32)] + split(bias_ref[0:1, :]) + [jnp.zeros((5, HID), F32)], axis=0
    ).astype(BF16)
    for s in range(8):
        spot = jnp.where(rows < 8, rows * 8 + s, jnp.where(rows < 11, 64 + rows - 8, -1))
        pick = jnp.where(col == spot, 1.0, 0.0).astype(BF16)
        wb_ref[pl.ds(s * HID, HID), :] = lax.dot_general(
            first, pick, cols, preferred_element_type=F32).astype(BF16)
    eye = jnp.where(iota((HID, HID), 0) == iota((HID, HID), 1), 0.5, 0.0).astype(BF16)
    eye16 = jnp.where(iota((16, 16), 0) == iota((16, 16), 1), 1.0, 0.0).astype(BF16)
    for layer, ref in ((0, w1_ref), (1, w2_ref)):
        turned = lax.dot_general(whid_ref[pl.ds(layer * HID, HID), :], eye, cols,
                                 preferred_element_type=F32)
        brow = jnp.concatenate(
            split(bias_ref[layer + 1 : layer + 2, :]) + [jnp.zeros((13, HID), F32)], axis=0
        ).astype(BF16)
        bcol = lax.dot_general(brow, eye16, cols, preferred_element_type=F32)
        ref[...] = jnp.concatenate([turned, bcol], axis=1).astype(BF16)
    wo_ref[...] = jnp.broadcast_to(0.5 * wout_ref[...].astype(F32), (16, HID)).astype(BF16)


def window_kernel(prim_ref, yfl_ref, yfr_ref, xlo_ref, xhi_ref, win_ref, whid_ref, wout_ref, bias_ref,
                  yp_ref, sxlo_ref, sxhi_ref, wb_ref, w1_ref, w2_ref, wo_ref, left_ref, right_ref):
    prepare_weights(win_ref, whid_ref, wout_ref, bias_ref, wb_ref, w1_ref, w2_ref, wo_ref)
    lane = iota((8, LANES), 1)
    window, block = lane % 32, lane // 32
    own = jnp.where(window < 16, window - 6, LANES - 26 + window)
    own = jnp.minimum(jnp.maximum(own, 0), LANES - 1)
    spot = block * 32 + jnp.where(window < 16, jnp.minimum(window + 2, 7), jnp.maximum(window - 26, 0))
    left_ref[...] = yfl_ref[pl.ds(0, YROWS), :].astype(F32)
    right_ref[...] = yfr_ref[pl.ds(0, YROWS), :].astype(F32)
    low, high = window < 6, window >= 26
    for f in range(8):
        for o in range(2):
            here = [[ref[pl.ds((f * 2 + h) * CX + o * 8, 8), :] for h in range(2)]
                    for ref in (left_ref, right_ref)]
            for g in range(YG):
                v = None
                for b in range(4):
                    piece = take(prim_ref[pl.ds((f * NZ + b * YG + g) * CX + o * 8, 8), :], own)
                    v = piece if v is None else jnp.where(block == b, piece, v)
                index = spot + g % 4 * ENDS
                for side, where in ((0, low), (1, high)):
                    v = jnp.where(where, take(here[side][g // 4], index), v)
                yp_ref[pl.ds((f * YG + g) * CX + o * 8, 8), :] = v
    rows = 8 * NZ
    sxlo_ref[pl.ds(0, rows), :] = xlo_ref[...]
    sxhi_ref[pl.ds(0, rows), :] = xhi_ref[...]
    for f in range(0, 8, 2):
        for ref, start in ((sxlo_ref, 0), (sxhi_ref, CX - 1)):
            ref[pl.ds(rows + f * YG, 2 * YG), :] = yp_ref[
                pl.ds(f * YPLANE + start, 2 * YG, stride=CX), :].astype(BF16)


def ready_kernel(maps_ref, prim_ref, yp_ref, yadv_ref, x_ref, u_ref, fz_ref, sz_ref, ch_ref):
    mhd_bulk(YG, yp_ref, u_ref, fz_ref, sz_ref, ch_ref, yadv_ref, 4, True)

    source, half, _, _ = read_maps(maps_ref)
    tail = bias_rows(LANES)
    load = plane_loader(prim_ref)

    def up_of(f, z):
        return load(f, lax.rem(z + 1, NZ))

    def dn_of(f, z):
        return load(f, lax.rem(z + NZ - 1, NZ))

    @pl.loop(0, HALF, unroll=4)
    def _(z):
        both = [features(load, zz, up_of, dn_of) for zz in (z, z + HALF)]
        at = pl.ds(pl.multiple_of(z * LANES, LANES), LANES)
        for o in range(2):
            parts = []
            for a, b in zip(*both):
                a, b = a[o * 8 : o * 8 + 8], b[o * 8 : o * 8 + 8]
                parts.append(jnp.where(half == 1, take(b, source), take(a, source)))
            x_ref[pl.ds(o * KIN, KIN), at] = jnp.concatenate(parts + [tail], axis=0).astype(BF16)


def edge_kernel(maps_ref, prim_ref, bulk_ref, yp_ref, ybulk_ref, x_ref,
                xlo_ref, xhi_ref, yfl_ref, yfr_ref, wb_ref, w1_ref, w2_ref, wo_ref,
                rest_ref, badv_ref, yb_ref, ky_ref, kape_ref, sxlo_ref, sxhi_ref,
                lo_ref, hi_ref, yadv_ref):
    lane8 = iota((8, LANES), 1)
    sub = iota((8, LANES), 0)
    lo_ref[...] = xlo_ref[...].astype(F32)
    hi_ref[...] = xhi_ref[...].astype(F32)
    yrows = 8 * NZ

    yadv_ref[...] = ybulk_ref[...]
    badv_ref[...] = bulk_ref[pl.ds(4 * PLANE, 3 * PLANE), :]
    for lo in (True, False):
        start = 0 if lo else CX - 1
        ref = lo_ref if lo else hi_ref

        def add_window(c, step):
            at = pl.ds(c * YPLANE + start, YG, stride=CX)
            yadv_ref[at, :] = yadv_ref[at, :] + step

        x_ends(lambda f: yp_ref[pl.ds(f * YPLANE + start, YG, stride=CX), :],
               lambda f: ref[pl.ds(yrows + f * YG, YG), :], lo, add_window)
    yb_ref[...] = yadv_ref[pl.ds(4 * YPLANE, 3 * YPLANE), :]
    on_edge = jnp.logical_or(lane8 == 0, lane8 == LANES - 1)
    for c in (0, 1, 2, 3, 7):
        k = c if c < 4 else 4
        for z in range(NZ):
            b, g = z // YG, z % YG
            index = b * 32 + jnp.where(lane8 == LANES - 1, 25, 6)
            for o in range(2):
                at = pl.ds(c * PLANE + z * CX + o * 8, 8)
                edge = take(yadv_ref[pl.ds(c * YPLANE + g * CX + o * 8, 8), :], index)
                to = pl.ds(k * PLANE + z * CX + o * 8, 8)
                rest_ref[to, :] = jnp.where(on_edge, edge, bulk_ref[at, :])
    at_end = jnp.logical_or(lane8 == 0, lane8 == LANES - 1)
    for zs in range(0, NZ, 8):
        for lo in (True, False):
            start = zs * CX + (0 if lo else CX - 1)
            ref = lo_ref if lo else hi_ref

            def add_block(c, step):
                if 4 <= c < 7:
                    at = pl.ds((c - 4) * PLANE + start, 8, stride=CX)
                    badv_ref[at, :] = badv_ref[at, :] + step
                else:
                    at = pl.ds(min(c, 4) * PLANE + start, 8, stride=CX)
                    rest_ref[at, :] = rest_ref[at, :] + jnp.where(at_end, 0.0, step)

            x_ends(lambda f: prim_ref[pl.ds(f * PLANE + start, 8, stride=CX), :],
                   lambda f: ref[pl.ds(f * NZ + zs, 8), :], lo, add_block)

    source, half, back, ends = read_maps(maps_ref)
    tail = bias_rows(LANES)
    parts = []
    for lo in (True, False):
        start = 0 if lo else CX - 1
        ref = lo_ref if lo else hi_ref

        def row_of(f, x=start):
            return prim_ref[pl.ds(f * PLANE + x, NZ, stride=CX), :]

        def dx(f, v):
            beyond = ref[pl.ds(f * NZ, NZ), :]
            within = row_of(f, start + (1 if lo else -1))
            return 0.5 * (within - beyond) if lo else 0.5 * (beyond - within)

        def dy(v):
            return 0.5 * (next_lane(v) - prev_lane(v))

        p = [row_of(f) for f in range(8)]

        def dz(f):
            return 0.5 * (next_row(p[f]) - prev_row(p[f]))

        fs = feature_list(p[0], p[1:4], p[4:7], p[7], dx, dy, dz)
        for q in range(2):
            packed = [jnp.where(half == 1, take(v[HALF + q * 8 : HALF + q * 8 + 8], source),
                                take(v[q * 8 : q * 8 + 8], source)) for v in fs]
            parts.append(jnp.concatenate(packed + [tail], axis=0))
    xend = jnp.concatenate(parts, axis=1).astype(BF16)

    def yload(f, z):
        return yp_ref[pl.ds((f * YG + z) * CX, CX), :]

    def yup(f, z):
        return yload(f, z + 1) if z + 1 < YG else pltpu.roll(yload(f, 0), LANES - 32, 1)

    def ydn(f, z):
        return yload(f, z - 1) if z > 0 else pltpu.roll(yload(f, YG - 1), 32, 1)

    def patch_x(f, z):
        at = pl.ds(yrows + f * YG + z, 1)
        return lo_ref[at, :], hi_ref[at, :]

    window, block = lane8 % 32, lane8 // 32
    inner = window % 8
    from_window = block * 32 + jnp.where(inner < 4, inner + 3, inner + 21)
    ycells = {(o, q): [jnp.zeros((8, LANES), F32)] * 8 for o in range(2) for q in range(2)}
    for g in range(YG):
        fs = features(yload, g, yup, ydn, patch_x)
        mine = window // 8 == g % 4
        for o in range(2):
            ycells[o, g // 4] = [jnp.where(mine, take(v[o * 8 : o * 8 + 8], from_window), a)
                                 for v, a in zip(fs, ycells[o, g // 4])]
    yend = jnp.concatenate([jnp.concatenate(ycells[o, q] + [tail], axis=0)
                            for o in range(2) for q in range(2)], axis=1).astype(BF16)

    us = []
    for o, s in ((0, 1), (0, 2), (1, 5), (1, 6)):
        us.append(jnp.dot(wb_ref[pl.ds(s * HID, HID), :], x_ref[pl.ds(o * KIN, KIN), :],
                          preferred_element_type=F32))
    for cells in (xend, yend):
        ue = [jnp.dot(wb_ref[pl.ds(s * HID, HID), :], cells, preferred_element_type=F32) for s in range(8)]
        for part in range(2):
            us.append(jnp.concatenate(ue[part * 4 : part * 4 + 4], axis=1))
    rates = closure_rates(us, w1_ref[...], w2_ref[...], wo_ref[...])

    def by_row(first, k):
        acc = jnp.zeros((8, LANES), F32)
        for s in range(8):
            at = (s % 4) * 512 + k * LANES
            acc = jnp.where(sub == s, rates[first + s // 4][:8, at : at + LANES], acc)
        return acc

    low = jnp.full((NZ, LANES), RATE_LOW, BF16)
    for e in range(6):
        packed = []
        for q in range(2):
            if e in (0, 5):
                acc = by_row(4, (0 if e == 0 else 2) + q)
            else:
                acc = jnp.zeros((8, LANES), F32)
                for k in range(8):
                    z = q * 8 + k
                    acc = jnp.where(sub == k, rates[e - 1][:8, z * LANES : (z + 1) * LANES], acc)
            packed.append(acc)
            kape_ref[pl.ds(e * HALF + q * 8, 8), :] = acc
        full = []
        for h in range(2):
            listed = back[h] >= 0
            for q in range(2):
                full.append(jnp.where(listed, take(packed[q], jnp.maximum(back[h], 0)), RATE_LOW))
        full = jnp.concatenate(full, axis=0).astype(BF16)
        if e < 3:
            sxlo_ref[pl.ds((12 + e) * NZ, NZ), :] = full
        else:
            sxhi_ref[pl.ds((12 + e - 2) * NZ, NZ), :] = full
    sxlo_ref[pl.ds(15 * NZ, NZ), :] = low
    sxhi_ref[pl.ds(12 * NZ, NZ), :] = low

    mine = jnp.where(window < 16, ends[0], ends[1])
    left = yfl_ref[pl.ds(YROWS, 16), :].astype(F32)[:8]
    right = yfr_ref[pl.ds(YROWS, 16), :].astype(F32)[:8]
    listed = jnp.where(window < 6, left, jnp.where(window >= 26, right, mine.astype(F32))) > 0.5
    known = jnp.where(window < 16, window - 3, window - 21)
    known = jnp.minimum(jnp.maximum(known, 0), 7)
    for o in range(2):
        for q in range(2):
            got = by_row(6, o * 2 + q)
            for g in range(4):
                k = take(got, block * 32 + g * 8 + known)
                ky_ref[pl.ds((q * 4 + g) * CX + o * 8, 8), :] = jnp.where(listed, k, RATE_LOW)

    for f in range(3):
        for r in range(4):
            at = pl.ds((f * 4 + r) * NZ, NZ)
            sxlo_ref[at, :] = badv_ref[pl.ds(f * PLANE + r, NZ, stride=CX), :].astype(BF16)
            sxhi_ref[at, :] = badv_ref[pl.ds(f * PLANE + CX - 4 + r, NZ, stride=CX), :].astype(BF16)
    for f in range(4):
        ref, base = (yb_ref, f * YPLANE) if f < 3 else (ky_ref, 0)
        for dst, start in ((sxlo_ref, 0), (sxhi_ref, CX - 4)):
            for r in range(0, 4, 2):
                pair = [ref[pl.ds(base + start + r + k, YG, stride=CX), :] for k in range(2)]
                dst[pl.ds(16 * NZ + (f * 4 + r) * YG, 2 * YG), :] = jnp.concatenate(pair, axis=0).astype(BF16)


def inner_rates(o, x_ref, wb_ref, w1_ref, w2_ref, wo_ref, kp_ref):
    sub = iota((8, LANES), 0)
    which = range(3, 8) if o == 0 else range(5)
    us = [jnp.dot(wb_ref[pl.ds(s * HID, HID), :], x_ref[pl.ds(o * KIN, KIN), :],
                  preferred_element_type=F32) for s in which]
    rates = closure_rates(us, w1_ref[...], w2_ref[...], wo_ref[...])
    for z in range(HALF):
        acc = jnp.zeros((8, LANES), F32)
        for s, r in zip(which, rates):
            acc = jnp.where(sub == s, r[:8, z * LANES : (z + 1) * LANES], acc)
        kp_ref[pl.ds(z * 8, 8), :] = acc


def inner_kernel(maps_ref, x_ref, kape_ref, wb_ref, w1_ref, w2_ref, wo_ref,
                 kap_ref, kp_ref):
    rows = HALF * 8
    for o in range(2):
        inner_rates(o, x_ref, wb_ref, w1_ref, w2_ref, wo_ref, kp_ref.at[pl.ds(o * rows, rows), :])
    _, _, back, _ = read_maps(maps_ref)
    for e in range(6):
        x = e if e < 3 else rows + 2 + e
        kp_ref[pl.ds(x, HALF, stride=8), :] = kape_ref[pl.ds(e * HALF, HALF), :]
    for h in range(2):
        listed = back[h] >= 0
        index = jnp.maximum(back[h], 0)
        for z in range(HALF):
            for o in range(2):
                k = kp_ref[pl.ds(o * rows + z * 8, 8), :]
                kap_ref[pl.ds((h * HALF + z) * CX + o * 8, 8), :] = jnp.where(
                    listed, take(k, index), RATE_LOW)


DEEP = CX + 8


def diffuse_kernel(rest_ref, b_ref, kap_ref, yb_ref, kapy_ref, xlo_ref, xhi_ref, out_ref,
                   m0, m1, km, y0, y1, ky, xl, xh, done, sems):
    copies = [pltpu.make_async_copy(rest_ref.at[pl.ds(0, 4 * PLANE), :],
                                    out_ref.at[pl.ds(0, 4 * PLANE), :], sems.at[0]),
              pltpu.make_async_copy(rest_ref.at[pl.ds(4 * PLANE, PLANE), :],
                                    out_ref.at[pl.ds(7 * PLANE, PLANE), :], sems.at[1])]
    for copy in copies:
        copy.start()
    lane = iota((8, LANES), 1)
    window, block = lane % 32, lane // 32

    def build(field, own_ref, own_at, yown_ref, yown_at, main, edge):
        for z in range(NZ):
            main[pl.ds(z * DEEP, CX), :] = own_ref[pl.ds(own_at + z * CX, CX), :]
        for g in range(YG):
            edge[pl.ds(g * DEEP, CX), :] = yown_ref[pl.ds(yown_at + g * CX, CX), :]
        for r in range(4):
            for src, row in ((xh, CX + r), (xl, CX + 4 + r)):
                at = pl.ds((field * 4 + r) * NZ, NZ)
                main[pl.ds(row, NZ, stride=DEEP), :] = src[at, :]
                at = pl.ds(16 * NZ + (field * 4 + r) * YG, YG)
                edge[pl.ds(row, YG, stride=DEEP), :] = src[at, :]

    xl[...] = xlo_ref[...].astype(F32)
    xh[...] = xhi_ref[...].astype(F32)
    build(3, kap_ref, 0, kapy_ref, 0, km, ky)
    own = jnp.where(window < 16, window - 6, LANES - 26 + window)
    own = jnp.minimum(jnp.maximum(own, 0), LANES - 1)
    made = jnp.logical_or(window < 7, window >= 25)
    for g in range(YG):
        for o in range(3):
            v = None
            for b in range(4):
                piece = take(km[pl.ds((b * YG + g) * DEEP + o * 8, 8), :], own)
                v = piece if v is None else jnp.where(block == b, piece, v)
            at = pl.ds(g * DEEP + o * 8, 8)
            ky[at, :] = jnp.where(made, ky[at, :], v)

    def relax(c, up, dn, k):
        total = next_row(c) + prev_row(c) + next_lane(c) + prev_lane(c) + (up + dn)
        return c + k * (total - 6.0 * c)

    def at(z):
        return pl.ds(z * DEEP, DEEP)

    on_edge = jnp.logical_or(lane < 5, lane >= LANES - 5)
    for comp in range(3):
        build(comp, b_ref, comp * PLANE, yb_ref, comp * YPLANE, m0, y0)
        mains, edges = (m0, m1), (y0, y1)
        for step in range(SUB):
            a, b = mains[step % 2], mains[1 - step % 2]
            ea, eb = edges[step % 2], edges[1 - step % 2]
            for g in range(YG):
                up = ea[at(g + 1), :] if g + 1 < YG else pltpu.roll(ea[at(0), :], LANES - 32, 1)
                dn = ea[at(g - 1), :] if g > 0 else pltpu.roll(ea[at(YG - 1), :], 32, 1)
                eb[at(g), :] = relax(ea[at(g), :], up, dn, ky[at(g), :])
            dn, c = a[at(NZ - 1), :], a[at(0), :]
            for z in range(NZ):
                up = a[at((z + 1) % NZ), :]
                new = relax(c, up, dn, km[at(z), :])
                dn, c = c, up
                if step < SUB - 1:
                    b[at(z), :] = new
                    continue
                k, g = z // YG, z % YG
                index = k * 32 + jnp.where(lane < 5, 6 + lane, lane - (LANES - 26))
                index = jnp.minimum(jnp.maximum(index, 0), LANES - 1)
                for o in range(2):
                    e = take(eb[pl.ds(g * DEEP + o * 8, 8), :], index)
                    done[pl.ds(comp * PLANE + z * CX + o * 8, 8), :] = jnp.where(on_edge, e, new[o * 8 : o * 8 + 8])
        copy = pltpu.make_async_copy(done.at[pl.ds(comp * PLANE, PLANE), :],
                                     out_ref.at[pl.ds((4 + comp) * PLANE, PLANE), :], sems.at[2 + comp])
        copy.start()
        copies.append(copy)
    for copy in copies:
        copy.wait()


def struct(shape, dtype=F32):
    return jax.ShapeDtypeStruct(shape, dtype)


def params(mib):
    return pltpu.CompilerParams(vmem_limit_bytes=mib << 20)


def cost(us):
    return pl.CostEstimate(flops=us * 500_000_000, bytes_accessed=us << 20, transcendentals=0)


VSPEC = pl.BlockSpec(memory_space=pltpu.VMEM)


def step_up(axis):
    n = lax.axis_size(axis)
    return [(i, (i + 1) % n) for i in range(n)]


def step_down(axis):
    n = lax.axis_size(axis)
    return [((i + 1) % n, i) for i in range(n)]


def shards(primitive, current_sheet_bricks, brick_count, w_in, w_hid, w_out, b_hid):
    shape = primitive.shape
    prim = primitive.reshape(8 * PLANE, LANES)
    bricks = current_sheet_bricks.reshape(1, -1)
    count = brick_count.reshape(1, 1)

    blo, bhi, maps = pl.pallas_call(
        pack_kernel,
        in_specs=[pl.BlockSpec(memory_space=pltpu.HBM)] * 3,
        out_shape=[struct((YROWS + 16, LANES), BF16)] * 2 + [struct((48, LANES), jnp.int32)],
        scratch_shapes=[pltpu.VMEM((8 * PLANE, LANES), F32), pltpu.SMEM((1, 8), jnp.int32),
                        pltpu.SMEM((1, 1), jnp.int32), pltpu.SemaphoreType.DMA((10,))],
        compiler_params=params(60),
        name="pack",
    )(bricks, count, prim)
    yfl = lax.ppermute(bhi, "row", step_up("row"))
    yfr = lax.ppermute(blo, "row", step_down("row"))

    def mhd_scratch(planes):
        many = pltpu.VMEM((8 * planes * CX, LANES), F32)
        return [many, many, pltpu.VMEM((planes * CX, LANES), F32), many]

    adv, xmlo, xmhi = pl.pallas_call(
        bulk_kernel,
        out_shape=[struct((8 * PLANE, LANES))] + [struct((8 * NZ, LANES), BF16)] * 2,
        scratch_shapes=mhd_scratch(NZ),
        compiler_params=params(20),
        cost_estimate=cost(4),
        name="bulk",
    )(prim)

    sxrows = 8 * NZ + 8 * YG
    weights = [struct((8 * HID, KIN), BF16), struct((HID, KHID), BF16), struct((HID, KHID), BF16),
               struct((16, HID), BF16)]
    yp, slo, shi, *closure = pl.pallas_call(
        window_kernel,
        out_shape=[struct((8 * YPLANE, LANES))] + [struct((sxrows, LANES), BF16)] * 2 + weights,
        scratch_shapes=[pltpu.VMEM((YROWS, LANES), F32)] * 2,
        compiler_params=params(12),
        cost_estimate=cost(1),
        name="windows",
    )(prim, yfl, yfr, xmlo, xmhi, w_in, w_hid.reshape(2 * HID, HID), w_out.reshape(1, HID), b_hid)
    xlo = lax.ppermute(shi, "col", step_up("col"))
    xhi = lax.ppermute(slo, "col", step_down("col"))

    yadv, xcells = pl.pallas_call(
        ready_kernel,
        out_shape=[struct((8 * YPLANE, LANES)), struct((2 * KIN, WIDE), BF16)],
        scratch_shapes=mhd_scratch(YG),
        compiler_params=params(16),
        cost_estimate=cost(4),
        name="ready",
    )(maps, prim, yp)

    xrows = 16 * NZ + 16 * YG
    rest, badv, yb, ky, kape, sxlo, sxhi = pl.pallas_call(
        edge_kernel,
        in_specs=[VSPEC] * 14,
        out_shape=[struct((5 * PLANE, LANES)), struct((3 * PLANE, LANES)), struct((3 * YPLANE, LANES)),
                   struct((YPLANE, LANES)), struct((6 * HALF, LANES)),
                   struct((xrows, LANES), BF16), struct((xrows, LANES), BF16)],
        scratch_shapes=[pltpu.VMEM((sxrows, LANES), F32)] * 2 + [pltpu.VMEM((8 * YPLANE, LANES), F32)],
        compiler_params=params(32),
        cost_estimate=cost(8),
        name="edges",
    )(maps, prim, adv, yp, yadv, xcells, xlo, xhi, yfl, yfr, *closure)

    gothi = lax.ppermute(sxlo, "col", step_down("col"))
    gotlo = lax.ppermute(sxhi, "col", step_up("col"))

    kap = pl.pallas_call(
        inner_kernel,
        in_specs=[VSPEC] * 7,
        out_shape=struct((PLANE, LANES)),
        scratch_shapes=[pltpu.VMEM((HALF * CX, LANES), F32)],
        compiler_params=params(24),
        cost_estimate=cost(6),
        name="inner",
    )(maps, xcells, kape, *closure)

    out = pl.pallas_call(
        diffuse_kernel,
        out_specs=pl.BlockSpec(memory_space=pltpu.HBM),
        out_shape=struct((8 * PLANE, LANES)),
        scratch_shapes=[pltpu.VMEM((NZ * DEEP, LANES), F32)] * 3
        + [pltpu.VMEM((YG * DEEP, LANES), F32)] * 3
        + [pltpu.VMEM((xrows, LANES), F32)] * 2
        + [pltpu.VMEM((3 * PLANE, LANES), F32), pltpu.SemaphoreType.DMA((5,))],
        compiler_params=params(16),
        name="diffuse",
    )(rest, badv, kap, yb, ky, gotlo, gothi)
    return out.reshape(shape)


def solution(mesh):
    return jax.shard_map(
        shards,
        mesh=mesh,
        in_specs=(
            P(None, None, "col", "row"),
            P("row", "col", None),
            P("row", "col"),
            P(),
            P(),
            P(),
            P(),
        ),
        out_specs=P(None, None, "col", "row"),
        check_vma=False,
    )
```

```python
import jax
import jax.numpy as jnp
from jax import lax
from jax.experimental import pallas as pl
from jax.experimental.pallas import tpu as pltpu
from jax.sharding import PartitionSpec as P

BRICK = 16
SUB = 4
ADIABATIC = 5.0 / 3.0
TIME_STEP = 0.02
RATE_LOW = 0.02
RATE_SPAN = 0.14
GELU_A = 0.7978845608
GELU_B = 0.7978845608 * 0.044715
F32 = jnp.float32
BF16 = jnp.bfloat16
LANES = 128
NZ = 32
CX = 16
HID = 128
PLANE = NZ * CX
KIN = 80
KHID = HID + 16


def iota(shape, dim):
    return lax.broadcasted_iota(jnp.int32, shape, dim)


def take(values, index):
    return jnp.take_along_axis(values, index, axis=1, mode="promise_in_bounds")


def next_row(v):
    return pltpu.roll(v, v.shape[0] - 1, 0)


def prev_row(v):
    return pltpu.roll(v, 1, 0)


def next_lane(v):
    return pltpu.roll(v, v.shape[1] - 1, 1)


def prev_lane(v):
    return pltpu.roll(v, 1, 1)


def derive(p):
    rho, pr = p[0], p[7]
    v, b = p[1:4], p[4:7]
    m = [rho * c for c in v]
    b2 = b[0] * b[0] + b[1] * b[1] + b[2] * b[2]
    v2 = v[0] * v[0] + v[1] * v[1] + v[2] * v[2]
    vb = v[0] * b[0] + v[1] * b[1] + v[2] * b[2]
    pt = pr + 0.5 * b2
    en = 1.5 * pr + 0.5 * (rho * v2 + b2)
    wave = ADIABATIC * pr + b2
    fast = wave * lax.rsqrt(wave * rho)
    ep = en + pt
    tens = {(i, j): m[i] * v[j] - b[i] * b[j] for i in range(3) for j in range(i, 3)}
    elec = {(i, j): v[i] * b[j] - b[i] * v[j] for i in range(3) for j in range(i + 1, 3)}
    fluxes = []
    for d in range(3):
        rows = [m[d]]
        for c in range(3):
            t = tens[(min(c, d), max(c, d))]
            rows.append(t + pt if c == d else t)
        for c in range(3):
            rows.append(None if c == d else (elec[(d, c)] if d < c else -elec[(c, d)]))
        rows.append(ep * v[d] - b[d] * vb)
        fluxes.append(rows)
    speeds = [jnp.abs(c) + fast for c in v]
    return [rho] + m + list(b) + [en], fluxes, speeds


def face(rows, u, un, f, fn, s, sn):
    a = 0.5 * jnp.maximum(s, sn)
    out = {}
    for c in rows:
        diss = a * (un[c] - u[c])
        out[c] = -diss if f[c] is None else 0.5 * (f[c] + fn[c]) - diss
    return out


def gelu_twice(u):
    u = u.astype(BF16)
    t = jnp.tanh(u * (jnp.asarray(GELU_A, BF16) + jnp.asarray(GELU_B, BF16) * (u * u)))
    return u + u * t


def closure_rates(first, w1, w2, wo):
    us = first
    for w in (w1, w2):
        hs = [jnp.concatenate([gelu_twice(u), bias_rows(u.shape[1]).astype(BF16)], axis=0) for u in us]
        us = [jnp.dot(w, h, preferred_element_type=F32) for h in hs]
    hs = [gelu_twice(u) for u in us]
    scores = [jnp.dot(wo, h, preferred_element_type=F32) for h in hs]
    return [(RATE_LOW + 0.5 * RATE_SPAN) + (0.5 * RATE_SPAN) * jnp.tanh(0.5 * s) for s in scores]


def features(load, z, up_of, dn_of, patch_x=None):
    row = iota((CX, LANES), 0)

    def dx(f, v):
        up, dn = next_row(v), prev_row(v)
        if patch_x is not None:
            lo, hi = patch_x(f, z)
            up = jnp.where(row == CX - 1, hi, up)
            dn = jnp.where(row == 0, lo, dn)
        return 0.5 * (up - dn)

    def dy(v):
        return 0.5 * (next_lane(v) - prev_lane(v))

    def dz(f):
        return 0.5 * (up_of(f, z) - dn_of(f, z))

    rho, vx, vy, vz, bx, by, bz, pr = [load(f, z) for f in range(8)]
    return feature_list(rho, (vx, vy, vz), (bx, by, bz), pr, lambda f, v: dx(f, v), dy, dz)


def feature_list(rho, v, b, pr, dx, dy, dz):
    jx = dy(b[2]) - dz(5)
    jy = dz(4) - dx(6, b[2])
    jz = dx(5, b[1]) - dy(b[0])
    div = dx(1, v[0]) + dy(v[1]) + dz(3)
    return [jx, jy, jz, div, rho, pr, b[0] * b[0] + b[1] * b[1] + b[2] * b[2],
            v[0] * v[0] + v[1] * v[1] + v[2] * v[2]]


def bias_rows(n):
    return jnp.where(iota((16, n), 0) < 3, 1.0, 0.0)


def plane_at(f, z):
    return pl.ds(pl.multiple_of((f * NZ + z) * CX, CX), CX)


def plane_loader(prim_ref):
    def load(f, z):
        return prim_ref[plane_at(f, z), :]

    return load


HALF = NZ // 2
WIDE = HALF * LANES
YG = NZ // 4
YPLANE = YG * CX
ENDS = 8
YROWS = 8 * 2 * CX


def pack_kernel(bricks_hbm, count_hbm, hbm_ref, lo_ref, hi_ref, maps_ref, prim_ref, bricks_ref, count_ref, sems):
    lane = iota((8, LANES), 1)
    spot = lane % ENDS

    def fetch(f):
        at = pl.ds(f * PLANE, PLANE)
        return pltpu.make_async_copy(hbm_ref.at[at, :], prim_ref.at[at, :], sems.at[f])

    for f in range(8):
        fetch(f).start()
    lists = [pltpu.make_async_copy(bricks_hbm, bricks_ref, sems.at[8]),
             pltpu.make_async_copy(count_hbm, count_ref, sems.at[9])]
    for copy in lists:
        copy.start()
    for f in range(8):
        fetch(f).wait()
        for h in range(2):
            los, his = [], []
            for o in range(2):
                lo = jnp.zeros((8, LANES), F32)
                hi = jnp.zeros((8, LANES), F32)
                for spot_z in range(HALF):
                    z = spot_z // 4 * YG + h * 4 + spot_z % 4
                    v = prim_ref[pl.ds((f * NZ + z) * CX + o * 8, 8), :]
                    mine = lane // ENDS == spot_z
                    lo = jnp.where(mine, take(v, spot), lo)
                    hi = jnp.where(mine, take(v, spot + (LANES - ENDS)), hi)
                los.append(lo)
                his.append(hi)
            at = pl.ds((f * 2 + h) * CX, CX)
            lo_ref[at, :] = jnp.concatenate(los, axis=0).astype(BF16)
            hi_ref[at, :] = jnp.concatenate(his, axis=0).astype(BF16)
    for copy in lists:
        copy.wait()
    source, half, back, ends = brick_rows(bricks_ref, count_ref)
    second = lane >= LANES // 2
    listed = [jnp.where(second, ends[1][side], ends[0][side]) for side in range(2)]
    for k, v in enumerate([source, half] + back + listed):
        maps_ref[pl.ds(k * 8, 8), :] = v
    for ref, flag in ((lo_ref, listed[0]), (hi_ref, listed[1])):
        ref[pl.ds(YROWS, 16), :] = jnp.concatenate([flag, flag], axis=0).astype(F32).astype(BF16)


def brick_rows(bricks_ref, count_ref):
    lane = iota((8, LANES), 1)
    slot, inner = lane // BRICK, lane % BRICK
    source = jnp.zeros((8, LANES), jnp.int32)
    half = jnp.zeros((8, LANES), jnp.int32)
    back = [jnp.full((8, LANES), -1, jnp.int32) for _ in range(2)]
    per_half = LANES // BRICK
    ends = [[0, 0], [0, 0]]
    for j in range(8):
        b = bricks_ref[0, j]
        bz, by = b // per_half, b % per_half
        source = jnp.where(slot == j, by * BRICK + inner, source)
        half = jnp.where(slot == j, bz, half)
        for h in range(2):
            use = jnp.logical_and(bz == h, j < count_ref[0, 0])
            want = jnp.where(use, by, -1)
            back[h] = jnp.where(slot == want, j * BRICK + inner, back[h])
            for side, end in enumerate((0, per_half - 1)):
                ends[h][side] = jnp.where(want == end, 1, ends[h][side])
    return source, half, back, ends


def read_maps(maps_ref):
    source, half, back0, back1, low, high = [maps_ref[pl.ds(k * 8, 8), :] for k in range(6)]
    return source, half, [back0, back1], [low, high]


def mhd_bulk(count, prim_ref, u_ref, fz_ref, sz_ref, ch_ref, out_ref, unroll, windows):
    rows = range(8)
    row, lane = iota((CX, LANES), 0), iota((CX, LANES), 1)

    def at(f, z):
        return pl.ds(pl.multiple_of((f * count + z) * CX, CX), CX)

    @pl.loop(0, count, unroll=unroll)
    def _(z):
        u, f, s = derive([prim_ref[at(k, z), :] for k in rows])

        def along(d, nxt, prv, last):
            un = {c: nxt(u[c]) for c in rows}
            fn = {c: None if f[d][c] is None else nxt(f[d][c]) for c in rows}
            fc = face(rows, u, un, f[d], fn, s[d], nxt(s[d]))
            out = {}
            for c in rows:
                inside = fc[c] if last is None else jnp.where(last, 0.0, fc[c])
                out[c] = inside - prv(inside)
            return out

        cx = along(0, next_row, prev_row, row == CX - 1)
        cy = along(1, next_lane, prev_lane, None if windows else lane == LANES - 1)
        for c in rows:
            ch_ref[at(c, z), :] = u[c] - TIME_STEP * (cx[c] + cy[c])
            u_ref[at(c, z), :] = u[c]
            if f[2][c] is not None:
                fz_ref[at(c, z), :] = f[2][c]
        sz_ref[at(0, z), :] = s[2]

    def zface(z, zn, turn):
        u = {c: u_ref[at(c, z), :] for c in rows}
        un = {c: turn(u_ref[at(c, zn), :]) for c in rows}
        f = {c: None if c == 6 else fz_ref[at(c, z), :] for c in rows}
        fn = {c: None if c == 6 else turn(fz_ref[at(c, zn), :]) for c in rows}
        return face(rows, u, un, f, fn, sz_ref[at(0, z), :], turn(sz_ref[at(0, zn), :]))

    def finish(z, before, here):
        for c in rows:
            out_ref[at(c, z), :] = ch_ref[at(c, z), :] - TIME_STEP * (here[c] - before[c])
        return tuple(here[c] for c in rows)

    if windows:
        last = zface(count - 1, 0, lambda v: pltpu.roll(v, LANES - 32, 1))
        before = tuple(pltpu.roll(last[c], 32, 1) for c in rows)
        for z in range(count):
            here = last if z == count - 1 else zface(z, z + 1, lambda v: v)
            before = finish(z, before, here)
    else:
        def step(z, before):
            return finish(z, before, zface(z, lax.rem(z + 1, count), lambda v: v))

        last = zface(count - 1, 0, lambda v: v)
        lax.fori_loop(0, count, step, tuple(last[c] for c in rows), unroll=unroll)


def x_ends(own_of, halo_of, lo, add):
    rows = range(8)
    uo, fo, so = derive([own_of(f) for f in rows])
    uh, fh, sh = derive([halo_of(f) for f in rows])
    if lo:
        fc = face(rows, uh, uo, fh[0], fo[0], sh[0], so[0])
    else:
        fc = face(rows, uo, uh, fo[0], fh[0], so[0], sh[0])
    for c in rows:
        step = TIME_STEP * fc[c]
        add(c, step if lo else -step)


def bulk_kernel(prim_ref, adv_ref, xlo_ref, xhi_ref, u_ref, fz_ref, sz_ref, ch_ref):
    mhd_bulk(NZ, prim_ref, u_ref, fz_ref, sz_ref, ch_ref, adv_ref, 4, False)
    for f in range(8):
        at = pl.ds(f * NZ, NZ)
        xlo_ref[at, :] = prim_ref[pl.ds(f * PLANE, NZ, stride=CX), :].astype(BF16)
        xhi_ref[at, :] = prim_ref[pl.ds(f * PLANE + CX - 1, NZ, stride=CX), :].astype(BF16)


def prepare_weights(win_ref, whid_ref, wout_ref, bias_ref, wb_ref, w1_ref, w2_ref, wo_ref):
    def split(b):
        hi = b.astype(BF16)
        r = b - hi.astype(F32)
        mid = r.astype(BF16)
        return [hi.astype(F32), mid.astype(F32), r - mid.astype(F32)]

    cols = (((0,), (0,)), ((), ()))
    rows = iota((16, KIN), 0)
    col = iota((16, KIN), 1)
    first = jnp.concatenate(
        [win_ref[...].astype(F32)] + split(bias_ref[0:1, :]) + [jnp.zeros((5, HID), F32)], axis=0
    ).astype(BF16)
    for s in range(8):
        spot = jnp.where(rows < 8, rows * 8 + s, jnp.where(rows < 11, 64 + rows - 8, -1))
        pick = jnp.where(col == spot, 1.0, 0.0).astype(BF16)
        wb_ref[pl.ds(s * HID, HID), :] = lax.dot_general(
            first, pick, cols, preferred_element_type=F32).astype(BF16)
    eye = jnp.where(iota((HID, HID), 0) == iota((HID, HID), 1), 0.5, 0.0).astype(BF16)
    eye16 = jnp.where(iota((16, 16), 0) == iota((16, 16), 1), 1.0, 0.0).astype(BF16)
    for layer, ref in ((0, w1_ref), (1, w2_ref)):
        turned = lax.dot_general(whid_ref[pl.ds(layer * HID, HID), :], eye, cols,
                                 preferred_element_type=F32)
        brow = jnp.concatenate(
            split(bias_ref[layer + 1 : layer + 2, :]) + [jnp.zeros((13, HID), F32)], axis=0
        ).astype(BF16)
        bcol = lax.dot_general(brow, eye16, cols, preferred_element_type=F32)
        ref[...] = jnp.concatenate([turned, bcol], axis=1).astype(BF16)
    wo_ref[...] = jnp.broadcast_to(0.5 * wout_ref[...].astype(F32), (16, HID)).astype(BF16)


def window_kernel(prim_ref, yfl_ref, yfr_ref, xlo_ref, xhi_ref, win_ref, whid_ref, wout_ref, bias_ref,
                  yp_ref, sxlo_ref, sxhi_ref, wb_ref, w1_ref, w2_ref, wo_ref, left_ref, right_ref):
    prepare_weights(win_ref, whid_ref, wout_ref, bias_ref, wb_ref, w1_ref, w2_ref, wo_ref)
    lane = iota((8, LANES), 1)
    window, block = lane % 32, lane // 32
    own = jnp.where(window < 16, window - 6, LANES - 26 + window)
    own = jnp.minimum(jnp.maximum(own, 0), LANES - 1)
    spot = block * 32 + jnp.where(window < 16, jnp.minimum(window + 2, 7), jnp.maximum(window - 26, 0))
    left_ref[...] = yfl_ref[pl.ds(0, YROWS), :].astype(F32)
    right_ref[...] = yfr_ref[pl.ds(0, YROWS), :].astype(F32)
    low, high = window < 6, window >= 26
    for f in range(8):
        for o in range(2):
            here = [[ref[pl.ds((f * 2 + h) * CX + o * 8, 8), :] for h in range(2)]
                    for ref in (left_ref, right_ref)]
            for g in range(YG):
                v = None
                for b in range(4):
                    piece = take(prim_ref[pl.ds((f * NZ + b * YG + g) * CX + o * 8, 8), :], own)
                    v = piece if v is None else jnp.where(block == b, piece, v)
                index = spot + g % 4 * ENDS
                for side, where in ((0, low), (1, high)):
                    v = jnp.where(where, take(here[side][g // 4], index), v)
                yp_ref[pl.ds((f * YG + g) * CX + o * 8, 8), :] = v
    rows = 8 * NZ
    sxlo_ref[pl.ds(0, rows), :] = xlo_ref[...]
    sxhi_ref[pl.ds(0, rows), :] = xhi_ref[...]
    for f in range(0, 8, 2):
        for ref, start in ((sxlo_ref, 0), (sxhi_ref, CX - 1)):
            ref[pl.ds(rows + f * YG, 2 * YG), :] = yp_ref[
                pl.ds(f * YPLANE + start, 2 * YG, stride=CX), :].astype(BF16)


def ready_kernel(maps_ref, prim_ref, yp_ref, yadv_ref, x_ref, u_ref, fz_ref, sz_ref, ch_ref):
    mhd_bulk(YG, yp_ref, u_ref, fz_ref, sz_ref, ch_ref, yadv_ref, 4, True)

    source, half, _, _ = read_maps(maps_ref)
    tail = bias_rows(LANES)
    load = plane_loader(prim_ref)

    def up_of(f, z):
        return load(f, lax.rem(z + 1, NZ))

    def dn_of(f, z):
        return load(f, lax.rem(z + NZ - 1, NZ))

    @pl.loop(0, HALF, unroll=4)
    def _(z):
        both = [features(load, zz, up_of, dn_of) for zz in (z, z + HALF)]
        at = pl.ds(pl.multiple_of(z * LANES, LANES), LANES)
        for o in range(2):
            parts = []
            for a, b in zip(*both):
                a, b = a[o * 8 : o * 8 + 8], b[o * 8 : o * 8 + 8]
                parts.append(jnp.where(half == 1, take(b, source), take(a, source)))
            x_ref[pl.ds(o * KIN, KIN), at] = jnp.concatenate(parts + [tail], axis=0).astype(BF16)


def edge_kernel(maps_ref, prim_ref, bulk_ref, yp_ref, ybulk_ref, x_ref,
                xlo_ref, xhi_ref, yfl_ref, yfr_ref, wb_ref, w1_ref, w2_ref, wo_ref,
                rest_ref, badv_ref, yb_ref, ky_ref, kape_ref, sxlo_ref, sxhi_ref,
                lo_ref, hi_ref, yadv_ref):
    lane8 = iota((8, LANES), 1)
    sub = iota((8, LANES), 0)
    lo_ref[...] = xlo_ref[...].astype(F32)
    hi_ref[...] = xhi_ref[...].astype(F32)
    yrows = 8 * NZ

    yadv_ref[...] = ybulk_ref[...]
    badv_ref[...] = bulk_ref[pl.ds(4 * PLANE, 3 * PLANE), :]
    for lo in (True, False):
        start = 0 if lo else CX - 1
        ref = lo_ref if lo else hi_ref

        def add_window(c, step):
            at = pl.ds(c * YPLANE + start, YG, stride=CX)
            yadv_ref[at, :] = yadv_ref[at, :] + step

        x_ends(lambda f: yp_ref[pl.ds(f * YPLANE + start, YG, stride=CX), :],
               lambda f: ref[pl.ds(yrows + f * YG, YG), :], lo, add_window)
    yb_ref[...] = yadv_ref[pl.ds(4 * YPLANE, 3 * YPLANE), :]
    on_edge = jnp.logical_or(lane8 == 0, lane8 == LANES - 1)
    for c in (0, 1, 2, 3, 7):
        k = c if c < 4 else 4
        for z in range(NZ):
            b, g = z // YG, z % YG
            index = b * 32 + jnp.where(lane8 == LANES - 1, 25, 6)
            for o in range(2):
                at = pl.ds(c * PLANE + z * CX + o * 8, 8)
                edge = take(yadv_ref[pl.ds(c * YPLANE + g * CX + o * 8, 8), :], index)
                to = pl.ds(k * PLANE + z * CX + o * 8, 8)
                rest_ref[to, :] = jnp.where(on_edge, edge, bulk_ref[at, :])
    at_end = jnp.logical_or(lane8 == 0, lane8 == LANES - 1)
    for zs in range(0, NZ, 8):
        for lo in (True, False):
            start = zs * CX + (0 if lo else CX - 1)
            ref = lo_ref if lo else hi_ref

            def add_block(c, step):
                if 4 <= c < 7:
                    at = pl.ds((c - 4) * PLANE + start, 8, stride=CX)
                    badv_ref[at, :] = badv_ref[at, :] + step
                else:
                    at = pl.ds(min(c, 4) * PLANE + start, 8, stride=CX)
                    rest_ref[at, :] = rest_ref[at, :] + jnp.where(at_end, 0.0, step)

            x_ends(lambda f: prim_ref[pl.ds(f * PLANE + start, 8, stride=CX), :],
                   lambda f: ref[pl.ds(f * NZ + zs, 8), :], lo, add_block)

    source, half, back, ends = read_maps(maps_ref)
    tail = bias_rows(LANES)
    parts = []
    for lo in (True, False):
        start = 0 if lo else CX - 1
        ref = lo_ref if lo else hi_ref

        def row_of(f, x=start):
            return prim_ref[pl.ds(f * PLANE + x, NZ, stride=CX), :]

        def dx(f, v):
            beyond = ref[pl.ds(f * NZ, NZ), :]
            within = row_of(f, start + (1 if lo else -1))
            return 0.5 * (within - beyond) if lo else 0.5 * (beyond - within)

        def dy(v):
            return 0.5 * (next_lane(v) - prev_lane(v))

        p = [row_of(f) for f in range(8)]

        def dz(f):
            return 0.5 * (next_row(p[f]) - prev_row(p[f]))

        fs = feature_list(p[0], p[1:4], p[4:7], p[7], dx, dy, dz)
        for q in range(2):
            packed = [jnp.where(half == 1, take(v[HALF + q * 8 : HALF + q * 8 + 8], source),
                                take(v[q * 8 : q * 8 + 8], source)) for v in fs]
            parts.append(jnp.concatenate(packed + [tail], axis=0))
    xend = jnp.concatenate(parts, axis=1).astype(BF16)

    def yload(f, z):
        return yp_ref[pl.ds((f * YG + z) * CX, CX), :]

    def yup(f, z):
        return yload(f, z + 1) if z + 1 < YG else pltpu.roll(yload(f, 0), LANES - 32, 1)

    def ydn(f, z):
        return yload(f, z - 1) if z > 0 else pltpu.roll(yload(f, YG - 1), 32, 1)

    def patch_x(f, z):
        at = pl.ds(yrows + f * YG + z, 1)
        return lo_ref[at, :], hi_ref[at, :]

    window, block = lane8 % 32, lane8 // 32
    inner = window % 8
    from_window = block * 32 + jnp.where(inner < 4, inner + 3, inner + 21)
    ycells = {(o, q): [jnp.zeros((8, LANES), F32)] * 8 for o in range(2) for q in range(2)}
    for g in range(YG):
        fs = features(yload, g, yup, ydn, patch_x)
        mine = window // 8 == g % 4
        for o in range(2):
            ycells[o, g // 4] = [jnp.where(mine, take(v[o * 8 : o * 8 + 8], from_window), a)
                                 for v, a in zip(fs, ycells[o, g // 4])]
    yend = jnp.concatenate([jnp.concatenate(ycells[o, q] + [tail], axis=0)
                            for o in range(2) for q in range(2)], axis=1).astype(BF16)

    us = []
    for o, s in ((0, 1), (0, 2), (1, 5), (1, 6)):
        us.append(jnp.dot(wb_ref[pl.ds(s * HID, HID), :], x_ref[pl.ds(o * KIN, KIN), :],
                          preferred_element_type=F32))
    for cells in (xend, yend):
        ue = [jnp.dot(wb_ref[pl.ds(s * HID, HID), :], cells, preferred_element_type=F32) for s in range(8)]
        for part in range(2):
            us.append(jnp.concatenate(ue[part * 4 : part * 4 + 4], axis=1))
    rates = closure_rates(us, w1_ref[...], w2_ref[...], wo_ref[...])

    def by_row(first, k):
        acc = jnp.zeros((8, LANES), F32)
        for s in range(8):
            at = (s % 4) * 512 + k * LANES
            acc = jnp.where(sub == s, rates[first + s // 4][:8, at : at + LANES], acc)
        return acc

    low = jnp.full((NZ, LANES), RATE_LOW, BF16)
    for e in range(6):
        packed = []
        for q in range(2):
            if e in (0, 5):
                acc = by_row(4, (0 if e == 0 else 2) + q)
            else:
                acc = jnp.zeros((8, LANES), F32)
                for k in range(8):
                    z = q * 8 + k
                    acc = jnp.where(sub == k, rates[e - 1][:8, z * LANES : (z + 1) * LANES], acc)
            packed.append(acc)
            kape_ref[pl.ds(e * HALF + q * 8, 8), :] = acc
        full = []
        for h in range(2):
            listed = back[h] >= 0
            for q in range(2):
                full.append(jnp.where(listed, take(packed[q], jnp.maximum(back[h], 0)), RATE_LOW))
        full = jnp.concatenate(full, axis=0).astype(BF16)
        if e < 3:
            sxlo_ref[pl.ds((12 + e) * NZ, NZ), :] = full
        else:
            sxhi_ref[pl.ds((12 + e - 2) * NZ, NZ), :] = full
    sxlo_ref[pl.ds(15 * NZ, NZ), :] = low
    sxhi_ref[pl.ds(12 * NZ, NZ), :] = low

    mine = jnp.where(window < 16, ends[0], ends[1])
    left = yfl_ref[pl.ds(YROWS, 16), :].astype(F32)[:8]
    right = yfr_ref[pl.ds(YROWS, 16), :].astype(F32)[:8]
    listed = jnp.where(window < 6, left, jnp.where(window >= 26, right, mine.astype(F32))) > 0.5
    known = jnp.where(window < 16, window - 3, window - 21)
    known = jnp.minimum(jnp.maximum(known, 0), 7)
    for o in range(2):
        for q in range(2):
            got = by_row(6, o * 2 + q)
            for g in range(4):
                k = take(got, block * 32 + g * 8 + known)
                ky_ref[pl.ds((q * 4 + g) * CX + o * 8, 8), :] = jnp.where(listed, k, RATE_LOW)

    for f in range(3):
        for r in range(4):
            at = pl.ds((f * 4 + r) * NZ, NZ)
            sxlo_ref[at, :] = badv_ref[pl.ds(f * PLANE + r, NZ, stride=CX), :].astype(BF16)
            sxhi_ref[at, :] = badv_ref[pl.ds(f * PLANE + CX - 4 + r, NZ, stride=CX), :].astype(BF16)
    for f in range(4):
        ref, base = (yb_ref, f * YPLANE) if f < 3 else (ky_ref, 0)
        for dst, start in ((sxlo_ref, 0), (sxhi_ref, CX - 4)):
            for r in range(0, 4, 2):
                pair = [ref[pl.ds(base + start + r + k, YG, stride=CX), :] for k in range(2)]
                dst[pl.ds(16 * NZ + (f * 4 + r) * YG, 2 * YG), :] = jnp.concatenate(pair, axis=0).astype(BF16)


def inner_rates(o, x_ref, wb_ref, w1_ref, w2_ref, wo_ref, kp_ref):
    sub = iota((8, LANES), 0)
    which = range(3, 8) if o == 0 else range(5)
    us = [jnp.dot(wb_ref[pl.ds(s * HID, HID), :], x_ref[pl.ds(o * KIN, KIN), :],
                  preferred_element_type=F32) for s in which]
    rates = closure_rates(us, w1_ref[...], w2_ref[...], wo_ref[...])
    for z in range(HALF):
        acc = jnp.zeros((8, LANES), F32)
        for s, r in zip(which, rates):
            acc = jnp.where(sub == s, r[:8, z * LANES : (z + 1) * LANES], acc)
        kp_ref[pl.ds(z * 8, 8), :] = acc


def inner_kernel(maps_ref, x_ref, kape_ref, wb_ref, w1_ref, w2_ref, wo_ref,
                 kap_ref, kp_ref):
    rows = HALF * 8
    for o in range(2):
        inner_rates(o, x_ref, wb_ref, w1_ref, w2_ref, wo_ref, kp_ref.at[pl.ds(o * rows, rows), :])
    _, _, back, _ = read_maps(maps_ref)
    for e in range(6):
        x = e if e < 3 else rows + 2 + e
        kp_ref[pl.ds(x, HALF, stride=8), :] = kape_ref[pl.ds(e * HALF, HALF), :]
    for h in range(2):
        listed = back[h] >= 0
        index = jnp.maximum(back[h], 0)
        for z in range(HALF):
            for o in range(2):
                k = kp_ref[pl.ds(o * rows + z * 8, 8), :]
                kap_ref[pl.ds((h * HALF + z) * CX + o * 8, 8), :] = jnp.where(
                    listed, take(k, index), RATE_LOW)


DEEP = CX + 8


def diffuse_kernel(rest_ref, b_ref, kap_ref, yb_ref, kapy_ref, xlo_ref, xhi_ref, out_ref,
                   m0, m1, km, y0, y1, ky, xl, xh, done, kc, kyc, sems):
    copies = [pltpu.make_async_copy(rest_ref.at[pl.ds(0, 4 * PLANE), :],
                                    out_ref.at[pl.ds(0, 4 * PLANE), :], sems.at[0]),
              pltpu.make_async_copy(rest_ref.at[pl.ds(4 * PLANE, PLANE), :],
                                    out_ref.at[pl.ds(7 * PLANE, PLANE), :], sems.at[1])]
    for copy in copies:
        copy.start()
    lane = iota((8, LANES), 1)
    window, block = lane % 32, lane // 32

    def build(field, own_ref, own_at, yown_ref, yown_at, main, edge):
        for z in range(NZ):
            main[pl.ds(z * DEEP, CX), :] = own_ref[pl.ds(own_at + z * CX, CX), :]
        for g in range(YG):
            edge[pl.ds(g * DEEP, CX), :] = yown_ref[pl.ds(yown_at + g * CX, CX), :]
        for r in range(4):
            for src, row in ((xh, CX + r), (xl, CX + 4 + r)):
                at = pl.ds((field * 4 + r) * NZ, NZ)
                main[pl.ds(row, NZ, stride=DEEP), :] = src[at, :]
                at = pl.ds(16 * NZ + (field * 4 + r) * YG, YG)
                edge[pl.ds(row, YG, stride=DEEP), :] = src[at, :]

    xl[...] = xlo_ref[...].astype(F32)
    xh[...] = xhi_ref[...].astype(F32)
    build(3, kap_ref, 0, kapy_ref, 0, km, ky)
    own = jnp.where(window < 16, window - 6, LANES - 26 + window)
    own = jnp.minimum(jnp.maximum(own, 0), LANES - 1)
    made = jnp.logical_or(window < 7, window >= 25)
    for g in range(YG):
        for o in range(3):
            v = None
            for b in range(4):
                piece = take(km[pl.ds((b * YG + g) * DEEP + o * 8, 8), :], own)
                v = piece if v is None else jnp.where(block == b, piece, v)
            at = pl.ds(g * DEEP + o * 8, 8)
            ky[at, :] = jnp.where(made, ky[at, :], v)

    kc[...] = 1.0 - 6.0 * km[...]
    kyc[...] = 1.0 - 6.0 * ky[...]

    def relax(c, up, dn, k, own):
        total = (next_row(c) + prev_row(c)) + (next_lane(c) + prev_lane(c)) + (up + dn)
        return own * c + k * total

    def at(z):
        return pl.ds(z * DEEP, DEEP)

    on_edge = jnp.logical_or(lane < 5, lane >= LANES - 5)
    for comp in range(3):
        build(comp, b_ref, comp * PLANE, yb_ref, comp * YPLANE, m0, y0)
        mains, edges = (m0, m1), (y0, y1)
        for step in range(SUB):
            a, b = mains[step % 2], mains[1 - step % 2]
            ea, eb = edges[step % 2], edges[1 - step % 2]
            for g in range(YG):
                up = ea[at(g + 1), :] if g + 1 < YG else pltpu.roll(ea[at(0), :], LANES - 32, 1)
                dn = ea[at(g - 1), :] if g > 0 else pltpu.roll(ea[at(YG - 1), :], 32, 1)
                eb[at(g), :] = relax(ea[at(g), :], up, dn, ky[at(g), :], kyc[at(g), :])
            dn, c = a[at(NZ - 1), :], a[at(0), :]
            for z in range(NZ):
                up = a[at((z + 1) % NZ), :]
                new = relax(c, up, dn, km[at(z), :], kc[at(z), :])
                dn, c = c, up
                if step < SUB - 1:
                    b[at(z), :] = new
                    continue
                k, g = z // YG, z % YG
                index = k * 32 + jnp.where(lane < 5, 6 + lane, lane - (LANES - 26))
                index = jnp.minimum(jnp.maximum(index, 0), LANES - 1)
                for o in range(2):
                    e = take(eb[pl.ds(g * DEEP + o * 8, 8), :], index)
                    done[pl.ds(comp * PLANE + z * CX + o * 8, 8), :] = jnp.where(on_edge, e, new[o * 8 : o * 8 + 8])
        copy = pltpu.make_async_copy(done.at[pl.ds(comp * PLANE, PLANE), :],
                                     out_ref.at[pl.ds((4 + comp) * PLANE, PLANE), :], sems.at[2 + comp])
        copy.start()
        copies.append(copy)
    for copy in copies:
        copy.wait()


def struct(shape, dtype=F32):
    return jax.ShapeDtypeStruct(shape, dtype)


def params(mib):
    return pltpu.CompilerParams(vmem_limit_bytes=mib << 20)


def cost(us):
    return pl.CostEstimate(flops=us * 500_000_000, bytes_accessed=us << 20, transcendentals=0)


VSPEC = pl.BlockSpec(memory_space=pltpu.VMEM)


def step_up(axis):
    n = lax.axis_size(axis)
    return [(i, (i + 1) % n) for i in range(n)]


def step_down(axis):
    n = lax.axis_size(axis)
    return [((i + 1) % n, i) for i in range(n)]


def shards(primitive, current_sheet_bricks, brick_count, w_in, w_hid, w_out, b_hid):
    shape = primitive.shape
    prim = primitive.reshape(8 * PLANE, LANES)
    bricks = current_sheet_bricks.reshape(1, -1)
    count = brick_count.reshape(1, 1)

    blo, bhi, maps = pl.pallas_call(
        pack_kernel,
        in_specs=[pl.BlockSpec(memory_space=pltpu.HBM)] * 3,
        out_shape=[struct((YROWS + 16, LANES), BF16)] * 2 + [struct((48, LANES), jnp.int32)],
        scratch_shapes=[pltpu.VMEM((8 * PLANE, LANES), F32), pltpu.SMEM((1, 8), jnp.int32),
                        pltpu.SMEM((1, 1), jnp.int32), pltpu.SemaphoreType.DMA((10,))],
        compiler_params=params(60),
        name="pack",
    )(bricks, count, prim)
    yfr = lax.ppermute(blo, "row", step_down("row"))
    yfl = lax.ppermute(bhi, "row", step_up("row"))

    def mhd_scratch(planes):
        many = pltpu.VMEM((8 * planes * CX, LANES), F32)
        return [many, many, pltpu.VMEM((planes * CX, LANES), F32), many]

    adv, xmlo, xmhi = pl.pallas_call(
        bulk_kernel,
        out_shape=[struct((8 * PLANE, LANES))] + [struct((8 * NZ, LANES), BF16)] * 2,
        scratch_shapes=mhd_scratch(NZ),
        compiler_params=params(20),
        cost_estimate=cost(4),
        name="bulk",
    )(prim)

    sxrows = 8 * NZ + 8 * YG
    weights = [struct((8 * HID, KIN), BF16), struct((HID, KHID), BF16), struct((HID, KHID), BF16),
               struct((16, HID), BF16)]
    yp, slo, shi, *closure = pl.pallas_call(
        window_kernel,
        out_shape=[struct((8 * YPLANE, LANES))] + [struct((sxrows, LANES), BF16)] * 2 + weights,
        scratch_shapes=[pltpu.VMEM((YROWS, LANES), F32)] * 2,
        compiler_params=params(12),
        cost_estimate=cost(1),
        name="windows",
    )(prim, yfl, yfr, xmlo, xmhi, w_in, w_hid.reshape(2 * HID, HID), w_out.reshape(1, HID), b_hid)
    xlo = lax.ppermute(shi, "col", step_up("col"))
    xhi = lax.ppermute(slo, "col", step_down("col"))

    yadv, xcells = pl.pallas_call(
        ready_kernel,
        out_shape=[struct((8 * YPLANE, LANES)), struct((2 * KIN, WIDE), BF16)],
        scratch_shapes=mhd_scratch(YG),
        compiler_params=params(16),
        cost_estimate=cost(4),
        name="ready",
    )(maps, prim, yp)

    xrows = 16 * NZ + 16 * YG
    rest, badv, yb, ky, kape, sxlo, sxhi = pl.pallas_call(
        edge_kernel,
        in_specs=[VSPEC] * 14,
        out_shape=[struct((5 * PLANE, LANES)), struct((3 * PLANE, LANES)), struct((3 * YPLANE, LANES)),
                   struct((YPLANE, LANES)), struct((6 * HALF, LANES)),
                   struct((xrows, LANES), BF16), struct((xrows, LANES), BF16)],
        scratch_shapes=[pltpu.VMEM((sxrows, LANES), F32)] * 2 + [pltpu.VMEM((8 * YPLANE, LANES), F32)],
        compiler_params=params(32),
        cost_estimate=cost(8),
        name="edges",
    )(maps, prim, adv, yp, yadv, xcells, xlo, xhi, yfl, yfr, *closure)

    gothi = lax.ppermute(sxlo, "col", step_down("col"))
    gotlo = lax.ppermute(sxhi, "col", step_up("col"))

    kap = pl.pallas_call(
        inner_kernel,
        in_specs=[VSPEC] * 7,
        out_shape=struct((PLANE, LANES)),
        scratch_shapes=[pltpu.VMEM((HALF * CX, LANES), F32)],
        compiler_params=params(24),
        cost_estimate=cost(6),
        name="inner",
    )(maps, xcells, kape, *closure)

    out = pl.pallas_call(
        diffuse_kernel,
        out_specs=pl.BlockSpec(memory_space=pltpu.HBM),
        out_shape=struct((8 * PLANE, LANES)),
        scratch_shapes=[pltpu.VMEM((NZ * DEEP, LANES), F32)] * 3
        + [pltpu.VMEM((YG * DEEP, LANES), F32)] * 3
        + [pltpu.VMEM((xrows, LANES), F32)] * 2
        + [pltpu.VMEM((3 * PLANE, LANES), F32), pltpu.VMEM((NZ * DEEP, LANES), F32),
           pltpu.VMEM((YG * DEEP, LANES), F32), pltpu.SemaphoreType.DMA((5,))],
        compiler_params=params(16),
        name="diffuse",
    )(rest, badv, kap, yb, ky, gotlo, gothi)
    return out.reshape(shape)


def solution(mesh):
    return jax.shard_map(
        shards,
        mesh=mesh,
        in_specs=(
            P(None, None, "col", "row"),
            P("row", "col", None),
            P("row", "col"),
            P(),
            P(),
            P(),
            P(),
        ),
        out_specs=P(None, None, "col", "row"),
        check_vma=False,
    )
```
